32 devices in a mesh: kz: 4 (over z), pen: 8 (over y, x, core).
Axes of the slice: x: 2, y: 2, z: 4, core: 2. Of those that a mesh axis runs over, the one named last changes fastest.
Arguments:
- spectrum: bfloat16 [64, 2, 64, 4096], P('kz', None, None, 'pen'), may hold values from -6 to 6
- depth_weights: bfloat16 [64, 16, 64], P('kz'), may hold values from -0.125 to 0.125
- pair_tilt: int32 [64, 16], P('kz'), may hold values from 0 to 15
- pair_tile_within: int32 [64, 16], P('kz'), may hold values from 0 to 1
- tilt_pos: int32 [16], replicated, may hold values from 0 to 15, each once
- owner: int32 [64], P('kz'), may hold values from 0 to 7, as said below
- measured: bfloat16 [32, 2, 4096], P(('kz', 'pen')), may hold values from -6 to 6
Outputs:
- updated: bfloat16 [64, 2, 64, 4096], P(('kz', 'pen'))
- residual: bfloat16 [32, 2, 4096], P(('kz', 'pen'))
The draws below stay inside these ranges and needn't reach their ends.
Inputs may be any that keep to these rules, and one draw needn't show every extreme that they name: Within every group of 16 consecutive blocks each owner value is taken by exactly 2 blocks.
All inputs are finite; a program needn't handle non-finite values.
Results may differ from the reference program's by a relative error of at most 0.004.
Values may be sent and summed in bfloat16 or wider, within the bound.
No kernel may reach another device: no remote copies, remote signals or barrier semaphores. Data moves between devices by JAX's collectives and lax.ppermute only.
A program may use at most 64 MiB of HBM per device.

```python
import jax
import jax.numpy as jnp
from jax import lax

DEPTH = 64
TILE = 4096
K = 16
TILTS = 16
B_DEV = 2
TILE_DEV = 1
PEN_BLOCKS = 16
NB = 64
NTILE = 32
TPT = 2


def draw_owner(key, part):
    key = jax.random.fold_in(key, 7)
    keys = jax.random.split(key, NB // PEN_BLOCKS)
    orders = jax.vmap(lambda single: jax.random.permutation(single, PEN_BLOCKS))(keys)
    return (orders // B_DEV).reshape(NB).astype(jnp.int32)


def plant(entries, stream_key, smallest, high):
    longest = entries.shape.index(max(entries.shape))
    spots = []
    for shift in (0, 1):
        where = [jax.random.randint(jax.random.fold_in(stream_key, axis), (), 0, length) for axis, length in enumerate(entries.shape)]
        where[longest] = (where[longest] + shift) % entries.shape[longest]
        spots.append(tuple(where))
    return entries.at[spots[0]].set(smallest).at[spots[1]].set(high)


def block_scale(own_key, dims, cuts, low, high):
    loudness = 1.0
    for axis_at, shards_of in cuts:
        steps = jax.random.uniform(jax.random.fold_in(jax.random.fold_in(own_key, 6), axis_at), (shards_of,), jnp.float32, low / len(cuts), high / len(cuts))
        loudness = loudness * jnp.repeat(jnp.exp(steps), dims[axis_at] // shards_of).reshape((-1,) + (1,) * (len(dims) - 1 - axis_at))
    return loudness


def noise(stream_key, extent, deviation, limit, pieces=(), held_as=jnp.bfloat16):
    array = jax.random.normal(stream_key, extent, jnp.float32) * deviation
    if len(pieces) > 0:
        array = block_scale(stream_key, extent, pieces, -0.22, 0.18) * array
    return jnp.clip(array, min=-limit, max=limit).astype(held_as)


def setup_inputs(seed: int = 0) -> dict:
    key_list = jax.random.split(jax.random.key(seed), 8)
    spectrum = noise(key_list[0], (NB, 2, DEPTH, TILE), 1.0, 6.0, ((0, 4), (3, 8)))
    depth_weights = noise(key_list[1], (NB, K, DEPTH), (DEPTH * B_DEV * K // TILE_DEV) ** -0.5, 0.125, ((0, 4),))
    pair_tilt = plant(jax.random.randint(key_list[2], (NB, K), 0, TILTS), jax.random.fold_in(key_list[2], 1), 0, TILTS - 1).astype(jnp.int32)
    pair_tile_within = plant(jax.random.randint(key_list[3], (NB, K), 0, TPT), jax.random.fold_in(key_list[3], 1), 0, TPT - 1).astype(jnp.int32)
    tilt_pos = jax.random.permutation(key_list[4], TILTS).astype(jnp.int32)
    owner = draw_owner(jax.random.fold_in(key_list[7], 71), 0)
    measured = noise(key_list[6], (NTILE, 2, TILE), 1.0, 6.0, ((0, 32),))
    return {"spectrum": spectrum, "depth_weights": depth_weights, "pair_tilt": pair_tilt, "pair_tile_within": pair_tile_within, "tilt_pos": tilt_pos, "owner": owner, "measured": measured}


def reference(spectrum, depth_weights, pair_tilt, pair_tile_within, tilt_pos, owner, measured):
    slot = (tilt_pos[pair_tilt] * TPT + pair_tile_within).astype(jnp.int32)

    def forward_one(total, input_arrays):
        block, weight_table, where = input_arrays
        part = jnp.einsum("kd,cdx->kcx", weight_table.astype(jnp.float32), block.astype(jnp.float32))
        return total.at[where].add(part.reshape(K, 2 * TILE)), None

    slices, _ = lax.scan(forward_one, jnp.zeros((NTILE, 2 * TILE), jnp.float32), (spectrum, depth_weights, slot))
    residual = (slices.reshape(NTILE, 2, TILE) - measured.astype(jnp.float32)).astype(jnp.bfloat16)

    grouped = owner.reshape(NB // PEN_BLOCKS, PEN_BLOCKS)
    ids = jnp.arange(PEN_BLOCKS, dtype=jnp.int32)
    same = grouped[:, :, None] == grouped[:, None, :]
    earlier = ids[None, :] < ids[:, None]
    rank = jnp.sum(same & earlier[None], axis=2).astype(jnp.int32)
    groups = jnp.arange(NB // PEN_BLOCKS, dtype=jnp.int32)[:, None]
    position = (groups * PEN_BLOCKS + grouped * B_DEV + rank).reshape(NB).astype(jnp.int32)
    inverse_map = jnp.zeros((NB,), jnp.int32).at[position].set(jnp.arange(NB, dtype=jnp.int32))

    def adjoint_one(index):
        block = spectrum[index].astype(jnp.float32)
        weight_table = depth_weights[index].astype(jnp.float32)
        used_flags = residual[slot[index]].astype(jnp.float32)
        gradient_volume = jnp.einsum("kd,kcx->cdx", weight_table, used_flags)
        return (block - 8.0 * gradient_volume).astype(jnp.bfloat16)

    updated = lax.map(adjoint_one, inverse_map)
    return updated, residual
```

```python
import jax
import jax.numpy as jnp
from jax import lax
from jax.experimental import pallas as pl
from jax.experimental.pallas import tpu as pltpu
from jax.sharding import PartitionSpec as P

BF16 = jnp.bfloat16
F32 = jnp.float32
I32 = jnp.int32
SMEM = pl.BlockSpec(memory_space=pltpu.SMEM)
VMEM = pl.BlockSpec(memory_space=pltpu.VMEM)
ANY = pl.BlockSpec(memory_space=pl.ANY)


def split_hi_lo(value):
    hi = value.astype(BF16)
    return hi, (value - hi.astype(F32)).astype(BF16)


def order_blocks(n_pen, per_owner, owner_ref, spectrum_ref, out_ref, count_ref, sems):
    blocks = spectrum_ref.shape[0]
    for o in range(n_pen):
        count_ref[o] = 0
    copies = []
    for b in range(blocks):
        o = owner_ref[b]
        r = count_ref[o]
        count_ref[o] = r + 1
        copy = pltpu.make_async_copy(spectrum_ref.at[b], out_ref.at[o * per_owner + r], sems.at[b])
        copy.start()
        copies.append(copy)
    for copy in copies:
        copy.wait()


def slots(tilt_pos_ref, tilt, within, tiles_per_tilt, flip):
    place = jnp.zeros_like(tilt)
    for t in range(tilt_pos_ref.shape[0]):
        place = jnp.where(tilt == t, tilt_pos_ref[t], place)
    return (place * tiles_per_tilt + within) ^ flip


def forward(n_kz, chunk, tiles_per_tilt, where_ref, tilt_pos_ref, tilt_ref, within_ref,
            weights_ref, spectrum_ref, *rest):
    outs, table = rest[:n_kz], rest[n_kz]
    blocks, pairs, depth = weights_ref.shape
    columns = spectrum_ref.shape[3]
    tiles = n_kz * chunk
    slot = slots(tilt_pos_ref, tilt_ref[...], within_ref[...], tiles_per_tilt, where_ref[0] * chunk)
    rows = lax.broadcasted_iota(I32, (tiles, pairs), 0)
    for b in range(blocks):
        hot = jnp.where(slot[b : b + 1, :] == rows, 1.0, 0.0).astype(BF16)
        hi, lo = split_hi_lo(jnp.dot(hot, weights_ref[b], preferred_element_type=F32))
        table[:tiles, b * depth : (b + 1) * depth] = hi
        table[tiles:, b * depth : (b + 1) * depth] = lo
    for c in range(2):
        both = jnp.dot(
            table[...],
            spectrum_ref[:, c].reshape(blocks * depth, columns),
            preferred_element_type=F32,
        )
        total = both[:tiles] + both[tiles:]
        for k in range(n_kz):
            outs[k][c * chunk : (c + 1) * chunk, :] = total[k * chunk : (k + 1) * chunk]


def adjoint_table(n_kz, chunk, n_pen, per_owner, tiles_per_tilt, where_ref, tilt_pos_ref, owner_ref,
                  tilt_ref, within_ref, weights_ref, out_ref, mine_ref, slot_ref):
    blocks, pairs, depth = weights_ref.shape
    rows_all = n_kz * 2 * chunk
    pen = where_ref[1]
    seen = jnp.int32(0)
    for b in range(blocks):
        hit = owner_ref[b] == pen

        @pl.when(hit)
        def _(b=b, seen=seen):
            mine_ref[seen] = b

        seen = seen + hit.astype(I32)
    slot = slots(tilt_pos_ref, tilt_ref[...], within_ref[...], tiles_per_tilt, where_ref[0] * chunk)
    slot_ref[...] = slot
    rows = lax.broadcasted_iota(I32, (rows_all, pairs), 0)
    for r in range(per_owner):
        b = mine_ref[r]
        at = slot_ref[pl.ds(b, 1), :]
        low = at & (chunk - 1)
        for c in range(2):
            place = (at - low) * 2 + c * chunk + low
            hot = jnp.where(place == rows, -8.0, 0.0).astype(BF16)
            hi, lo = split_hi_lo(jnp.dot(hot, weights_ref[b], preferred_element_type=F32))
            first = (c * per_owner + r) * depth
            out_ref[:rows_all, first : first + depth] = hi
            out_ref[rows_all:, first : first + depth] = lo


def residual_chunk(n_kz, *refs):
    parts, measured_ref, out_ref = refs[:n_kz], refs[n_kz], refs[n_kz + 1]
    total = parts[0][...]
    for part in parts[1:]:
        total = total + part[...]
    out_ref[...] = (total - measured_ref[...].astype(F32)).astype(BF16)


def adjoint(chunk, per_owner, where_ref, table_ref, tiles_ref, blocks_ref, out_ref, residual_ref):
    depth = blocks_ref.shape[3]
    r_tiles = tiles_ref[0]
    rows = r_tiles.shape[0]
    both = jnp.concatenate([r_tiles, r_tiles], axis=0)
    step = lax.dot_general(
        table_ref[...], both, (((0,), (0,)), ((), ())), preferred_element_type=F32
    )
    for r in range(per_owner):
        for c in range(2):
            first = (c * per_owner + r) * depth
            out_ref[r, c] = (blocks_ref[0, r, c].astype(F32) + step[first : first + depth]).astype(BF16)
    pick_row = lax.broadcasted_iota(I32, (16, rows), 0)
    pick_at = lax.broadcasted_iota(I32, (16, rows), 1)
    pick = jnp.where(pick_at == pick_row * chunk + where_ref[1], 1.0, 0.0)
    pick = jnp.where(pick_row < 2, pick, 0.0).astype(BF16)
    own = jnp.dot(pick, r_tiles, preferred_element_type=F32)
    residual_ref[0] = own[:2].astype(BF16)


def body(spectrum, depth_weights, pair_tilt, pair_tile_within, tilt_pos, owner, measured):
    n_pen = lax.axis_size("pen")
    n_kz = lax.axis_size("kz")
    blocks, _, depth, columns = spectrum.shape
    per_owner = blocks // n_pen
    pairs = depth_weights.shape[1]
    tile_dev, _, cells = measured.shape
    chunk = tile_dev * n_pen
    tiles = chunk * n_kz
    tiles_per_tilt = tiles // tilt_pos.shape[0]
    where = jnp.stack([lax.axis_index("kz"), lax.axis_index("pen")]).astype(I32)

    def call(kernel, *static):
        def bound(*refs):
            return kernel(*static, *refs)
        return bound

    outgoing = pl.pallas_call(
        call(order_blocks, n_pen, per_owner),
        out_shape=jax.ShapeDtypeStruct(spectrum.shape, BF16),
        in_specs=[SMEM, ANY],
        out_specs=ANY,
        scratch_shapes=[pltpu.SMEM((n_pen,), I32), pltpu.SemaphoreType.DMA((blocks,))],
    )(owner, spectrum)
    outgoing = outgoing.reshape(n_pen, per_owner, 2, depth, columns)
    incoming = lax.all_to_all(outgoing, "pen", split_axis=0, concat_axis=0, tiled=True)

    sent = measured.reshape(2, n_pen, columns).transpose(1, 0, 2)
    got = lax.all_to_all(sent, "pen", split_axis=0, concat_axis=0, tiled=True)
    measured_rows = got.transpose(1, 0, 2).reshape(2 * chunk, columns)

    parts = pl.pallas_call(
        call(forward, n_kz, chunk, tiles_per_tilt),
        out_shape=[jax.ShapeDtypeStruct((2 * chunk, columns), F32)] * n_kz,
        in_specs=[SMEM, SMEM, VMEM, VMEM, VMEM, VMEM],
        out_specs=[VMEM] * n_kz,
        scratch_shapes=[pltpu.VMEM((2 * tiles, blocks * depth), BF16)],
        compiler_params=pltpu.CompilerParams(vmem_limit_bytes=48 << 20),
    )(where, tilt_pos, pair_tilt, pair_tile_within, depth_weights, spectrum)

    def across(value, k):
        return lax.ppermute(value, "kz", [(i, i ^ k) for i in range(n_kz)])

    summed = [parts[0]] + [across(parts[k], k) for k in range(1, n_kz)]
    table = pl.pallas_call(
        call(adjoint_table, n_kz, chunk, n_pen, per_owner, tiles_per_tilt),
        out_shape=jax.ShapeDtypeStruct((4 * tiles, 2 * per_owner * depth), BF16),
        in_specs=[SMEM, SMEM, SMEM, VMEM, VMEM, VMEM],
        out_specs=VMEM,
        scratch_shapes=[pltpu.SMEM((per_owner,), I32), pltpu.VMEM((blocks, pairs), I32)],
    )(where, tilt_pos, owner, pair_tilt, pair_tile_within, depth_weights)

    own = pl.pallas_call(
        call(residual_chunk, n_kz),
        out_shape=jax.ShapeDtypeStruct((2 * chunk, columns), BF16),
        in_specs=[VMEM] * (n_kz + 1),
        out_specs=VMEM,
    )(*summed, measured_rows)

    held = jnp.concatenate([own] + [across(own, k) for k in range(1, n_kz)], axis=0)
    every = lax.all_gather(held, "pen", axis=0, tiled=False)

    updated, residual = pl.pallas_call(
        call(adjoint, chunk, per_owner),
        grid=(n_pen,),
        out_shape=[
            jax.ShapeDtypeStruct((per_owner, 2, depth, cells), BF16),
            jax.ShapeDtypeStruct((tile_dev, 2, cells), BF16),
        ],
        in_specs=[
            SMEM,
            pl.BlockSpec((4 * tiles, 2 * per_owner * depth), lambda p: (0, 0)),
            pl.BlockSpec((1, 2 * tiles, columns), lambda p: (p, 0, 0)),
            pl.BlockSpec((1, per_owner, 2, depth, columns), lambda p: (p, 0, 0, 0, 0)),
        ],
        out_specs=[
            pl.BlockSpec((per_owner, 2, depth, columns), lambda p: (0, 0, 0, p)),
            pl.BlockSpec((tile_dev, 2, columns), lambda p: (0, 0, p)),
        ],
        compiler_params=pltpu.CompilerParams(vmem_limit_bytes=48 << 20),
    )(where, table, every, incoming)
    return (updated, residual)


def solution(mesh):
    return jax.shard_map(
        body,
        mesh=mesh,
        in_specs=(
            P("kz", None, None, "pen"),
            P("kz", None, None),
            P("kz", None),
            P("kz", None),
            P(),
            P("kz"),
            P(("kz", "pen"), None, None),
        ),
        out_specs=(P(("kz", "pen"), None, None, None), P(("kz", "pen"), None, None)),
        check_vma=False,
    )
```

```python
import jax
import jax.numpy as jnp
from jax import lax
from jax.experimental import pallas as pl
from jax.experimental.pallas import tpu as pltpu
from jax.sharding import PartitionSpec as P

BF16 = jnp.bfloat16
F32 = jnp.float32
I32 = jnp.int32
SMEM = pl.BlockSpec(memory_space=pltpu.SMEM)
VMEM = pl.BlockSpec(memory_space=pltpu.VMEM)
ANY = pl.BlockSpec(memory_space=pl.ANY)


def split_hi_lo(value):
    hi = value.astype(BF16)
    return hi, (value - hi.astype(F32)).astype(BF16)


def order_blocks(n_pen, per_owner, owner_ref, spectrum_ref, out_ref, count_ref, sems):
    blocks = spectrum_ref.shape[0]
    for o in range(n_pen):
        count_ref[o] = 0
    copies = []
    for b in range(blocks):
        o = owner_ref[b]
        r = count_ref[o]
        count_ref[o] = r + 1
        copy = pltpu.make_async_copy(spectrum_ref.at[b], out_ref.at[o * per_owner + r], sems.at[b])
        copy.start()
        copies.append(copy)
    for copy in copies:
        copy.wait()


def slots(tilt_pos_ref, tilt, within, tiles_per_tilt, flip):
    place = jnp.zeros_like(tilt)
    for t in range(tilt_pos_ref.shape[0]):
        place = jnp.where(tilt == t, tilt_pos_ref[t], place)
    return (place * tiles_per_tilt + within) ^ flip


def forward(n_kz, chunk, tiles_per_tilt, tilt_pos_ref, tilt_ref, within_ref, weights_ref,
            spectrum_ref, *rest):
    outs, table = rest[:n_kz], rest[n_kz]
    blocks, pairs, depth = weights_ref.shape
    columns = spectrum_ref.shape[3]
    tiles = n_kz * chunk
    flip = lax.axis_index("kz") * chunk
    slot = slots(tilt_pos_ref, tilt_ref[...], within_ref[...], tiles_per_tilt, flip)
    rows = lax.broadcasted_iota(I32, (tiles, pairs), 0)
    for b in range(blocks):
        hot = jnp.where(slot[b : b + 1, :] == rows, 1.0, 0.0).astype(BF16)
        hi, lo = split_hi_lo(jnp.dot(hot, weights_ref[b], preferred_element_type=F32))
        table[:tiles, b * depth : (b + 1) * depth] = hi
        table[tiles:, b * depth : (b + 1) * depth] = lo
    for c in range(2):
        both = jnp.dot(
            table[...],
            spectrum_ref[:, c].reshape(blocks * depth, columns),
            preferred_element_type=F32,
        )
        total = both[:tiles] + both[tiles:]
        for k in range(n_kz):
            outs[k][c * chunk : (c + 1) * chunk, :] = total[k * chunk : (k + 1) * chunk]


def adjoint_table(n_kz, chunk, n_pen, per_owner, tiles_per_tilt, tilt_pos_ref, owner_ref,
                  tilt_ref, within_ref, weights_ref, out_ref, mine_ref, slot_ref):
    blocks, pairs, depth = weights_ref.shape
    rows_all = n_kz * 2 * chunk
    pen = lax.axis_index("pen")
    seen = jnp.int32(0)
    for b in range(blocks):
        hit = owner_ref[b] == pen

        @pl.when(hit)
        def _(b=b, seen=seen):
            mine_ref[seen] = b

        seen = seen + hit.astype(I32)
    flip = lax.axis_index("kz") * chunk
    slot_ref[...] = slots(tilt_pos_ref, tilt_ref[...], within_ref[...], tiles_per_tilt, flip)
    rows = lax.broadcasted_iota(I32, (rows_all, pairs), 0)
    for r in range(per_owner):
        b = mine_ref[r]
        at = slot_ref[pl.ds(b, 1), :]
        low = at & (chunk - 1)
        for c in range(2):
            place = (at - low) * 2 + c * chunk + low
            hot = jnp.where(place == rows, -8.0, 0.0).astype(BF16)
            hi, lo = split_hi_lo(jnp.dot(hot, weights_ref[b], preferred_element_type=F32))
            first = (c * per_owner + r) * depth
            out_ref[:rows_all, first : first + depth] = hi
            out_ref[rows_all:, first : first + depth] = lo


def adjoint(n_pen, chunk, per_owner, table_ref, tiles_ref, blocks_ref, out_ref, residual_ref,
            table, tiles, held, made, table_sem, tile_sems, in_sems, out_sems):
    depth, columns = blocks_ref.shape[3:]
    rows = tiles_ref.shape[1]
    get_table = pltpu.make_async_copy(table_ref, table, table_sem)
    get_table.start()
    gets, puts = [], []
    for p in range(n_pen):
        gets.append(
            (
                pltpu.make_async_copy(tiles_ref.at[p], tiles.at[p], tile_sems.at[p]),
                pltpu.make_async_copy(blocks_ref.at[p], held.at[p], in_sems.at[p]),
            )
        )
        for get in gets[p]:
            get.start()
    pick_row = lax.broadcasted_iota(I32, (16, rows), 0)
    pick_at = lax.broadcasted_iota(I32, (16, rows), 1)
    pick = jnp.where(pick_at == pick_row * chunk + lax.axis_index("pen"), 1.0, 0.0)
    pick = jnp.where(pick_row < 2, pick, 0.0).astype(BF16)
    get_table.wait()
    for p in range(n_pen):
        gets[p][0].wait()
        here = tiles[p]
        own = jnp.dot(pick, here, preferred_element_type=F32)
        residual_ref[0, :, p * columns : (p + 1) * columns] = own[:2].astype(BF16)
        step = lax.dot_general(
            table[...],
            jnp.concatenate([here, here], axis=0),
            (((0,), (0,)), ((), ())),
            preferred_element_type=F32,
        )
        gets[p][1].wait()
        for r in range(per_owner):
            for c in range(2):
                first = (c * per_owner + r) * depth
                made[p, r, c] = (held[p, r, c].astype(F32) + step[first : first + depth]).astype(BF16)
        to = out_ref.at[:, :, :, pl.ds(p * columns, columns)]
        puts.append(pltpu.make_async_copy(made.at[p], to, out_sems.at[p]))
        puts[p].start()
    for put in puts:
        put.wait()


def body(spectrum, depth_weights, pair_tilt, pair_tile_within, tilt_pos, owner, measured):
    n_pen = lax.axis_size("pen")
    n_kz = lax.axis_size("kz")
    blocks, _, depth, columns = spectrum.shape
    per_owner = blocks // n_pen
    pairs = depth_weights.shape[1]
    tile_dev, _, cells = measured.shape
    chunk = tile_dev * n_pen
    tiles = chunk * n_kz
    tiles_per_tilt = tiles // tilt_pos.shape[0]

    def call(kernel, *static):
        def bound(*refs):
            return kernel(*static, *refs)
        return bound

    outgoing = pl.pallas_call(
        call(order_blocks, n_pen, per_owner),
        out_shape=jax.ShapeDtypeStruct(spectrum.shape, BF16),
        in_specs=[SMEM, ANY],
        out_specs=VMEM,
        scratch_shapes=[pltpu.SMEM((n_pen,), I32), pltpu.SemaphoreType.DMA((blocks,))],
    )(owner, spectrum)
    outgoing = outgoing.reshape(n_pen, per_owner, 2, depth, columns)
    incoming = lax.all_to_all(outgoing, "pen", split_axis=0, concat_axis=0, tiled=True)

    sent = measured.reshape(2, n_pen, columns).transpose(1, 0, 2)
    got = lax.all_to_all(sent, "pen", split_axis=0, concat_axis=0, tiled=True)
    measured_rows = got.transpose(1, 0, 2).reshape(2 * chunk, columns)

    parts = pl.pallas_call(
        call(forward, n_kz, chunk, tiles_per_tilt),
        out_shape=[jax.ShapeDtypeStruct((2 * chunk, columns), F32)] * n_kz,
        in_specs=[SMEM, VMEM, VMEM, VMEM, VMEM],
        out_specs=[VMEM] * n_kz,
        scratch_shapes=[pltpu.VMEM((2 * tiles, blocks * depth), BF16)],
        compiler_params=pltpu.CompilerParams(vmem_limit_bytes=48 << 20),
    )(tilt_pos, pair_tilt, pair_tile_within, depth_weights, spectrum)

    def across(value, k):
        return lax.ppermute(value, "kz", [(i, i ^ k) for i in range(n_kz)])

    summed = [parts[0]] + [across(parts[k], k) for k in range(1, n_kz)]
    table = pl.pallas_call(
        call(adjoint_table, n_kz, chunk, n_pen, per_owner, tiles_per_tilt),
        out_shape=jax.ShapeDtypeStruct((4 * tiles, 2 * per_owner * depth), BF16),
        in_specs=[SMEM, SMEM, VMEM, VMEM, VMEM],
        out_specs=VMEM,
        scratch_shapes=[pltpu.SMEM((per_owner,), I32), pltpu.VMEM((blocks, pairs), I32)],
    )(tilt_pos, owner, pair_tilt, pair_tile_within, depth_weights)

    total = summed[0]
    for part in summed[1:]:
        total = total + part
    own = (total - measured_rows.astype(F32)).astype(BF16)

    held = jnp.concatenate([own] + [across(own, k) for k in range(1, n_kz)], axis=0)
    every = lax.all_gather(held, "pen", axis=0, tiled=False)

    piece = (n_pen, per_owner, 2, depth, columns)
    updated, residual = pl.pallas_call(
        call(adjoint, n_pen, chunk, per_owner),
        out_shape=[
            jax.ShapeDtypeStruct((per_owner, 2, depth, cells), BF16),
            jax.ShapeDtypeStruct((tile_dev, 2, cells), BF16),
        ],
        in_specs=[ANY, ANY, ANY],
        out_specs=[ANY, VMEM],
        scratch_shapes=[
            pltpu.VMEM(table.shape, BF16),
            pltpu.VMEM(every.shape, BF16),
            pltpu.VMEM(piece, BF16),
            pltpu.VMEM(piece, BF16),
            pltpu.SemaphoreType.DMA,
            pltpu.SemaphoreType.DMA((n_pen,)),
            pltpu.SemaphoreType.DMA((n_pen,)),
            pltpu.SemaphoreType.DMA((n_pen,)),
        ],
        compiler_params=pltpu.CompilerParams(vmem_limit_bytes=60 << 20),
    )(table, every, incoming)
    return (updated, residual)


def solution(mesh):
    return jax.shard_map(
        body,
        mesh=mesh,
        in_specs=(
            P("kz", None, None, "pen"),
            P("kz", None, None),
            P("kz", None),
            P("kz", None),
            P(),
            P("kz"),
            P(("kz", "pen"), None, None),
        ),
        out_specs=(P(("kz", "pen"), None, None, None), P(("kz", "pen"), None, None)),
        check_vma=False,
    )
```

```python
import jax
import jax.numpy as jnp
from jax import lax
from jax.experimental import pallas as pl
from jax.experimental.pallas import tpu as pltpu
from jax.sharding import PartitionSpec as P

BF16 = jnp.bfloat16
F32 = jnp.float32
I32 = jnp.int32
SMEM = pl.BlockSpec(memory_space=pltpu.SMEM)
VMEM = pl.BlockSpec(memory_space=pltpu.VMEM)
ANY = pl.BlockSpec(memory_space=pl.ANY)


def split_hi_lo(value):
    hi = value.astype(BF16)
    return hi, (value - hi.astype(F32)).astype(BF16)


def order_blocks(per_owner, owner_ref, spectrum_ref, out_ref, inverse_ref, count_ref, sems):
    blocks = spectrum_ref.shape[0]
    for o in range(blocks // per_owner):
        count_ref[o] = 0
    gets = []
    for b in range(blocks):
        o = owner_ref[b]
        r = count_ref[o]
        count_ref[o] = r + 1
        at = o * per_owner + r
        inverse_ref[at] = b
        gets.append(pltpu.make_async_copy(spectrum_ref.at[b], out_ref.at[at], sems.at[b]))
        gets[b].start()
    for get in gets:
        get.wait()


def slots(tilt_pos_ref, tilt, within, tiles_per_tilt, flip):
    place = jnp.zeros_like(tilt)
    for t in range(tilt_pos_ref.shape[0]):
        place = jnp.where(tilt == t, tilt_pos_ref[t], place)
    return (place * tiles_per_tilt + within) ^ flip


def forward(n_kz, chunk, tiles_per_tilt, inverse_ref, tilt_pos_ref, tilt_ref, within_ref,
            weights_ref, spectrum_ref, *rest):
    outs, table, slot_ref = rest[:n_kz], rest[n_kz], rest[n_kz + 1]
    blocks, pairs, depth = weights_ref.shape
    columns = spectrum_ref.shape[3]
    tiles = n_kz * chunk
    flip = lax.axis_index("kz") * chunk
    slot_ref[...] = slots(tilt_pos_ref, tilt_ref[...], within_ref[...], tiles_per_tilt, flip)
    rows = lax.broadcasted_iota(I32, (tiles, pairs), 0)
    for at in range(blocks):
        b = inverse_ref[at]
        hot = jnp.where(slot_ref[pl.ds(b, 1), :] == rows, 1.0, 0.0).astype(BF16)
        hi, lo = split_hi_lo(jnp.dot(hot, weights_ref[b], preferred_element_type=F32))
        table[:tiles, at * depth : (at + 1) * depth] = hi
        table[tiles:, at * depth : (at + 1) * depth] = lo
    for c in range(2):
        both = jnp.dot(
            table[...],
            spectrum_ref[:, c].reshape(blocks * depth, columns),
            preferred_element_type=F32,
        )
        total = both[:tiles] + both[tiles:]
        for k in range(n_kz):
            outs[k][c * chunk : (c + 1) * chunk, :] = total[k * chunk : (k + 1) * chunk]


def adjoint_table(n_kz, chunk, per_owner, tiles_per_tilt, inverse_ref, tilt_pos_ref, tilt_ref,
                  within_ref, weights_ref, out_ref, slot_ref):
    depth = weights_ref.shape[2]
    pairs = weights_ref.shape[1]
    rows_all = n_kz * 2 * chunk
    flip = lax.axis_index("kz") * chunk
    slot_ref[...] = slots(tilt_pos_ref, tilt_ref[...], within_ref[...], tiles_per_tilt, flip)
    rows = lax.broadcasted_iota(I32, (rows_all, pairs), 0)
    for r in range(per_owner):
        b = inverse_ref[lax.axis_index("pen") * per_owner + r]
        at = slot_ref[pl.ds(b, 1), :]
        low = at & (chunk - 1)
        for c in range(2):
            place = (at - low) * 2 + c * chunk + low
            hot = jnp.where(place == rows, -8.0, 0.0).astype(BF16)
            hi, lo = split_hi_lo(jnp.dot(hot, weights_ref[b], preferred_element_type=F32))
            first = (c * per_owner + r) * depth
            out_ref[:rows_all, first : first + depth] = hi
            out_ref[rows_all:, first : first + depth] = lo


def adjoint(n_pen, chunk, per_owner, table_ref, blocks_ref, *rest):
    tile_refs, rest = rest[:n_pen], rest[n_pen:]
    out_ref, residual_ref, made, out_sems = rest
    depth, columns = blocks_ref.shape[3:]
    rows = tile_refs[0].shape[0]
    pen = lax.axis_index("pen")
    puts = []
    pick_row = lax.broadcasted_iota(I32, (16, rows), 0)
    pick_at = lax.broadcasted_iota(I32, (16, rows), 1)
    pick = jnp.where(pick_at == pick_row * chunk + pen, 1.0, 0.0)
    pick = jnp.where(pick_row < 2, pick, 0.0).astype(BF16)
    for j in range(n_pen):
        first_column = pl.multiple_of((pen ^ j) * columns, columns)
        here = tile_refs[j][...]
        own = jnp.dot(pick, here, preferred_element_type=F32)
        residual_ref[0, :, pl.ds(first_column, columns)] = own[:2].astype(BF16)
        step = lax.dot_general(
            table_ref[...],
            jnp.concatenate([here, here], axis=0),
            (((0,), (0,)), ((), ())),
            preferred_element_type=F32,
        )
        for r in range(per_owner):
            for c in range(2):
                first = (c * per_owner + r) * depth
                held = blocks_ref[pen ^ j, r, c].astype(F32)
                made[j, r, c] = (held + step[first : first + depth]).astype(BF16)
        to = out_ref.at[:, :, :, pl.ds(first_column, columns)]
        puts.append(pltpu.make_async_copy(made.at[j], to, out_sems.at[j]))
        puts[j].start()
    for put in puts:
        put.wait()


def body(spectrum, depth_weights, pair_tilt, pair_tile_within, tilt_pos, owner, measured):
    n_pen = lax.axis_size("pen")
    n_kz = lax.axis_size("kz")
    blocks, _, depth, columns = spectrum.shape
    per_owner = blocks // n_pen
    pairs = depth_weights.shape[1]
    tile_dev, _, cells = measured.shape
    chunk = tile_dev * n_pen
    tiles = chunk * n_kz
    tiles_per_tilt = tiles // tilt_pos.shape[0]

    def call(kernel, *static):
        def bound(*refs):
            return kernel(*static, *refs)
        return bound

    ordered, inverse = pl.pallas_call(
        call(order_blocks, per_owner),
        out_shape=[
            jax.ShapeDtypeStruct(spectrum.shape, BF16),
            jax.ShapeDtypeStruct((blocks,), I32),
        ],
        in_specs=[SMEM, ANY],
        out_specs=[VMEM, SMEM],
        scratch_shapes=[pltpu.SMEM((n_pen,), I32), pltpu.SemaphoreType.DMA((blocks,))],
        compiler_params=pltpu.CompilerParams(vmem_limit_bytes=8 << 20),
    )(owner, spectrum)
    outgoing = ordered.reshape(n_pen, per_owner, 2, depth, columns)
    incoming = lax.all_to_all(outgoing, "pen", split_axis=0, concat_axis=0, tiled=True)

    parts = pl.pallas_call(
        call(forward, n_kz, chunk, tiles_per_tilt),
        out_shape=[jax.ShapeDtypeStruct((2 * chunk, columns), F32)] * n_kz,
        in_specs=[SMEM, SMEM, VMEM, VMEM, VMEM, VMEM],
        out_specs=[VMEM] * n_kz,
        scratch_shapes=[
            pltpu.VMEM((2 * tiles, blocks * depth), BF16),
            pltpu.VMEM((blocks, pairs), I32),
        ],
        compiler_params=pltpu.CompilerParams(vmem_limit_bytes=16 << 20),
    )(inverse, tilt_pos, pair_tilt, pair_tile_within, depth_weights, ordered)

    def across(value, k):
        return lax.ppermute(value, "kz", [(i, i ^ k) for i in range(n_kz)])

    summed = [parts[0]] + [across(parts[k], k) for k in range(1, n_kz)]
    table = pl.pallas_call(
        call(adjoint_table, n_kz, chunk, per_owner, tiles_per_tilt),
        out_shape=jax.ShapeDtypeStruct((4 * tiles, 2 * per_owner * depth), BF16),
        in_specs=[SMEM, SMEM, VMEM, VMEM, VMEM],
        out_specs=VMEM,
        scratch_shapes=[pltpu.VMEM((blocks, pairs), I32)],
        compiler_params=pltpu.CompilerParams(vmem_limit_bytes=8 << 20),
    )(inverse, tilt_pos, pair_tilt, pair_tile_within, depth_weights)

    sent = measured.reshape(2, n_pen, columns).transpose(1, 0, 2)
    got = lax.all_to_all(sent, "pen", split_axis=0, concat_axis=0, tiled=True)
    measured_rows = got.transpose(1, 0, 2).reshape(2 * chunk, columns)
    total = summed[0]
    for part in summed[1:]:
        total = total + part
    own = (total - measured_rows.astype(F32)).astype(BF16)

    def between(value, k):
        return lax.ppermute(value, "pen", [(i, i ^ k) for i in range(n_pen)])

    held = jnp.concatenate([own] + [across(own, k) for k in range(1, n_kz)], axis=0)
    every = [held] + [between(held, k) for k in range(2, n_pen, 2)]
    every = [tile for kept in every for tile in (kept, between(kept, 1))]

    updated, residual = pl.pallas_call(
        call(adjoint, n_pen, chunk, per_owner),
        out_shape=[
            jax.ShapeDtypeStruct((per_owner, 2, depth, cells), BF16),
            jax.ShapeDtypeStruct((tile_dev, 2, cells), BF16),
        ],
        in_specs=[VMEM] * (n_pen + 2),
        out_specs=[ANY, VMEM],
        scratch_shapes=[
            pltpu.VMEM((n_pen, per_owner, 2, depth, columns), BF16),
            pltpu.SemaphoreType.DMA((n_pen,)),
        ],
        compiler_params=pltpu.CompilerParams(vmem_limit_bytes=16 << 20),
    )(table, incoming, *every)
    return (updated, residual)


def solution(mesh):
    return jax.shard_map(
        body,
        mesh=mesh,
        in_specs=(
            P("kz", None, None, "pen"),
            P("kz", None, None),
            P("kz", None),
            P("kz", None),
            P(),
            P("kz"),
            P(("kz", "pen"), None, None),
        ),
        out_specs=(P(("kz", "pen"), None, None, None), P(("kz", "pen"), None, None)),
        check_vma=False,
    )
```

```python
import jax
import jax.numpy as jnp
from jax import lax
from jax.experimental import pallas as pl
from jax.experimental.pallas import tpu as pltpu
from jax.sharding import PartitionSpec as P

BF16 = jnp.bfloat16
F32 = jnp.float32
I32 = jnp.int32
SMEM = pl.BlockSpec(memory_space=pltpu.SMEM)
VMEM = pl.BlockSpec(memory_space=pltpu.VMEM)
ANY = pl.BlockSpec(memory_space=pl.ANY)


def split_hi_lo(value):
    hi = value.astype(BF16)
    return hi, (value - hi.astype(F32)).astype(BF16)


def order_blocks(per_owner, owner_ref, spectrum_ref, out_ref, inverse_ref, held, owner, count,
                 owner_sem, in_sems, out_sems):
    blocks = spectrum_ref.shape[0]
    get_owner = pltpu.make_async_copy(owner_ref, owner, owner_sem)
    get_owner.start()
    gets, puts = [], []
    for b in range(blocks):
        gets.append(pltpu.make_async_copy(spectrum_ref.at[b], held.at[b], in_sems.at[b]))
        gets[b].start()
    for o in range(blocks // per_owner):
        count[o] = 0
    get_owner.wait()
    for b in range(blocks):
        o = owner[b]
        r = count[o]
        count[o] = r + 1
        at = o * per_owner + r
        inverse_ref[at] = b
        gets[b].wait()
        puts.append(pltpu.make_async_copy(held.at[b], out_ref.at[at], out_sems.at[b]))
        puts[b].start()
    for put in puts:
        put.wait()


def slots(tilt_pos_ref, tilt, within, tiles_per_tilt, flip):
    place = jnp.zeros_like(tilt)
    for t in range(tilt_pos_ref.shape[0]):
        place = jnp.where(tilt == t, tilt_pos_ref[t], place)
    return (place * tiles_per_tilt + within) ^ flip


def forward(n_kz, chunk, tiles_per_tilt, tilt_pos_ref, tilt_ref, within_ref, weights_ref,
            spectrum_ref, after_ref, *rest):
    del after_ref
    outs, table = rest[:n_kz], rest[n_kz]
    blocks, pairs, depth = weights_ref.shape
    columns = spectrum_ref.shape[3]
    tiles = n_kz * chunk
    flip = lax.axis_index("kz") * chunk
    slot = slots(tilt_pos_ref, tilt_ref[...], within_ref[...], tiles_per_tilt, flip)
    rows = lax.broadcasted_iota(I32, (tiles, pairs), 0)
    for b in range(blocks):
        hot = jnp.where(slot[b : b + 1, :] == rows, 1.0, 0.0).astype(BF16)
        hi, lo = split_hi_lo(jnp.dot(hot, weights_ref[b], preferred_element_type=F32))
        table[:tiles, b * depth : (b + 1) * depth] = hi
        table[tiles:, b * depth : (b + 1) * depth] = lo
    for c in range(2):
        both = jnp.dot(
            table[...],
            spectrum_ref[:, c].reshape(blocks * depth, columns),
            preferred_element_type=F32,
        )
        total = both[:tiles] + both[tiles:]
        for k in range(n_kz):
            outs[k][c * chunk : (c + 1) * chunk, :] = total[k * chunk : (k + 1) * chunk]


def adjoint_table(n_kz, chunk, per_owner, tiles_per_tilt, inverse_ref, tilt_pos_ref, tilt_ref,
                  within_ref, weights_ref, out_ref, slot_ref):
    depth = weights_ref.shape[2]
    pairs = weights_ref.shape[1]
    rows_all = n_kz * 2 * chunk
    flip = lax.axis_index("kz") * chunk
    slot_ref[...] = slots(tilt_pos_ref, tilt_ref[...], within_ref[...], tiles_per_tilt, flip)
    rows = lax.broadcasted_iota(I32, (rows_all, pairs), 0)
    for r in range(per_owner):
        b = inverse_ref[lax.axis_index("pen") * per_owner + r]
        at = slot_ref[pl.ds(b, 1), :]
        low = at & (chunk - 1)
        for c in range(2):
            place = (at - low) * 2 + c * chunk + low
            hot = jnp.where(place == rows, -8.0, 0.0).astype(BF16)
            hi, lo = split_hi_lo(jnp.dot(hot, weights_ref[b], preferred_element_type=F32))
            first = (c * per_owner + r) * depth
            out_ref[:rows_all, first : first + depth] = hi
            out_ref[rows_all:, first : first + depth] = lo


def adjoint(n_pen, chunk, per_owner, table_ref, blocks_ref, *rest):
    tile_refs, rest = rest[:n_pen], rest[n_pen:]
    out_ref, residual_ref, made, out_sems = rest
    depth, columns = blocks_ref.shape[3:]
    rows = tile_refs[0].shape[0]
    pen = lax.axis_index("pen")
    puts = []
    pick_row = lax.broadcasted_iota(I32, (16, rows), 0)
    pick_at = lax.broadcasted_iota(I32, (16, rows), 1)
    pick = jnp.where(pick_at == pick_row * chunk + pen, 1.0, 0.0)
    pick = jnp.where(pick_row < 2, pick, 0.0).astype(BF16)
    for j in range(n_pen):
        first_column = pl.multiple_of((pen ^ j) * columns, columns)
        here = tile_refs[j][...]
        own = jnp.dot(pick, here, preferred_element_type=F32)
        residual_ref[0, :, pl.ds(first_column, columns)] = own[:2].astype(BF16)
        step = lax.dot_general(
            table_ref[...],
            jnp.concatenate([here, here], axis=0),
            (((0,), (0,)), ((), ())),
            preferred_element_type=F32,
        )
        for r in range(per_owner):
            for c in range(2):
                first = (c * per_owner + r) * depth
                held = blocks_ref[pen ^ j, r, c].astype(F32)
                made[j, r, c] = (held + step[first : first + depth]).astype(BF16)
        to = out_ref.at[:, :, :, pl.ds(first_column, columns)]
        puts.append(pltpu.make_async_copy(made.at[j], to, out_sems.at[j]))
        puts[j].start()
    for put in puts:
        put.wait()


def body(spectrum, depth_weights, pair_tilt, pair_tile_within, tilt_pos, owner, measured):
    n_pen = lax.axis_size("pen")
    n_kz = lax.axis_size("kz")
    blocks, _, depth, columns = spectrum.shape
    per_owner = blocks // n_pen
    pairs = depth_weights.shape[1]
    tile_dev, _, cells = measured.shape
    chunk = tile_dev * n_pen
    tiles = chunk * n_kz
    tiles_per_tilt = tiles // tilt_pos.shape[0]

    def call(kernel, *static):
        def bound(*refs):
            return kernel(*static, *refs)
        return bound

    ordered, inverse = pl.pallas_call(
        call(order_blocks, per_owner),
        out_shape=[
            jax.ShapeDtypeStruct(spectrum.shape, BF16),
            jax.ShapeDtypeStruct((blocks,), I32),
        ],
        in_specs=[ANY, ANY],
        out_specs=[ANY, SMEM],
        scratch_shapes=[
            pltpu.VMEM(spectrum.shape, BF16),
            pltpu.SMEM((blocks,), I32),
            pltpu.SMEM((n_pen,), I32),
            pltpu.SemaphoreType.DMA,
            pltpu.SemaphoreType.DMA((blocks,)),
            pltpu.SemaphoreType.DMA((blocks,)),
        ],
        compiler_params=pltpu.CompilerParams(vmem_limit_bytes=62 << 20),
    )(owner, spectrum)
    outgoing = ordered.reshape(n_pen, per_owner, 2, depth, columns)
    incoming = lax.all_to_all(outgoing, "pen", split_axis=0, concat_axis=0, tiled=True)

    parts = pl.pallas_call(
        call(forward, n_kz, chunk, tiles_per_tilt),
        out_shape=[jax.ShapeDtypeStruct((2 * chunk, columns), F32)] * n_kz,
        in_specs=[SMEM, VMEM, VMEM, VMEM, VMEM, ANY],
        out_specs=[VMEM] * n_kz,
        scratch_shapes=[pltpu.VMEM((2 * tiles, blocks * depth), BF16)],
        compiler_params=pltpu.CompilerParams(vmem_limit_bytes=16 << 20),
    )(tilt_pos, pair_tilt, pair_tile_within, depth_weights, spectrum, inverse)

    def across(value, k):
        return lax.ppermute(value, "kz", [(i, i ^ k) for i in range(n_kz)])

    summed = [parts[0]] + [across(parts[k], k) for k in range(1, n_kz)]
    table = pl.pallas_call(
        call(adjoint_table, n_kz, chunk, per_owner, tiles_per_tilt),
        out_shape=jax.ShapeDtypeStruct((4 * tiles, 2 * per_owner * depth), BF16),
        in_specs=[SMEM, SMEM, VMEM, VMEM, VMEM],
        out_specs=VMEM,
        scratch_shapes=[pltpu.VMEM((blocks, pairs), I32)],
        compiler_params=pltpu.CompilerParams(vmem_limit_bytes=8 << 20),
    )(inverse, tilt_pos, pair_tilt, pair_tile_within, depth_weights)

    sent = measured.reshape(2, n_pen, columns).transpose(1, 0, 2)
    got = lax.all_to_all(sent, "pen", split_axis=0, concat_axis=0, tiled=True)
    measured_rows = got.transpose(1, 0, 2).reshape(2 * chunk, columns)
    total = summed[0]
    for part in summed[1:]:
        total = total + part
    own = (total - measured_rows.astype(F32)).astype(BF16)

    def between(value, k):
        return lax.ppermute(value, "pen", [(i, i ^ k) for i in range(n_pen)])

    held = jnp.concatenate([own] + [across(own, k) for k in range(1, n_kz)], axis=0)
    every = [held] + [between(held, k) for k in range(2, n_pen, 2)]
    every = [tile for kept in every for tile in (kept, between(kept, 1))]

    updated, residual = pl.pallas_call(
        call(adjoint, n_pen, chunk, per_owner),
        out_shape=[
            jax.ShapeDtypeStruct((per_owner, 2, depth, cells), BF16),
            jax.ShapeDtypeStruct((tile_dev, 2, cells), BF16),
        ],
        in_specs=[VMEM] * (n_pen + 2),
        out_specs=[ANY, VMEM],
        scratch_shapes=[
            pltpu.VMEM((n_pen, per_owner, 2, depth, columns), BF16),
            pltpu.SemaphoreType.DMA((n_pen,)),
        ],
        compiler_params=pltpu.CompilerParams(vmem_limit_bytes=16 << 20),
    )(table, incoming, *every)
    return (updated, residual)


def solution(mesh):
    return jax.shard_map(
        body,
        mesh=mesh,
        in_specs=(
            P("kz", None, None, "pen"),
            P("kz", None, None),
            P("kz", None),
            P("kz", None),
            P(),
            P("kz"),
            P(("kz", "pen"), None, None),
        ),
        out_specs=(P(("kz", "pen"), None, None, None), P(("kz", "pen"), None, None)),
        check_vma=False,
    )
```

```python
import jax
import jax.numpy as jnp
from jax import lax
from jax.experimental import pallas as pl
from jax.experimental.pallas import tpu as pltpu
from jax.sharding import PartitionSpec as P

BF16 = jnp.bfloat16
F32 = jnp.float32
I32 = jnp.int32
SMEM = pl.BlockSpec(memory_space=pltpu.SMEM)
VMEM = pl.BlockSpec(memory_space=pltpu.VMEM)
ANY = pl.BlockSpec(memory_space=pl.ANY)


def split_hi_lo(value):
    hi = value.astype(BF16)
    return hi, (value - hi.astype(F32)).astype(BF16)


def order_blocks(n_pen, per_owner, owner_ref, spectrum_ref, measured_ref, *rest):
    chips = n_pen // 2
    first_ref, outs, inverse_ref, rest = rest[0], rest[1 : 1 + chips], rest[1 + chips], rest[2 + chips :]
    held, tile, below, owner, count, owner_sem, tile_sem, in_sems, out_sems, below_sems = rest
    blocks, rows, columns = spectrum_ref.shape
    pen = lax.axis_index("pen")
    get_owner = pltpu.make_async_copy(owner_ref, owner, owner_sem)
    get_owner.start()
    get_tile = pltpu.make_async_copy(measured_ref, tile, tile_sem)
    get_tile.start()
    gets, puts = [], []
    for b in range(blocks):
        gets.append(pltpu.make_async_copy(spectrum_ref.at[b], held.at[b], in_sems.at[b]))
        gets[b].start()
    for o in range(n_pen):
        count[o] = 0
    get_owner.wait()
    for b in range(blocks):
        o = owner[b]
        r = count[o]
        count[o] = r + 1
        inverse_ref[o * per_owner + r] = b
    get_tile.wait()
    for o in range(n_pen):
        part = tile[0, :, o * columns : (o + 1) * columns].astype(F32)
        below[o] = jnp.concatenate([part, jnp.zeros((14, columns), F32)], axis=0).astype(BF16)
        puts.append(pltpu.make_async_copy(below.at[o], first_ref.at[o, pl.ds(rows, 16)], below_sems.at[o]))
        puts[-1].start()
    for get in gets:
        get.wait()
    for o in range(n_pen):
        from_ref = held.at[inverse_ref[o * per_owner]]
        puts.append(pltpu.make_async_copy(from_ref, first_ref.at[o, pl.ds(0, rows)], out_sems.at[o, 0]))
        puts[-1].start()
    for q in range(n_pen):
        for r in range(1, per_owner):
            from_ref = held.at[inverse_ref[(pen ^ q) * per_owner + r]]
            puts.append(pltpu.make_async_copy(from_ref, outs[q // 2].at[q % 2, r - 1], out_sems.at[q, r]))
            puts[-1].start()
    for put in puts:
        put.wait()


def slots(tilt_pos_ref, tilt, within, tiles_per_tilt, flip):
    place = jnp.zeros_like(tilt)
    for t in range(tilt_pos_ref.shape[0]):
        place = jnp.where(tilt == t, tilt_pos_ref[t], place)
    return (place * tiles_per_tilt + within) ^ flip


def forward(n_kz, chunk, tiles_per_tilt, tilt_pos_ref, tilt_ref, within_ref, weights_ref,
            spectrum_ref, after_ref, *rest):
    del after_ref
    outs, table = rest[:n_kz], rest[n_kz]
    blocks, pairs, depth = weights_ref.shape
    columns = spectrum_ref.shape[3]
    tiles = n_kz * chunk
    flip = lax.axis_index("kz") * chunk
    slot = slots(tilt_pos_ref, tilt_ref[...], within_ref[...], tiles_per_tilt, flip)
    rows = lax.broadcasted_iota(I32, (tiles, pairs), 0)
    for b in range(blocks):
        hot = jnp.where(slot[b : b + 1, :] == rows, 1.0, 0.0).astype(BF16)
        hi, lo = split_hi_lo(jnp.dot(hot, weights_ref[b], preferred_element_type=F32))
        table[:tiles, b * depth : (b + 1) * depth] = hi
        table[tiles:, b * depth : (b + 1) * depth] = lo
    for c in range(2):
        both = jnp.dot(
            table[...],
            spectrum_ref[:, c].reshape(blocks * depth, columns),
            preferred_element_type=F32,
        )
        total = both[:tiles] + both[tiles:]
        for k in range(n_kz):
            outs[k][c * chunk : (c + 1) * chunk, :] = total[k * chunk : (k + 1) * chunk]


def adjoint_table(n_kz, chunk, per_owner, tiles_per_tilt, inverse_ref, tilt_pos_ref, tilt_ref,
                  within_ref, weights_ref, out_ref, slot_ref):
    depth = weights_ref.shape[2]
    pairs = weights_ref.shape[1]
    rows_all = n_kz * 2 * chunk
    flip = lax.axis_index("kz") * chunk
    slot_ref[...] = slots(tilt_pos_ref, tilt_ref[...], within_ref[...], tiles_per_tilt, flip)
    rows = lax.broadcasted_iota(I32, (rows_all, pairs), 0)
    for r in range(per_owner):
        b = inverse_ref[lax.axis_index("pen") * per_owner + r]
        at = slot_ref[pl.ds(b, 1), :]
        low = at & (chunk - 1)
        for c in range(2):
            place = (at - low) * 2 + c * chunk + low
            hot = jnp.where(place == rows, -8.0, 0.0).astype(BF16)
            hi, lo = split_hi_lo(jnp.dot(hot, weights_ref[b], preferred_element_type=F32))
            first = (r * 2 + c) * depth
            out_ref[:rows_all, first : first + depth] = hi
            out_ref[rows_all:, first : first + depth] = lo


def residual_chunk(n_kz, n_pen, *refs):
    parts, first_ref = refs[:n_kz], refs[n_kz]
    out_ref, below, sems = refs[n_kz + 1 + n_pen // 2], *refs[-2:]
    skip = first_ref.shape[1] - 16
    gets = []
    for p in range(n_pen):
        from_ref = first_ref.at[p, pl.ds(skip, 16)]
        gets.append(pltpu.make_async_copy(from_ref, below.at[pl.ds(16 * p, 16)], sems.at[p]))
        gets[p].start()
    total = parts[0][...]
    for part in parts[1:]:
        total = total + part[...]
    to = lax.broadcasted_iota(I32, (2 * n_pen, 16 * n_pen), 0)
    at = lax.broadcasted_iota(I32, (2 * n_pen, 16 * n_pen), 1)
    from_row = jnp.where(to >= n_pen, (to - n_pen) * 16 + 1, to * 16)
    pick = jnp.where(at == from_row, 1.0, 0.0).astype(BF16)
    for get in gets:
        get.wait()
    measured = jnp.dot(pick, below[...], preferred_element_type=F32)
    out_ref[...] = (total - measured).astype(BF16)


def adjoint(n_pen, chunk, per_owner, table_ref, first_ref, *rest):
    chips = n_pen // 2
    kept, swapped, tile_refs, rest = rest[:chips], rest[chips:n_pen], rest[n_pen : 2 * n_pen], rest[2 * n_pen :]
    out_ref, residual_ref, made, out_sems = rest
    span, columns = swapped[0].shape[1:]
    rows = tile_refs[0].shape[0]
    pen = lax.axis_index("pen")
    puts = []
    pick_row = lax.broadcasted_iota(I32, (16, rows), 0)
    pick_at = lax.broadcasted_iota(I32, (16, rows), 1)
    pick = jnp.where(pick_at == pick_row * chunk + pen, 1.0, 0.0)
    pick = jnp.where(pick_row < 2, pick, 0.0).astype(BF16)
    for q in range(n_pen):
        first_column = pl.multiple_of((pen ^ q) * columns, columns)
        later = swapped[q // 2] if q % 2 else kept[q // 2].at[0]
        here = tile_refs[q][...]
        own = jnp.dot(pick, here, preferred_element_type=F32)
        residual_ref[0, :, pl.ds(first_column, columns)] = own[:2].astype(BF16)
        step = lax.dot_general(
            table_ref[...],
            jnp.concatenate([here, here], axis=0),
            (((0,), (0,)), ((), ())),
            preferred_element_type=F32,
        )
        for r in range(per_owner):
            held = later[r - 1] if r else first_ref[pen ^ q, :span]
            made[q, r] = (held.astype(F32) + step[r * span : (r + 1) * span]).astype(BF16)
        to = out_ref.at[:, :, pl.ds(first_column, columns)]
        puts.append(pltpu.make_async_copy(made.at[q], to, out_sems.at[q]))
        puts[-1].start()
    for put in puts:
        put.wait()


def body(spectrum, depth_weights, pair_tilt, pair_tile_within, tilt_pos, owner, measured):
    n_pen = lax.axis_size("pen")
    n_kz = lax.axis_size("kz")
    blocks, _, depth, columns = spectrum.shape
    per_owner = blocks // n_pen
    pairs = depth_weights.shape[1]
    tile_dev, _, cells = measured.shape
    chunk = tile_dev * n_pen
    tiles = chunk * n_kz
    tiles_per_tilt = tiles // tilt_pos.shape[0]
    chips = n_pen // 2

    def call(kernel, *static):
        def bound(*refs):
            return kernel(*static, *refs)
        return bound

    def across(value, k):
        return lax.ppermute(value, "kz", [(i, i ^ k) for i in range(n_kz)])

    def between(value, k):
        return lax.ppermute(value, "pen", [(i, i ^ k) for i in range(n_pen)])

    span = 2 * depth
    first, *outs, inverse = pl.pallas_call(
        call(order_blocks, n_pen, per_owner),
        out_shape=[jax.ShapeDtypeStruct((n_pen, span + 16, columns), BF16)]
        + [jax.ShapeDtypeStruct((2, per_owner - 1, span, columns), BF16)] * chips
        + [jax.ShapeDtypeStruct((blocks,), I32)],
        in_specs=[ANY, ANY, ANY],
        out_specs=[ANY] * (chips + 1) + [SMEM],
        scratch_shapes=[
            pltpu.VMEM((blocks, span, columns), BF16),
            pltpu.VMEM(measured.shape, BF16),
            pltpu.VMEM((n_pen, 16, columns), BF16),
            pltpu.SMEM((blocks,), I32),
            pltpu.SMEM((n_pen,), I32),
            pltpu.SemaphoreType.DMA,
            pltpu.SemaphoreType.DMA,
            pltpu.SemaphoreType.DMA((blocks,)),
            pltpu.SemaphoreType.DMA((n_pen, per_owner)),
            pltpu.SemaphoreType.DMA((n_pen,)),
        ],
        compiler_params=pltpu.CompilerParams(vmem_limit_bytes=62 << 20),
    )(owner, spectrum.reshape(blocks, span, columns), measured)
    first = lax.all_to_all(first, "pen", split_axis=0, concat_axis=0, tiled=True)

    parts = pl.pallas_call(
        call(forward, n_kz, chunk, tiles_per_tilt),
        out_shape=[jax.ShapeDtypeStruct((2 * chunk, columns), F32)] * n_kz,
        in_specs=[SMEM, VMEM, VMEM, VMEM, VMEM, ANY],
        out_specs=[VMEM] * n_kz,
        scratch_shapes=[pltpu.VMEM((2 * tiles, blocks * depth), BF16)],
        compiler_params=pltpu.CompilerParams(vmem_limit_bytes=16 << 20),
    )(tilt_pos, pair_tilt, pair_tile_within, depth_weights, spectrum, inverse)

    summed = [parts[0]] + [across(parts[k], k) for k in range(1, n_kz)]
    table = pl.pallas_call(
        call(adjoint_table, n_kz, chunk, per_owner, tiles_per_tilt),
        out_shape=jax.ShapeDtypeStruct((4 * tiles, 2 * per_owner * depth), BF16),
        in_specs=[SMEM, SMEM, VMEM, VMEM, VMEM],
        out_specs=VMEM,
        scratch_shapes=[pltpu.VMEM((blocks, pairs), I32)],
        compiler_params=pltpu.CompilerParams(vmem_limit_bytes=8 << 20),
    )(inverse, tilt_pos, pair_tilt, pair_tile_within, depth_weights)

    own, *outs = pl.pallas_call(
        call(residual_chunk, n_kz, n_pen),
        out_shape=[jax.ShapeDtypeStruct((2 * chunk, columns), BF16)]
        + [jax.ShapeDtypeStruct(out.shape, BF16) for out in outs],
        in_specs=[VMEM] * n_kz + [ANY] * (chips + 1),
        out_specs=[VMEM] + [ANY] * chips,
        scratch_shapes=[
            pltpu.VMEM((16 * n_pen, columns), BF16),
            pltpu.SemaphoreType.DMA((n_pen,)),
        ],
        input_output_aliases={n_kz + 1 + i: 1 + i for i in range(chips)},
        compiler_params=pltpu.CompilerParams(vmem_limit_bytes=56 << 20),
    )(*summed, first, *outs)
    kept = [outs[0]] + [between(outs[i], 2 * i) for i in range(1, chips)]

    held = own
    step = 1
    while step < n_kz:
        held = jnp.concatenate([held, across(held, step)], axis=0)
        step *= 2
    every = [held] + [between(held, k) for k in range(2, n_pen, 2)]
    every = [tile for one in every for tile in (one, between(one, 1))]
    swapped = [between(one[1], 1) for one in kept]

    updated, residual = pl.pallas_call(
        call(adjoint, n_pen, chunk, per_owner),
        out_shape=[
            jax.ShapeDtypeStruct((per_owner, span, cells), BF16),
            jax.ShapeDtypeStruct((tile_dev, 2, cells), BF16),
        ],
        in_specs=[VMEM] * (2 * n_pen + 2),
        out_specs=[ANY, VMEM],
        scratch_shapes=[
            pltpu.VMEM((n_pen, per_owner, span, columns), BF16),
            pltpu.SemaphoreType.DMA((n_pen,)),
        ],
        compiler_params=pltpu.CompilerParams(vmem_limit_bytes=16 << 20),
    )(table, first, *kept, *swapped, *every)
    updated = updated.reshape(per_owner, 2, depth, cells)
    return (updated, residual)


def solution(mesh):
    return jax.shard_map(
        body,
        mesh=mesh,
        in_specs=(
            P("kz", None, None, "pen"),
            P("kz", None, None),
            P("kz", None),
            P("kz", None),
            P(),
            P("kz"),
            P(("kz", "pen"), None, None),
        ),
        out_specs=(P(("kz", "pen"), None, None, None), P(("kz", "pen"), None, None)),
        check_vma=False,
    )
```

```python
import jax
import jax.numpy as jnp
from jax import lax
from jax.experimental import pallas as pl
from jax.experimental.pallas import tpu as pltpu
from jax.sharding import PartitionSpec as P

BF16 = jnp.bfloat16
F32 = jnp.float32
I32 = jnp.int32
SMEM = pl.BlockSpec(memory_space=pltpu.SMEM)
VMEM = pl.BlockSpec(memory_space=pltpu.VMEM)
ANY = pl.BlockSpec(memory_space=pl.ANY)


def split_hi_lo(value):
    hi = value.astype(BF16)
    return hi, (value - hi.astype(F32)).astype(BF16)


def order_blocks(n_pen, per_owner, owner_ref, spectrum_ref, *rest):
    chips = n_pen // 2
    outs, (inverse_ref, held, owner, count, owner_sem, in_sems, out_sems) = rest[:chips], rest[chips:]
    blocks = spectrum_ref.shape[0]
    pen = lax.axis_index("pen")
    get_owner = pltpu.make_async_copy(owner_ref, owner, owner_sem)
    get_owner.start()
    gets, puts = [], []
    for b in range(blocks):
        gets.append(pltpu.make_async_copy(spectrum_ref.at[b], held.at[b], in_sems.at[b]))
        gets[b].start()
    for o in range(n_pen):
        count[o] = 0
    get_owner.wait()
    for b in range(blocks):
        o = owner[b]
        r = count[o]
        count[o] = r + 1
        inverse_ref[o * per_owner + r] = b
    for get in gets:
        get.wait()
    for q in range(n_pen):
        for r in range(per_owner):
            from_ref = held.at[inverse_ref[(pen ^ q) * per_owner + r]]
            puts.append(pltpu.make_async_copy(from_ref, outs[q // 2].at[q % 2, r], out_sems.at[q, r]))
            puts[-1].start()
    for put in puts:
        put.wait()


def slots(tilt_pos_ref, tilt, within, tiles_per_tilt, flip):
    place = jnp.zeros_like(tilt)
    for t in range(tilt_pos_ref.shape[0]):
        place = jnp.where(tilt == t, tilt_pos_ref[t], place)
    return (place * tiles_per_tilt + within) ^ flip


def forward(n_kz, chunk, tiles_per_tilt, tilt_pos_ref, tilt_ref, within_ref, weights_ref,
            spectrum_ref, after_ref, kept_ref, sent_ref, table):
    del after_ref
    blocks, pairs, depth = weights_ref.shape
    columns = spectrum_ref.shape[3]
    tiles = n_kz * chunk
    flip = lax.axis_index("kz") * chunk
    slot = slots(tilt_pos_ref, tilt_ref[...], within_ref[...], tiles_per_tilt, flip)
    rows = lax.broadcasted_iota(I32, (tiles, pairs), 0)
    for b in range(blocks):
        hot = jnp.where(slot[b : b + 1, :] == rows, 1.0, 0.0).astype(BF16)
        hi, lo = split_hi_lo(jnp.dot(hot, weights_ref[b], preferred_element_type=F32))
        table[:tiles, b * depth : (b + 1) * depth] = hi
        table[tiles:, b * depth : (b + 1) * depth] = lo
    for c in range(2):
        both = jnp.dot(
            table[...],
            spectrum_ref[:, c].reshape(blocks * depth, columns),
            preferred_element_type=F32,
        )
        total = both[:tiles] + both[tiles:]
        for k in range(n_kz):
            out_ref = sent_ref if k % 2 else kept_ref
            out_ref[k // 2, c * chunk : (c + 1) * chunk, :] = total[k * chunk : (k + 1) * chunk]


def adjoint_table(n_kz, chunk, per_owner, tiles_per_tilt, inverse_ref, tilt_pos_ref, tilt_ref,
                  within_ref, weights_ref, out_ref, slot_ref):
    depth = weights_ref.shape[2]
    pairs = weights_ref.shape[1]
    rows_all = n_kz * 2 * chunk
    flip = lax.axis_index("kz") * chunk
    slot_ref[...] = slots(tilt_pos_ref, tilt_ref[...], within_ref[...], tiles_per_tilt, flip)
    rows = lax.broadcasted_iota(I32, (rows_all, pairs), 0)
    for r in range(per_owner):
        b = inverse_ref[lax.axis_index("pen") * per_owner + r]
        at = slot_ref[pl.ds(b, 1), :]
        low = at & (chunk - 1)
        for c in range(2):
            place = (at - low) * 2 + c * chunk + low
            hot = jnp.where(place == rows, -8.0, 0.0).astype(BF16)
            hi, lo = split_hi_lo(jnp.dot(hot, weights_ref[b], preferred_element_type=F32))
            first = (c * per_owner + r) * depth
            out_ref[:rows_all, first : first + depth] = hi
            out_ref[rows_all:, first : first + depth] = lo


def other_core(*refs):
    count = len(refs) // 2
    in_refs, out_refs = refs[: count - 1], refs[count:-1]
    sems = refs[-1]
    copies = []
    for i, (in_ref, out_ref) in enumerate(zip(in_refs, out_refs)):
        copies.append(pltpu.make_async_copy(in_ref.at[1], out_ref, sems.at[i]))
        copies[i].start()
    for copy in copies:
        copy.wait()


def adjoint(n_pen, chunk, per_owner, table_ref, *rest):
    chips = n_pen // 2
    kept, swapped, tile_refs, rest = rest[:chips], rest[chips:n_pen], rest[n_pen : 2 * n_pen], rest[2 * n_pen :]
    out_ref, residual_ref, made, out_sems = rest
    depth, columns = swapped[0].shape[2:]
    rows = tile_refs[0].shape[0]
    pen = lax.axis_index("pen")
    puts = []
    pick_row = lax.broadcasted_iota(I32, (16, rows), 0)
    pick_at = lax.broadcasted_iota(I32, (16, rows), 1)
    pick = jnp.where(pick_at == pick_row * chunk + pen, 1.0, 0.0)
    pick = jnp.where(pick_row < 2, pick, 0.0).astype(BF16)
    for q in range(n_pen):
        first_column = pl.multiple_of((pen ^ q) * columns, columns)
        blocks = swapped[q // 2] if q % 2 else kept[q // 2].at[0]
        here = tile_refs[q][...]
        own = jnp.dot(pick, here, preferred_element_type=F32)
        residual_ref[0, :, pl.ds(first_column, columns)] = own[:2].astype(BF16)
        step = lax.dot_general(
            table_ref[...],
            jnp.concatenate([here, here], axis=0),
            (((0,), (0,)), ((), ())),
            preferred_element_type=F32,
        )
        for r in range(per_owner):
            for c in range(2):
                first = (c * per_owner + r) * depth
                held = blocks[r, c].astype(F32)
                made[q, r, c] = (held + step[first : first + depth]).astype(BF16)
        to = out_ref.at[:, :, :, pl.ds(first_column, columns)]
        puts.append(pltpu.make_async_copy(made.at[q], to, out_sems.at[q]))
        puts[-1].start()
    for put in puts:
        put.wait()


def body(spectrum, depth_weights, pair_tilt, pair_tile_within, tilt_pos, owner, measured):
    n_pen = lax.axis_size("pen")
    n_kz = lax.axis_size("kz")
    blocks, _, depth, columns = spectrum.shape
    per_owner = blocks // n_pen
    pairs = depth_weights.shape[1]
    tile_dev, _, cells = measured.shape
    chunk = tile_dev * n_pen
    tiles = chunk * n_kz
    tiles_per_tilt = tiles // tilt_pos.shape[0]

    chips = n_pen // 2

    def call(kernel, *static):
        def bound(*refs):
            return kernel(*static, *refs)
        return bound

    def across(value, k):
        return lax.ppermute(value, "kz", [(i, i ^ k) for i in range(n_kz)])

    def between(value, k):
        return lax.ppermute(value, "pen", [(i, i ^ k) for i in range(n_pen)])

    *outs, inverse = pl.pallas_call(
        call(order_blocks, n_pen, per_owner),
        out_shape=[jax.ShapeDtypeStruct((2, per_owner, 2, depth, columns), BF16)] * chips
        + [jax.ShapeDtypeStruct((blocks,), I32)],
        in_specs=[ANY, ANY],
        out_specs=[ANY] * chips + [SMEM],
        scratch_shapes=[
            pltpu.VMEM(spectrum.shape, BF16),
            pltpu.SMEM((blocks,), I32),
            pltpu.SMEM((n_pen,), I32),
            pltpu.SemaphoreType.DMA,
            pltpu.SemaphoreType.DMA((blocks,)),
            pltpu.SemaphoreType.DMA((n_pen, per_owner)),
        ],
        compiler_params=pltpu.CompilerParams(vmem_limit_bytes=62 << 20),
    )(owner, spectrum)
    far_first = [between(outs[i], 2 * i) for i in range(chips - 1, 0, -1)]
    kept = [outs[0]] + far_first[::-1]

    sums, sent = pl.pallas_call(
        call(forward, n_kz, chunk, tiles_per_tilt),
        out_shape=[jax.ShapeDtypeStruct((n_kz // 2, 2 * chunk, columns), F32)] * 2,
        in_specs=[SMEM, VMEM, VMEM, VMEM, VMEM, ANY],
        out_specs=[VMEM, VMEM],
        scratch_shapes=[pltpu.VMEM((2 * tiles, blocks * depth), BF16)],
        compiler_params=pltpu.CompilerParams(vmem_limit_bytes=16 << 20),
    )(tilt_pos, pair_tilt, pair_tile_within, depth_weights, spectrum, inverse)
    sums = sums + across(sent, 1)
    step = 2
    while step < n_kz:
        sums = sums.reshape(-1, 2, 2 * chunk, columns)
        sums = sums[:, 0] + across(sums[:, 1], step)
        step *= 2

    table = pl.pallas_call(
        call(adjoint_table, n_kz, chunk, per_owner, tiles_per_tilt),
        out_shape=jax.ShapeDtypeStruct((4 * tiles, 2 * per_owner * depth), BF16),
        in_specs=[SMEM, SMEM, VMEM, VMEM, VMEM],
        out_specs=VMEM,
        scratch_shapes=[pltpu.VMEM((blocks, pairs), I32)],
        compiler_params=pltpu.CompilerParams(vmem_limit_bytes=8 << 20),
    )(inverse, tilt_pos, pair_tilt, pair_tile_within, depth_weights)

    sent = measured.reshape(2, n_pen, columns).transpose(1, 0, 2)
    got = lax.all_to_all(sent, "pen", split_axis=0, concat_axis=0, tiled=True)
    measured_rows = got.transpose(1, 0, 2).reshape(2 * chunk, columns)
    own = (sums.reshape(2 * chunk, columns) - measured_rows.astype(F32)).astype(BF16)

    held = own
    step = 1
    while step < n_kz:
        held = jnp.concatenate([held, across(held, step)], axis=0)
        step *= 2
    other = pl.pallas_call(
        other_core,
        out_shape=[jax.ShapeDtypeStruct(outs[0].shape[1:], BF16)] * (chips - 1),
        in_specs=[ANY] * chips,
        out_specs=[ANY] * (chips - 1),
        scratch_shapes=[pltpu.SemaphoreType.DMA((chips - 1,))],
        compiler_params=pltpu.CompilerParams(vmem_limit_bytes=8 << 20),
    )(*kept[1:], held)
    swapped = [between(one, 1) for one in [outs[0][1], *other]]
    every = [held] + [between(held, k) for k in range(2, n_pen, 2)]
    every = [tile for one in every for tile in (one, between(one, 1))]

    updated, residual = pl.pallas_call(
        call(adjoint, n_pen, chunk, per_owner),
        out_shape=[
            jax.ShapeDtypeStruct((per_owner, 2, depth, cells), BF16),
            jax.ShapeDtypeStruct((tile_dev, 2, cells), BF16),
        ],
        in_specs=[VMEM] * (2 * n_pen + 1),
        out_specs=[ANY, VMEM],
        scratch_shapes=[
            pltpu.VMEM((n_pen, per_owner, 2, depth, columns), BF16),
            pltpu.SemaphoreType.DMA((n_pen,)),
        ],
        compiler_params=pltpu.CompilerParams(vmem_limit_bytes=16 << 20),
    )(table, *kept, *swapped, *every)
    return (updated, residual)


def solution(mesh):
    return jax.shard_map(
        body,
        mesh=mesh,
        in_specs=(
            P("kz", None, None, "pen"),
            P("kz", None, None),
            P("kz", None),
            P("kz", None),
            P(),
            P("kz"),
            P(("kz", "pen"), None, None),
        ),
        out_specs=(P(("kz", "pen"), None, None, None), P(("kz", "pen"), None, None)),
        check_vma=False,
    )
```

```python
import jax
import jax.numpy as jnp
from jax import lax
from jax.experimental import pallas as pl
from jax.experimental.pallas import tpu as pltpu
from jax.sharding import PartitionSpec as P

BF16 = jnp.bfloat16
F32 = jnp.float32
I32 = jnp.int32
SMEM = pl.BlockSpec(memory_space=pltpu.SMEM)
VMEM = pl.BlockSpec(memory_space=pltpu.VMEM)
ANY = pl.BlockSpec(memory_space=pl.ANY)


def split_hi_lo(value):
    hi = value.astype(BF16)
    return hi, (value - hi.astype(F32)).astype(BF16)


def distance(n_pen, q):
    return (n_pen - q // 2 * 2) % n_pen + q % 2


def slots(tilt_pos_ref, tilt, within, tiles_per_tilt, flip):
    place = jnp.zeros_like(tilt)
    for t in range(tilt_pos_ref.shape[0]):
        place = jnp.where(tilt == t, tilt_pos_ref[t], place)
    return (place * tiles_per_tilt + within) ^ flip


def order_and_forward(n_pen, n_kz, chunk, per_owner, tiles_per_tilt, owner_ref, tilt_pos_ref, tilt_ref,
                      within_ref, weights_ref, spectrum_ref, *rest):
    chips = n_pen // 2
    outs, rest = rest[:chips], rest[chips:]
    inverse_ref, kept_ref, sent_ref, held, owner, tilt_pos, tilt, within, weights, rest = *rest[:9], rest[9:]
    count, table, kept, sent, small_sems, in_sems, out_sems, sum_sems = rest
    blocks, pairs, depth = weights_ref.shape
    columns = spectrum_ref.shape[3]
    tiles = n_kz * chunk
    pen = lax.axis_index("pen")
    small = []
    for i, (from_ref, to) in enumerate(
        ((owner_ref, owner), (tilt_pos_ref, tilt_pos), (tilt_ref, tilt), (within_ref, within), (weights_ref, weights))
    ):
        small.append(pltpu.make_async_copy(from_ref, to, small_sems.at[i]))
        small[i].start()
    gets, puts = [], []
    for b in range(blocks):
        gets.append(pltpu.make_async_copy(spectrum_ref.at[b], held.at[b], in_sems.at[b]))
        gets[b].start()
    for o in range(n_pen):
        count[o] = 0
    for copy in small:
        copy.wait()
    for b in range(blocks):
        o = owner[b]
        r = count[o]
        count[o] = r + 1
        inverse_ref[o * per_owner + r] = b
    slot = slots(tilt_pos, tilt[...], within[...], tiles_per_tilt, lax.axis_index("kz") * chunk)
    rows = lax.broadcasted_iota(I32, (tiles, pairs), 0)
    for b in range(blocks):
        hot = jnp.where(slot[b : b + 1, :] == rows, 1.0, 0.0).astype(BF16)
        hi, lo = split_hi_lo(jnp.dot(hot, weights[b], preferred_element_type=F32))
        table[:tiles, b * depth : (b + 1) * depth] = hi
        table[tiles:, b * depth : (b + 1) * depth] = lo
    for get in gets:
        get.wait()
    for q in range(n_pen):
        for r in range(per_owner):
            from_ref = held.at[inverse_ref[(pen ^ distance(n_pen, q)) * per_owner + r]]
            puts.append(pltpu.make_async_copy(from_ref, outs[q // 2].at[q % 2, r], out_sems.at[q, r]))
            puts[-1].start()
    for c in range(2):
        both = jnp.dot(
            table[...],
            held[:, c].reshape(blocks * depth, columns),
            preferred_element_type=F32,
        )
        total = both[:tiles] + both[tiles:]
        for k in range(n_kz):
            to = sent if k % 2 else kept
            to[k // 2, c * chunk : (c + 1) * chunk, :] = total[k * chunk : (k + 1) * chunk]
    puts.append(pltpu.make_async_copy(kept, kept_ref, sum_sems.at[0]))
    puts[-1].start()
    puts.append(pltpu.make_async_copy(sent, sent_ref, sum_sems.at[1]))
    puts[-1].start()
    for put in puts:
        put.wait()


def residual_and_table(n_kz, chunk, per_owner, tiles_per_tilt, inverse_ref, tilt_pos_ref, tilt_ref, within_ref,
                       weights_ref, sums_ref, arrived_ref, measured_ref, own_ref, out_ref, slot_ref):
    own_ref[...] = (sums_ref[...] + arrived_ref[...] - measured_ref[...].astype(F32)).astype(BF16)
    pairs, depth = weights_ref.shape[1:]
    rows_all = n_kz * 2 * chunk
    flip = lax.axis_index("kz") * chunk
    slot_ref[...] = slots(tilt_pos_ref, tilt_ref[...], within_ref[...], tiles_per_tilt, flip)
    rows = lax.broadcasted_iota(I32, (rows_all, pairs), 0)
    for r in range(per_owner):
        b = inverse_ref[lax.axis_index("pen") * per_owner + r]
        at = slot_ref[pl.ds(b, 1), :]
        low = at & (chunk - 1)
        for c in range(2):
            place = (at - low) * 2 + c * chunk + low
            hot = jnp.where(place == rows, -8.0, 0.0).astype(BF16)
            hi, lo = split_hi_lo(jnp.dot(hot, weights_ref[b], preferred_element_type=F32))
            first = (c * per_owner + r) * depth
            out_ref[:rows_all, first : first + depth] = hi
            out_ref[rows_all:, first : first + depth] = lo


def other_core(*refs):
    count = len(refs) // 2
    in_refs, out_refs = refs[: count - 1], refs[count:-1]
    sems = refs[-1]
    copies = []
    for i, (in_ref, out_ref) in enumerate(zip(in_refs, out_refs)):
        copies.append(pltpu.make_async_copy(in_ref.at[1], out_ref, sems.at[i]))
        copies[i].start()
    for copy in copies:
        copy.wait()


def adjoint(n_pen, chunk, per_owner, table_ref, *rest):
    chips = n_pen // 2
    kept, swapped, tile_refs, rest = rest[:chips], rest[chips:n_pen], rest[n_pen : 2 * n_pen], rest[2 * n_pen :]
    out_ref, residual_ref, made, out_sems = rest
    depth, columns = swapped[0].shape[2:]
    rows = tile_refs[0].shape[0]
    pen = lax.axis_index("pen")
    puts = []
    pick_row = lax.broadcasted_iota(I32, (16, rows), 0)
    pick_at = lax.broadcasted_iota(I32, (16, rows), 1)
    pick = jnp.where(pick_at == pick_row * chunk + pen, 1.0, 0.0)
    pick = jnp.where(pick_row < 2, pick, 0.0).astype(BF16)
    for q in range(n_pen):
        first_column = pl.multiple_of((pen ^ distance(n_pen, q)) * columns, columns)
        blocks = swapped[q // 2] if q % 2 else kept[q // 2].at[0]
        here = tile_refs[q][...]
        own = jnp.dot(pick, here, preferred_element_type=F32)
        residual_ref[0, :, pl.ds(first_column, columns)] = own[:2].astype(BF16)
        step = lax.dot_general(
            table_ref[...],
            jnp.concatenate([here, here], axis=0),
            (((0,), (0,)), ((), ())),
            preferred_element_type=F32,
        )
        for r in range(per_owner):
            for c in range(2):
                first = (c * per_owner + r) * depth
                held = blocks[r, c].astype(F32)
                made[q, r, c] = (held + step[first : first + depth]).astype(BF16)
        to = out_ref.at[:, :, :, pl.ds(first_column, columns)]
        puts.append(pltpu.make_async_copy(made.at[q], to, out_sems.at[q]))
        puts[-1].start()
    for put in puts:
        put.wait()


def body(spectrum, depth_weights, pair_tilt, pair_tile_within, tilt_pos, owner, measured):
    n_pen = lax.axis_size("pen")
    n_kz = lax.axis_size("kz")
    blocks, _, depth, columns = spectrum.shape
    per_owner = blocks // n_pen
    pairs = depth_weights.shape[1]
    tile_dev, _, cells = measured.shape
    chunk = tile_dev * n_pen
    tiles = chunk * n_kz
    tiles_per_tilt = tiles // tilt_pos.shape[0]

    chips = n_pen // 2

    def call(kernel, *static):
        def bound(*refs):
            return kernel(*static, *refs)
        return bound

    def across(value, k):
        return lax.ppermute(value, "kz", [(i, i ^ k) for i in range(n_kz)])

    def between(value, k):
        return lax.ppermute(value, "pen", [(i, i ^ k) for i in range(n_pen)])

    group = jax.ShapeDtypeStruct((n_kz // 2, 2 * chunk, columns), F32)
    *outs, inverse, sums, sent_sums = pl.pallas_call(
        call(order_and_forward, n_pen, n_kz, chunk, per_owner, tiles_per_tilt),
        out_shape=[jax.ShapeDtypeStruct((2, per_owner, 2, depth, columns), BF16)] * chips
        + [jax.ShapeDtypeStruct((blocks,), I32), group, group],
        in_specs=[ANY] * 6,
        out_specs=[ANY] * chips + [SMEM, ANY, ANY],
        scratch_shapes=[
            pltpu.VMEM(spectrum.shape, BF16),
            pltpu.SMEM((blocks,), I32),
            pltpu.SMEM(tilt_pos.shape, I32),
            pltpu.VMEM(pair_tilt.shape, I32),
            pltpu.VMEM(pair_tile_within.shape, I32),
            pltpu.VMEM(depth_weights.shape, BF16),
            pltpu.SMEM((n_pen,), I32),
            pltpu.VMEM((2 * tiles, blocks * depth), BF16),
            pltpu.VMEM(group.shape, F32),
            pltpu.VMEM(group.shape, F32),
            pltpu.SemaphoreType.DMA((5,)),
            pltpu.SemaphoreType.DMA((blocks,)),
            pltpu.SemaphoreType.DMA((n_pen, per_owner)),
            pltpu.SemaphoreType.DMA((2,)),
        ],
        compiler_params=pltpu.CompilerParams(vmem_limit_bytes=62 << 20),
    )(owner, tilt_pos, pair_tilt, pair_tile_within, depth_weights, spectrum)
    kept = [outs[0]] + [between(outs[i], distance(n_pen, 2 * i)) for i in range(1, chips)]

    arrived = across(sent_sums, 1)
    step = 2
    while step < n_kz:
        sums = (sums + arrived).reshape(-1, 2, 2 * chunk, columns)
        sums, arrived = sums[:, 0], across(sums[:, 1], step)
        step *= 2

    sent = measured.reshape(2, n_pen, columns).transpose(1, 0, 2)
    got = lax.all_to_all(sent, "pen", split_axis=0, concat_axis=0, tiled=True)
    measured_rows = got.transpose(1, 0, 2).reshape(2 * chunk, columns)
    own, table = pl.pallas_call(
        call(residual_and_table, n_kz, chunk, per_owner, tiles_per_tilt),
        out_shape=[
            jax.ShapeDtypeStruct((2 * chunk, columns), BF16),
            jax.ShapeDtypeStruct((4 * tiles, 2 * per_owner * depth), BF16),
        ],
        in_specs=[SMEM, SMEM] + [VMEM] * 6,
        out_specs=[VMEM, VMEM],
        scratch_shapes=[pltpu.VMEM((blocks, pairs), I32)],
        compiler_params=pltpu.CompilerParams(vmem_limit_bytes=8 << 20),
    )(
        inverse,
        tilt_pos,
        pair_tilt,
        pair_tile_within,
        depth_weights,
        sums.reshape(2 * chunk, columns),
        arrived.reshape(2 * chunk, columns),
        measured_rows,
    )

    held = own
    step = 1
    while step < n_kz:
        held = jnp.concatenate([held, across(held, step)], axis=0)
        step *= 2
    other = pl.pallas_call(
        other_core,
        out_shape=[jax.ShapeDtypeStruct(outs[0].shape[1:], BF16)] * (chips - 1),
        in_specs=[ANY] * chips,
        out_specs=[ANY] * (chips - 1),
        scratch_shapes=[pltpu.SemaphoreType.DMA((chips - 1,))],
        compiler_params=pltpu.CompilerParams(vmem_limit_bytes=8 << 20),
    )(*kept[1:], held)
    swapped = [between(one, 1) for one in [outs[0][1], *other]]
    every = [held] + [between(held, distance(n_pen, 2 * i)) for i in range(1, chips)]
    every = [tile for one in every for tile in (one, between(one, 1))]

    updated, residual = pl.pallas_call(
        call(adjoint, n_pen, chunk, per_owner),
        out_shape=[
            jax.ShapeDtypeStruct((per_owner, 2, depth, cells), BF16),
            jax.ShapeDtypeStruct((tile_dev, 2, cells), BF16),
        ],
        in_specs=[VMEM] * (2 * n_pen + 1),
        out_specs=[ANY, VMEM],
        scratch_shapes=[
            pltpu.VMEM((n_pen, per_owner, 2, depth, columns), BF16),
            pltpu.SemaphoreType.DMA((n_pen,)),
        ],
        compiler_params=pltpu.CompilerParams(vmem_limit_bytes=16 << 20),
    )(table, *kept, *swapped, *every)
    return (updated, residual)


def solution(mesh):
    return jax.shard_map(
        body,
        mesh=mesh,
        in_specs=(
            P("kz", None, None, "pen"),
            P("kz", None, None),
            P("kz", None),
            P("kz", None),
            P(),
            P("kz"),
            P(("kz", "pen"), None, None),
        ),
        out_specs=(P(("kz", "pen"), None, None, None), P(("kz", "pen"), None, None)),
        check_vma=False,
    )
```

```python
import jax
import jax.numpy as jnp
from jax import lax
from jax.experimental import pallas as pl
from jax.experimental.pallas import tpu as pltpu
from jax.sharding import PartitionSpec as P

BF16 = jnp.bfloat16
F32 = jnp.float32
I32 = jnp.int32
SMEM = pl.BlockSpec(memory_space=pltpu.SMEM)
VMEM = pl.BlockSpec(memory_space=pltpu.VMEM)
ANY = pl.BlockSpec(memory_space=pl.ANY)


def split_hi_lo(value):
    hi = value.astype(BF16)
    return hi, (value - hi.astype(F32)).astype(BF16)


def distance(n_pen, q):
    return (n_pen - q // 2 * 2) % n_pen + q % 2


def slots(tilt_pos_ref, tilt, within, tiles_per_tilt, flip):
    place = jnp.zeros_like(tilt)
    for t in range(tilt_pos_ref.shape[0]):
        place = jnp.where(tilt == t, tilt_pos_ref[t], place)
    return (place * tiles_per_tilt + within) ^ flip


def order_and_forward(n_pen, n_kz, chunk, per_owner, tiles_per_tilt, owner_ref, tilt_pos_ref, tilt_ref,
                      within_ref, weights_ref, spectrum_ref, *rest):
    chips = n_pen // 2
    outs, rest = rest[:chips], rest[chips:]
    inverse_ref, kept_ref, sent_ref, held, owner, tilt_pos, tilt, within, weights, rest = *rest[:9], rest[9:]
    count, table, kept, sent, small_sems, in_sems, out_sems, sum_sems = rest
    blocks, pairs, depth = weights_ref.shape
    columns = spectrum_ref.shape[3]
    tiles = n_kz * chunk
    pen = lax.axis_index("pen")
    small = []
    for i, (from_ref, to) in enumerate(
        ((owner_ref, owner), (tilt_pos_ref, tilt_pos), (tilt_ref, tilt), (within_ref, within), (weights_ref, weights))
    ):
        small.append(pltpu.make_async_copy(from_ref, to, small_sems.at[i]))
        small[i].start()
    gets, puts = [], []
    for b in range(blocks):
        gets.append(pltpu.make_async_copy(spectrum_ref.at[b], held.at[b], in_sems.at[b]))
        gets[b].start()
    for o in range(n_pen):
        count[o] = 0
    for copy in small:
        copy.wait()
    for b in range(blocks):
        o = owner[b]
        r = count[o]
        count[o] = r + 1
        inverse_ref[o * per_owner + r] = b
    slot = slots(tilt_pos, tilt[...], within[...], tiles_per_tilt, lax.axis_index("kz") * chunk)
    rows = lax.broadcasted_iota(I32, (tiles, pairs), 0)
    for b in range(blocks):
        hot = jnp.where(slot[b : b + 1, :] == rows, 1.0, 0.0).astype(BF16)
        hi, lo = split_hi_lo(jnp.dot(hot, weights[b], preferred_element_type=F32))
        table[:tiles, b * depth : (b + 1) * depth] = hi
        table[tiles:, b * depth : (b + 1) * depth] = lo
    for get in gets:
        get.wait()
    for q in range(n_pen):
        for r in range(per_owner):
            from_ref = held.at[inverse_ref[(pen ^ distance(n_pen, q)) * per_owner + r]]
            puts.append(pltpu.make_async_copy(from_ref, outs[q // 2].at[q % 2, r], out_sems.at[q, r]))
            puts[-1].start()
    for c in range(2):
        both = jnp.dot(
            table[...],
            held[:, c].reshape(blocks * depth, columns),
            preferred_element_type=F32,
        )
        total = both[:tiles] + both[tiles:]
        for k in range(n_kz):
            to = sent if k % 2 else kept
            to[k // 2, c * chunk : (c + 1) * chunk, :] = total[k * chunk : (k + 1) * chunk]
    puts.append(pltpu.make_async_copy(kept, kept_ref, sum_sems.at[0]))
    puts[-1].start()
    puts.append(pltpu.make_async_copy(sent, sent_ref, sum_sems.at[1]))
    puts[-1].start()
    for put in puts:
        put.wait()


def residual_and_table(n_kz, chunk, per_owner, tiles_per_tilt, inverse_ref, tilt_pos_ref, tilt_ref, within_ref,
                       weights_ref, sums_ref, arrived_ref, measured_ref, own_ref, out_ref, slot_ref):
    own_ref[...] = (sums_ref[...] + arrived_ref[...] - measured_ref[...].astype(F32)).astype(BF16)
    pairs, depth = weights_ref.shape[1:]
    rows_all = n_kz * 2 * chunk
    flip = lax.axis_index("kz") * chunk
    slot_ref[...] = slots(tilt_pos_ref, tilt_ref[...], within_ref[...], tiles_per_tilt, flip)
    rows = lax.broadcasted_iota(I32, (rows_all, pairs), 0)
    for r in range(per_owner):
        b = inverse_ref[lax.axis_index("pen") * per_owner + r]
        at = slot_ref[pl.ds(b, 1), :]
        low = at & (chunk - 1)
        for c in range(2):
            place = (at - low) * 2 + c * chunk + low
            hot = jnp.where(place == rows, -8.0, 0.0).astype(BF16)
            hi, lo = split_hi_lo(jnp.dot(hot, weights_ref[b], preferred_element_type=F32))
            first = (c * per_owner + r) * depth
            out_ref[:rows_all, first : first + depth] = hi
            out_ref[rows_all:, first : first + depth] = lo


def join_tiles(first_ref, second_ref, *rest):
    out_ref = rest[-1]
    rows = first_ref.shape[0]
    out_ref[:rows] = first_ref[...]
    out_ref[rows:] = second_ref[...]


def other_core(count, *refs):
    in_refs, out_refs, sems = refs[:count], refs[-1 - count : -1], refs[-1]
    copies = []
    for i, (in_ref, out_ref) in enumerate(zip(in_refs, out_refs)):
        copies.append(pltpu.make_async_copy(in_ref.at[1], out_ref, sems.at[i]))
        copies[i].start()
    for copy in copies:
        copy.wait()


def adjoint(n_pen, per_owner, core, table_ref, blocks, tile_refs, out_ref, made, out_sems):
    pen = lax.axis_index("pen")
    depth, columns = made.shape[3:]
    puts = []
    for i in range(n_pen // 2):
        first_column = pl.multiple_of((pen ^ distance(n_pen, 2 * i + core)) * columns, columns)
        here = tile_refs[i][...]
        step = lax.dot_general(
            table_ref[...],
            jnp.concatenate([here, here], axis=0),
            (((0,), (0,)), ((), ())),
            preferred_element_type=F32,
        )
        for r in range(per_owner):
            for c in range(2):
                first = (c * per_owner + r) * depth
                held = blocks[i][r, c].astype(F32)
                made[i, r, c] = (held + step[first : first + depth]).astype(BF16)
        to = out_ref.at[:, :, :, pl.ds(first_column, columns)]
        puts.append(pltpu.make_async_copy(made.at[i], to, out_sems.at[i]))
        puts[-1].start()
    return puts


def adjoint_like(n_pen, per_owner, table_ref, *rest):
    chips = n_pen // 2
    kept, tile_refs, (out_ref, made, out_sems) = rest[:chips], rest[chips:n_pen], rest[n_pen:]
    blocks = [one.at[0] for one in kept]
    for put in adjoint(n_pen, per_owner, 0, table_ref, blocks, tile_refs, out_ref, made, out_sems):
        put.wait()


def adjoint_other(n_pen, chunk, per_owner, table_ref, begun_ref, *rest):
    del begun_ref
    chips = n_pen // 2
    swapped, tile_refs, rest = rest[:chips], rest[chips : chips + n_pen], rest[chips + n_pen :]
    out_ref, residual_ref, made, out_sems = rest
    rows, columns = tile_refs[0].shape
    pen = lax.axis_index("pen")
    puts = adjoint(n_pen, per_owner, 1, table_ref, swapped, tile_refs[1::2], out_ref, made, out_sems)
    pick_row = lax.broadcasted_iota(I32, (16, rows), 0)
    pick_at = lax.broadcasted_iota(I32, (16, rows), 1)
    pick = jnp.where(pick_at == pick_row * chunk + pen, 1.0, 0.0)
    pick = jnp.where(pick_row < 2, pick, 0.0).astype(BF16)
    for q in range(n_pen):
        first_column = pl.multiple_of((pen ^ distance(n_pen, q)) * columns, columns)
        own = jnp.dot(pick, tile_refs[q][...], preferred_element_type=F32)
        residual_ref[0, :, pl.ds(first_column, columns)] = own[:2].astype(BF16)
    for put in puts:
        put.wait()


def body(spectrum, depth_weights, pair_tilt, pair_tile_within, tilt_pos, owner, measured):
    n_pen = lax.axis_size("pen")
    n_kz = lax.axis_size("kz")
    blocks, _, depth, columns = spectrum.shape
    per_owner = blocks // n_pen
    pairs = depth_weights.shape[1]
    tile_dev, _, cells = measured.shape
    chunk = tile_dev * n_pen
    tiles = chunk * n_kz
    tiles_per_tilt = tiles // tilt_pos.shape[0]

    chips = n_pen // 2

    def call(kernel, *static):
        def bound(*refs):
            return kernel(*static, *refs)
        return bound

    def across(value, k):
        return lax.ppermute(value, "kz", [(i, i ^ k) for i in range(n_kz)])

    def between(value, k):
        return lax.ppermute(value, "pen", [(i, i ^ k) for i in range(n_pen)])

    pair = (per_owner, 2, depth, columns)
    group = jax.ShapeDtypeStruct((n_kz // 2, 2 * chunk, columns), F32)
    *outs, inverse, sums, sent_sums = pl.pallas_call(
        call(order_and_forward, n_pen, n_kz, chunk, per_owner, tiles_per_tilt),
        out_shape=[jax.ShapeDtypeStruct((2, per_owner, 2, depth, columns), BF16)] * chips
        + [jax.ShapeDtypeStruct((blocks,), I32), group, group],
        in_specs=[ANY] * 6,
        out_specs=[ANY] * chips + [SMEM, ANY, ANY],
        scratch_shapes=[
            pltpu.VMEM(spectrum.shape, BF16),
            pltpu.SMEM((blocks,), I32),
            pltpu.SMEM(tilt_pos.shape, I32),
            pltpu.VMEM(pair_tilt.shape, I32),
            pltpu.VMEM(pair_tile_within.shape, I32),
            pltpu.VMEM(depth_weights.shape, BF16),
            pltpu.SMEM((n_pen,), I32),
            pltpu.VMEM((2 * tiles, blocks * depth), BF16),
            pltpu.VMEM(group.shape, F32),
            pltpu.VMEM(group.shape, F32),
            pltpu.SemaphoreType.DMA((5,)),
            pltpu.SemaphoreType.DMA((blocks,)),
            pltpu.SemaphoreType.DMA((n_pen, per_owner)),
            pltpu.SemaphoreType.DMA((2,)),
        ],
        compiler_params=pltpu.CompilerParams(vmem_limit_bytes=62 << 20),
    )(owner, tilt_pos, pair_tilt, pair_tile_within, depth_weights, spectrum)
    kept = [outs[0]] + [between(outs[i], distance(n_pen, 2 * i)) for i in range(1, chips)]

    arrived = across(sent_sums, 1)
    step = 2
    while step < n_kz:
        sums = (sums + arrived).reshape(-1, 2, 2 * chunk, columns)
        sums, arrived = sums[:, 0], across(sums[:, 1], step)
        step *= 2

    sent = measured.reshape(2, n_pen, columns).transpose(1, 0, 2)
    got = lax.all_to_all(sent, "pen", split_axis=0, concat_axis=0, tiled=True)
    measured_rows = got.transpose(1, 0, 2).reshape(2 * chunk, columns)
    own, table = pl.pallas_call(
        call(residual_and_table, n_kz, chunk, per_owner, tiles_per_tilt),
        out_shape=[
            jax.ShapeDtypeStruct((2 * chunk, columns), BF16),
            jax.ShapeDtypeStruct((4 * tiles, 2 * per_owner * depth), BF16),
        ],
        in_specs=[SMEM, SMEM] + [VMEM] * 6,
        out_specs=[VMEM, VMEM],
        scratch_shapes=[pltpu.VMEM((blocks, pairs), I32)],
        compiler_params=pltpu.CompilerParams(vmem_limit_bytes=8 << 20),
    )(
        inverse,
        tilt_pos,
        pair_tilt,
        pair_tile_within,
        depth_weights,
        sums.reshape(2 * chunk, columns),
        arrived.reshape(2 * chunk, columns),
        measured_rows,
    )

    held = own
    step = 1
    while 2 * step < n_kz:
        held = jnp.concatenate([held, across(held, step)], axis=0)
        step *= 2
    def take_other(arrived, after):
        return pl.pallas_call(
            call(other_core, len(arrived)),
            out_shape=[jax.ShapeDtypeStruct(pair, BF16)] * len(arrived),
            in_specs=[ANY] * (len(arrived) + len(after)),
            out_specs=[ANY] * len(arrived),
            scratch_shapes=[pltpu.SemaphoreType.DMA((len(arrived),))],
            compiler_params=pltpu.CompilerParams(vmem_limit_bytes=8 << 20),
        )(*arrived, *after)

    swapped = [between(one, 1) for one in [outs[0][1], *take_other(kept[1:2], [held])]]
    held = pl.pallas_call(
        join_tiles,
        out_shape=jax.ShapeDtypeStruct((2 * tiles, columns), BF16),
        in_specs=[VMEM, VMEM, ANY, ANY],
        out_specs=VMEM,
        compiler_params=pltpu.CompilerParams(vmem_limit_bytes=8 << 20),
    )(held, across(held, step), *swapped)
    like = [held] + [between(held, distance(n_pen, 2 * i)) for i in range(1, chips)]
    swapped = swapped + [between(one, 1) for one in take_other(kept[2:], like[1:])]
    every = [tile for one in like for tile in (one, between(one, 1))]

    scratch = [pltpu.VMEM((chips, *pair), BF16), pltpu.SemaphoreType.DMA((chips,))]
    begun = pl.pallas_call(
        call(adjoint_like, n_pen, per_owner),
        out_shape=jax.ShapeDtypeStruct((per_owner, 2, depth, cells), BF16),
        in_specs=[VMEM] * (n_pen + 1),
        out_specs=ANY,
        scratch_shapes=scratch,
        compiler_params=pltpu.CompilerParams(vmem_limit_bytes=16 << 20),
    )(table, *kept, *like)
    updated, residual = pl.pallas_call(
        call(adjoint_other, n_pen, chunk, per_owner),
        out_shape=[
            jax.ShapeDtypeStruct(begun.shape, BF16),
            jax.ShapeDtypeStruct((tile_dev, 2, cells), BF16),
        ],
        in_specs=[VMEM, ANY] + [VMEM] * (chips + n_pen),
        out_specs=[ANY, VMEM],
        scratch_shapes=scratch,
        input_output_aliases={1: 0},
        compiler_params=pltpu.CompilerParams(vmem_limit_bytes=16 << 20),
    )(table, begun, *swapped, *every)
    return (updated, residual)


def solution(mesh):
    return jax.shard_map(
        body,
        mesh=mesh,
        in_specs=(
            P("kz", None, None, "pen"),
            P("kz", None, None),
            P("kz", None),
            P("kz", None),
            P(),
            P("kz"),
            P(("kz", "pen"), None, None),
        ),
        out_specs=(P(("kz", "pen"), None, None, None), P(("kz", "pen"), None, None)),
        check_vma=False,
    )
```

```python
import jax
import jax.numpy as jnp
from jax import lax
from jax.experimental import pallas as pl
from jax.experimental.pallas import tpu as pltpu
from jax.sharding import PartitionSpec as P

BF16 = jnp.bfloat16
F32 = jnp.float32
I32 = jnp.int32
SMEM = pl.BlockSpec(memory_space=pltpu.SMEM)
VMEM = pl.BlockSpec(memory_space=pltpu.VMEM)
ANY = pl.BlockSpec(memory_space=pl.ANY)


def split_hi_lo(value):
    hi = value.astype(BF16)
    return hi, (value - hi.astype(F32)).astype(BF16)


def distance(n_pen, q):
    return (n_pen - q // 2 * 2) % n_pen + q % 2


def slots(tilt_pos_ref, tilt, within, tiles_per_tilt, flip):
    place = jnp.zeros_like(tilt)
    for t in range(tilt_pos_ref.shape[0]):
        place = jnp.where(tilt == t, tilt_pos_ref[t], place)
    return (place * tiles_per_tilt + within) ^ flip


def order_and_forward(n_pen, n_kz, chunk, per_owner, tiles_per_tilt, owner_ref, tilt_pos_ref, tilt_ref,
                      within_ref, weights_ref, spectrum_ref, *rest):
    chips = n_pen // 2
    outs, rest = rest[:chips], rest[chips:]
    inverse_ref, kept_ref, sent_ref, held, owner, tilt_pos, tilt, within, weights, rest = *rest[:9], rest[9:]
    count, table, kept, sent, small_sems, in_sems, out_sems, sum_sems = rest
    blocks, pairs, depth = weights_ref.shape
    columns = spectrum_ref.shape[3]
    tiles = n_kz * chunk
    pen = lax.axis_index("pen")
    small = []
    for i, (from_ref, to) in enumerate(
        ((owner_ref, owner), (tilt_pos_ref, tilt_pos), (tilt_ref, tilt), (within_ref, within), (weights_ref, weights))
    ):
        small.append(pltpu.make_async_copy(from_ref, to, small_sems.at[i]))
        small[i].start()
    gets, puts = [], []
    for b in range(blocks):
        gets.append(pltpu.make_async_copy(spectrum_ref.at[b], held.at[b], in_sems.at[b]))
        gets[b].start()
    for o in range(n_pen):
        count[o] = 0
    for copy in small:
        copy.wait()
    for b in range(blocks):
        o = owner[b]
        r = count[o]
        count[o] = r + 1
        inverse_ref[o * per_owner + r] = b
    slot = slots(tilt_pos, tilt[...], within[...], tiles_per_tilt, lax.axis_index("kz") * chunk)
    rows = lax.broadcasted_iota(I32, (tiles, pairs), 0)
    for b in range(blocks):
        hot = jnp.where(slot[b : b + 1, :] == rows, 1.0, 0.0).astype(BF16)
        hi, lo = split_hi_lo(jnp.dot(hot, weights[b], preferred_element_type=F32))
        table[:tiles, b * depth : (b + 1) * depth] = hi
        table[tiles:, b * depth : (b + 1) * depth] = lo
    for get in gets:
        get.wait()
    for q in range(n_pen):
        for r in range(per_owner):
            from_ref = held.at[inverse_ref[(pen ^ distance(n_pen, q)) * per_owner + r]]
            puts.append(pltpu.make_async_copy(from_ref, outs[q // 2].at[q % 2, r], out_sems.at[q, r]))
            puts[-1].start()
    for c in range(2):
        both = jnp.dot(
            table[...],
            held[:, c].reshape(blocks * depth, columns),
            preferred_element_type=F32,
        )
        total = both[:tiles] + both[tiles:]
        for k in range(n_kz):
            to = sent if k % 2 else kept
            to[k // 2, c * chunk : (c + 1) * chunk, :] = total[k * chunk : (k + 1) * chunk]
    puts.append(pltpu.make_async_copy(kept, kept_ref, sum_sems.at[0]))
    puts[-1].start()
    puts.append(pltpu.make_async_copy(sent, sent_ref, sum_sems.at[1]))
    puts[-1].start()
    for put in puts:
        put.wait()


def residual_and_table(n_kz, chunk, per_owner, tiles_per_tilt, inverse_ref, tilt_pos_ref, tilt_ref, within_ref,
                       weights_ref, sums_ref, arrived_ref, measured_ref, own_ref, out_ref, slot_ref):
    own_ref[...] = (sums_ref[...] + arrived_ref[...] - measured_ref[...].astype(F32)).astype(BF16)
    pairs, depth = weights_ref.shape[1:]
    rows_all = n_kz * 2 * chunk
    flip = lax.axis_index("kz") * chunk
    slot_ref[...] = slots(tilt_pos_ref, tilt_ref[...], within_ref[...], tiles_per_tilt, flip)
    rows = lax.broadcasted_iota(I32, (rows_all, pairs), 0)
    for r in range(per_owner):
        b = inverse_ref[lax.axis_index("pen") * per_owner + r]
        at = slot_ref[pl.ds(b, 1), :]
        low = at & (chunk - 1)
        for c in range(2):
            place = (at - low) * 2 + c * chunk + low
            hot = jnp.where(place == rows, -8.0, 0.0).astype(BF16)
            hi, lo = split_hi_lo(jnp.dot(hot, weights_ref[b], preferred_element_type=F32))
            first = (c * per_owner + r) * depth
            out_ref[:rows_all, first : first + depth] = hi
            out_ref[rows_all:, first : first + depth] = lo


def join_tiles(first_ref, second_ref, *rest):
    out_ref = rest[-1]
    rows = first_ref.shape[0]
    out_ref[:rows] = first_ref[...]
    out_ref[rows:] = second_ref[...]


def other_core(count, *refs):
    in_refs, (out_ref, sems) = refs[:count], refs[-2:]
    copies = []
    for i, in_ref in enumerate(in_refs):
        copies.append(pltpu.make_async_copy(in_ref.at[1], out_ref.at[i], sems.at[i]))
        copies[i].start()
    for copy in copies:
        copy.wait()


def stack_tiles(*refs):
    in_refs, out_ref = refs[:-1], refs[-1]
    for i, in_ref in enumerate(in_refs):
        out_ref[i] = in_ref[...]


def adjoint(n_pen, chunk, per_owner, core, table_ref, blocks, tiles, out_ref, residual_ref, made, out_sems):
    pen = lax.axis_index("pen")
    depth, columns = made.shape[3:]
    rows = tiles[0].shape[0]
    pick_row = lax.broadcasted_iota(I32, (16, rows), 0)
    pick_at = lax.broadcasted_iota(I32, (16, rows), 1)
    pick = jnp.where(pick_at == pick_row * chunk + pen, 1.0, 0.0)
    pick = jnp.where(pick_row < 2, pick, 0.0).astype(BF16)
    puts = []
    for i in range(n_pen // 2):
        first_column = pl.multiple_of((pen ^ distance(n_pen, 2 * i + core)) * columns, columns)
        here = tiles[i][...]
        step = lax.dot_general(
            table_ref[...],
            jnp.concatenate([here, here], axis=0),
            (((0,), (0,)), ((), ())),
            preferred_element_type=F32,
        )
        for r in range(per_owner):
            for c in range(2):
                first = (c * per_owner + r) * depth
                held = blocks[i][r, c].astype(F32)
                made[i, r, c] = (held + step[first : first + depth]).astype(BF16)
        to = out_ref.at[:, :, :, pl.ds(first_column, columns)]
        puts.append(pltpu.make_async_copy(made.at[i], to, out_sems.at[i]))
        puts[-1].start()
        own = jnp.dot(pick, here, preferred_element_type=F32)
        residual_ref[0, :, pl.ds(first_column, columns)] = own[:2].astype(BF16)
    for put in puts:
        put.wait()


def adjoint_like(n_pen, chunk, per_owner, table_ref, *rest):
    chips = n_pen // 2
    kept, tiles, (out_ref, residual_ref, made, out_sems) = rest[:chips], rest[chips:n_pen], rest[n_pen:]
    residual_ref[...] = jnp.zeros_like(residual_ref)
    blocks = [one.at[0] for one in kept]
    adjoint(n_pen, chunk, per_owner, 0, table_ref, blocks, tiles, out_ref, residual_ref, made, out_sems)


def adjoint_other(n_pen, chunk, per_owner, table_ref, begun_ref, part_ref, own_ref, far_ref, near_ref, tiles_ref,
                  out_ref, residual_ref, made, out_sems):
    del begun_ref
    chips = n_pen // 2
    residual_ref[...] = part_ref[...]
    blocks = [own_ref, far_ref] + [near_ref.at[i] for i in range(chips - 2)]
    tiles = [tiles_ref.at[i] for i in range(chips)]
    adjoint(n_pen, chunk, per_owner, 1, table_ref, blocks, tiles, out_ref, residual_ref, made, out_sems)


def body(spectrum, depth_weights, pair_tilt, pair_tile_within, tilt_pos, owner, measured):
    n_pen = lax.axis_size("pen")
    n_kz = lax.axis_size("kz")
    blocks, _, depth, columns = spectrum.shape
    per_owner = blocks // n_pen
    pairs = depth_weights.shape[1]
    tile_dev, _, cells = measured.shape
    chunk = tile_dev * n_pen
    tiles = chunk * n_kz
    tiles_per_tilt = tiles // tilt_pos.shape[0]

    chips = n_pen // 2

    def call(kernel, *static):
        def bound(*refs):
            return kernel(*static, *refs)
        return bound

    def across(value, k):
        return lax.ppermute(value, "kz", [(i, i ^ k) for i in range(n_kz)])

    def between(value, k):
        return lax.ppermute(value, "pen", [(i, i ^ k) for i in range(n_pen)])

    pair = (per_owner, 2, depth, columns)
    group = jax.ShapeDtypeStruct((n_kz // 2, 2 * chunk, columns), F32)
    *outs, inverse, sums, sent_sums = pl.pallas_call(
        call(order_and_forward, n_pen, n_kz, chunk, per_owner, tiles_per_tilt),
        out_shape=[jax.ShapeDtypeStruct((2, per_owner, 2, depth, columns), BF16)] * chips
        + [jax.ShapeDtypeStruct((blocks,), I32), group, group],
        in_specs=[ANY] * 6,
        out_specs=[ANY] * chips + [SMEM, ANY, ANY],
        scratch_shapes=[
            pltpu.VMEM(spectrum.shape, BF16),
            pltpu.SMEM((blocks,), I32),
            pltpu.SMEM(tilt_pos.shape, I32),
            pltpu.VMEM(pair_tilt.shape, I32),
            pltpu.VMEM(pair_tile_within.shape, I32),
            pltpu.VMEM(depth_weights.shape, BF16),
            pltpu.SMEM((n_pen,), I32),
            pltpu.VMEM((2 * tiles, blocks * depth), BF16),
            pltpu.VMEM(group.shape, F32),
            pltpu.VMEM(group.shape, F32),
            pltpu.SemaphoreType.DMA((5,)),
            pltpu.SemaphoreType.DMA((blocks,)),
            pltpu.SemaphoreType.DMA((n_pen, per_owner)),
            pltpu.SemaphoreType.DMA((2,)),
        ],
        compiler_params=pltpu.CompilerParams(vmem_limit_bytes=62 << 20),
    )(owner, tilt_pos, pair_tilt, pair_tile_within, depth_weights, spectrum)
    kept = [outs[0]] + [between(outs[i], distance(n_pen, 2 * i)) for i in range(1, chips)]

    arrived = across(sent_sums, 1)
    step = 2
    while step < n_kz:
        sums = (sums + arrived).reshape(-1, 2, 2 * chunk, columns)
        sums, arrived = sums[:, 0], across(sums[:, 1], step)
        step *= 2

    sent = measured.reshape(2, n_pen, columns).transpose(1, 0, 2)
    got = lax.all_to_all(sent, "pen", split_axis=0, concat_axis=0, tiled=True)
    measured_rows = got.transpose(1, 0, 2).reshape(2 * chunk, columns)
    own, table = pl.pallas_call(
        call(residual_and_table, n_kz, chunk, per_owner, tiles_per_tilt),
        out_shape=[
            jax.ShapeDtypeStruct((2 * chunk, columns), BF16),
            jax.ShapeDtypeStruct((4 * tiles, 2 * per_owner * depth), BF16),
        ],
        in_specs=[SMEM, SMEM] + [VMEM] * 6,
        out_specs=[VMEM, VMEM],
        scratch_shapes=[pltpu.VMEM((blocks, pairs), I32)],
        compiler_params=pltpu.CompilerParams(vmem_limit_bytes=8 << 20),
    )(
        inverse,
        tilt_pos,
        pair_tilt,
        pair_tile_within,
        depth_weights,
        sums.reshape(2 * chunk, columns),
        arrived.reshape(2 * chunk, columns),
        measured_rows,
    )

    held = own
    step = 1
    while 2 * step < n_kz:
        held = jnp.concatenate([held, across(held, step)], axis=0)
        step *= 2
    def take_other(arrived, after):
        return pl.pallas_call(
            call(other_core, len(arrived)),
            out_shape=jax.ShapeDtypeStruct((len(arrived), *pair), BF16),
            in_specs=[ANY] * (len(arrived) + len(after)),
            out_specs=ANY,
            scratch_shapes=[pltpu.SemaphoreType.DMA((len(arrived),))],
            compiler_params=pltpu.CompilerParams(vmem_limit_bytes=8 << 20),
        )(*arrived, *after)

    own_swapped = between(outs[0][1], 1)
    far_swapped = between(take_other(kept[1:2], [held]), 1).reshape(pair)
    held = pl.pallas_call(
        join_tiles,
        out_shape=jax.ShapeDtypeStruct((2 * tiles, columns), BF16),
        in_specs=[VMEM, VMEM, ANY, ANY],
        out_specs=VMEM,
        compiler_params=pltpu.CompilerParams(vmem_limit_bytes=8 << 20),
    )(held, across(held, step), own_swapped, far_swapped)
    like = [held] + [between(held, distance(n_pen, 2 * i)) for i in range(1, chips)]
    near_swapped = between(take_other(kept[2:], like[1:]), 1)
    stacked = pl.pallas_call(
        stack_tiles,
        out_shape=jax.ShapeDtypeStruct((chips, 2 * tiles, columns), BF16),
        in_specs=[VMEM] * chips,
        out_specs=VMEM,
        compiler_params=pltpu.CompilerParams(vmem_limit_bytes=8 << 20),
    )(*like)
    other = between(stacked, 1)

    scratch = [pltpu.VMEM((chips, *pair), BF16), pltpu.SemaphoreType.DMA((chips,))]
    shapes = [
        jax.ShapeDtypeStruct((per_owner, 2, depth, cells), BF16),
        jax.ShapeDtypeStruct((tile_dev, 2, cells), BF16),
    ]
    begun, part = pl.pallas_call(
        call(adjoint_like, n_pen, chunk, per_owner),
        out_shape=shapes,
        in_specs=[VMEM] * (n_pen + 1),
        out_specs=[ANY, VMEM],
        scratch_shapes=scratch,
        compiler_params=pltpu.CompilerParams(vmem_limit_bytes=16 << 20),
    )(table, *kept, *like)
    updated, residual = pl.pallas_call(
        call(adjoint_other, n_pen, chunk, per_owner),
        out_shape=shapes,
        in_specs=[VMEM, ANY] + [VMEM] * 5,
        out_specs=[ANY, VMEM],
        scratch_shapes=scratch,
        input_output_aliases={1: 0},
        compiler_params=pltpu.CompilerParams(vmem_limit_bytes=16 << 20),
    )(table, begun, part, own_swapped, far_swapped, near_swapped, other)
    return (updated, residual)


def solution(mesh):
    return jax.shard_map(
        body,
        mesh=mesh,
        in_specs=(
            P("kz", None, None, "pen"),
            P("kz", None, None),
            P("kz", None),
            P("kz", None),
            P(),
            P("kz"),
            P(("kz", "pen"), None, None),
        ),
        out_specs=(P(("kz", "pen"), None, None, None), P(("kz", "pen"), None, None)),
        check_vma=False,
    )
```

```python
import jax
import jax.numpy as jnp
from jax import lax
from jax.experimental import pallas as pl
from jax.experimental.pallas import tpu as pltpu
from jax.sharding import PartitionSpec as P

BF16 = jnp.bfloat16
F32 = jnp.float32
I32 = jnp.int32
SMEM = pl.BlockSpec(memory_space=pltpu.SMEM)
VMEM = pl.BlockSpec(memory_space=pltpu.VMEM)
ANY = pl.BlockSpec(memory_space=pl.ANY)


def split_hi_lo(value):
    hi = value.astype(BF16)
    return hi, (value - hi.astype(F32)).astype(BF16)


def slots(tilt_pos_ref, tilt, within, tiles_per_tilt, flip):
    place = jnp.zeros_like(tilt)
    for t in range(tilt_pos_ref.shape[0]):
        place = jnp.where(tilt == t, tilt_pos_ref[t], place)
    return (place * tiles_per_tilt + within) ^ flip


def order_and_forward(n_pen, n_kz, chunk, per_owner, tiles_per_tilt, owner_ref, tilt_pos_ref, tilt_ref,
                      within_ref, weights_ref, spectrum_ref, *rest):
    chips = n_pen // 2
    outs, rest = rest[:chips], rest[chips:]
    inverse_ref, kept_ref, sent_ref, held, owner, tilt_pos, tilt, within, weights, rest = *rest[:9], rest[9:]
    count, table, kept, sent, small_sems, in_sems, out_sems, sum_sems = rest
    blocks, pairs, depth = weights_ref.shape
    columns = spectrum_ref.shape[3]
    tiles = n_kz * chunk
    pen = lax.axis_index("pen")
    small = []
    for i, (from_ref, to) in enumerate(
        ((owner_ref, owner), (tilt_pos_ref, tilt_pos), (tilt_ref, tilt), (within_ref, within), (weights_ref, weights))
    ):
        small.append(pltpu.make_async_copy(from_ref, to, small_sems.at[i]))
        small[i].start()
    gets, puts = [], []
    for b in range(blocks):
        gets.append(pltpu.make_async_copy(spectrum_ref.at[b], held.at[b], in_sems.at[b]))
        gets[b].start()
    for o in range(n_pen):
        count[o] = 0
    for copy in small:
        copy.wait()
    for b in range(blocks):
        o = owner[b]
        r = count[o]
        count[o] = r + 1
        inverse_ref[o * per_owner + r] = b
    slot = slots(tilt_pos, tilt[...], within[...], tiles_per_tilt, lax.axis_index("kz") * chunk)
    rows = lax.broadcasted_iota(I32, (tiles, pairs), 0)
    for b in range(blocks):
        hot = jnp.where(slot[b : b + 1, :] == rows, 1.0, 0.0).astype(BF16)
        hi, lo = split_hi_lo(jnp.dot(hot, weights[b], preferred_element_type=F32))
        table[:tiles, b * depth : (b + 1) * depth] = hi
        table[tiles:, b * depth : (b + 1) * depth] = lo
    for get in gets:
        get.wait()
    for q in range(n_pen):
        for r in range(per_owner):
            from_ref = held.at[inverse_ref[(pen ^ q) * per_owner + r]]
            puts.append(pltpu.make_async_copy(from_ref, outs[q // 2].at[q % 2, r], out_sems.at[q, r]))
            puts[-1].start()
    for c in range(2):
        both = jnp.dot(
            table[...],
            held[:, c].reshape(blocks * depth, columns),
            preferred_element_type=F32,
        )
        total = both[:tiles] + both[tiles:]
        for k in range(n_kz):
            to = sent if k % 2 else kept
            to[k // 2, c * chunk : (c + 1) * chunk, :] = total[k * chunk : (k + 1) * chunk]
    puts.append(pltpu.make_async_copy(kept, kept_ref, sum_sems.at[0]))
    puts[-1].start()
    puts.append(pltpu.make_async_copy(sent, sent_ref, sum_sems.at[1]))
    puts[-1].start()
    for put in puts:
        put.wait()


def residual_and_table(n_kz, chunk, per_owner, tiles_per_tilt, inverse_ref, tilt_pos_ref, tilt_ref, within_ref,
                       weights_ref, sums_ref, arrived_ref, measured_ref, own_ref, out_ref, slot_ref):
    own_ref[...] = (sums_ref[...] + arrived_ref[...] - measured_ref[...].astype(F32)).astype(BF16)
    pairs, depth = weights_ref.shape[1:]
    rows_all = n_kz * 2 * chunk
    flip = lax.axis_index("kz") * chunk
    slot_ref[...] = slots(tilt_pos_ref, tilt_ref[...], within_ref[...], tiles_per_tilt, flip)
    rows = lax.broadcasted_iota(I32, (rows_all, pairs), 0)
    for r in range(per_owner):
        b = inverse_ref[lax.axis_index("pen") * per_owner + r]
        at = slot_ref[pl.ds(b, 1), :]
        low = at & (chunk - 1)
        for c in range(2):
            place = (at - low) * 2 + c * chunk + low
            hot = jnp.where(place == rows, -8.0, 0.0).astype(BF16)
            hi, lo = split_hi_lo(jnp.dot(hot, weights_ref[b], preferred_element_type=F32))
            first = (c * per_owner + r) * depth
            out_ref[:rows_all, first : first + depth] = hi
            out_ref[rows_all:, first : first + depth] = lo


def join_tiles(first_ref, second_ref, *rest):
    out_ref = rest[-1]
    rows = first_ref.shape[0]
    out_ref[:rows] = first_ref[...]
    out_ref[rows:] = second_ref[...]


def other_core(count, *refs):
    in_refs, (out_ref, sems) = refs[:count], refs[-2:]
    copies = []
    for i, in_ref in enumerate(in_refs):
        copies.append(pltpu.make_async_copy(in_ref.at[1], out_ref.at[i], sems.at[i]))
        copies[i].start()
    for copy in copies:
        copy.wait()


def stack_tiles(*refs):
    in_refs, out_ref = refs[:-1], refs[-1]
    for i, in_ref in enumerate(in_refs):
        out_ref[i] = in_ref[...]


def adjoint(n_pen, chunk, per_owner, core, table_ref, blocks, tiles, out_ref, residual_ref, made, out_sems):
    pen = lax.axis_index("pen")
    depth, columns = made.shape[3:]
    rows = tiles[0].shape[0]
    pick_row = lax.broadcasted_iota(I32, (16, rows), 0)
    pick_at = lax.broadcasted_iota(I32, (16, rows), 1)
    pick = jnp.where(pick_at == pick_row * chunk + pen, 1.0, 0.0)
    pick = jnp.where(pick_row < 2, pick, 0.0).astype(BF16)
    puts = []
    for i in range(n_pen // 2):
        first_column = pl.multiple_of((pen ^ (2 * i + core)) * columns, columns)
        here = tiles[i][...]
        step = lax.dot_general(
            table_ref[...],
            jnp.concatenate([here, here], axis=0),
            (((0,), (0,)), ((), ())),
            preferred_element_type=F32,
        )
        for r in range(per_owner):
            for c in range(2):
                first = (c * per_owner + r) * depth
                held = blocks[i][r, c].astype(F32)
                made[i, r, c] = (held + step[first : first + depth]).astype(BF16)
        to = out_ref.at[:, :, :, pl.ds(first_column, columns)]
        puts.append(pltpu.make_async_copy(made.at[i], to, out_sems.at[i]))
        puts[-1].start()
        own = jnp.dot(pick, here, preferred_element_type=F32)
        residual_ref[0, :, pl.ds(first_column, columns)] = own[:2].astype(BF16)
    return puts


def adjoint_like(n_pen, chunk, per_owner, table_ref, *rest):
    chips = n_pen // 2
    kept, tiles, (out_ref, residual_ref, made, out_sems) = rest[:chips], rest[chips:n_pen], rest[n_pen:]
    residual_ref[...] = jnp.zeros_like(residual_ref)
    blocks = [one.at[0] for one in kept]
    for put in adjoint(n_pen, chunk, per_owner, 0, table_ref, blocks, tiles, out_ref, residual_ref, made, out_sems):
        put.wait()


def adjoint_other(n_pen, chunk, per_owner, table_ref, begun_ref, part_ref, own_ref, near_ref, far_ref, tiles_ref,
                  out_ref, residual_ref, made, out_sems, whole, whole_sem):
    del begun_ref
    chips = n_pen // 2
    whole[...] = part_ref[...]
    blocks = [own_ref, near_ref.at[0]] + [far_ref.at[i] for i in range(chips - 2)]
    tiles = [tiles_ref.at[i] for i in range(chips)]
    puts = adjoint(n_pen, chunk, per_owner, 1, table_ref, blocks, tiles, out_ref, whole, made, out_sems)
    puts.append(pltpu.make_async_copy(whole, residual_ref, whole_sem))
    puts[-1].start()
    for put in puts:
        put.wait()


def body(spectrum, depth_weights, pair_tilt, pair_tile_within, tilt_pos, owner, measured):
    n_pen = lax.axis_size("pen")
    n_kz = lax.axis_size("kz")
    blocks, _, depth, columns = spectrum.shape
    per_owner = blocks // n_pen
    pairs = depth_weights.shape[1]
    tile_dev, _, cells = measured.shape
    chunk = tile_dev * n_pen
    tiles = chunk * n_kz
    tiles_per_tilt = tiles // tilt_pos.shape[0]

    chips = n_pen // 2

    def call(kernel, *static):
        def bound(*refs):
            return kernel(*static, *refs)
        return bound

    def across(value, k):
        return lax.ppermute(value, "kz", [(i, i ^ k) for i in range(n_kz)])

    def between(value, k):
        return lax.ppermute(value, "pen", [(i, i ^ k) for i in range(n_pen)])

    pair = (per_owner, 2, depth, columns)
    group = jax.ShapeDtypeStruct((n_kz // 2, 2 * chunk, columns), F32)
    *outs, inverse, sums, sent_sums = pl.pallas_call(
        call(order_and_forward, n_pen, n_kz, chunk, per_owner, tiles_per_tilt),
        out_shape=[jax.ShapeDtypeStruct((2, per_owner, 2, depth, columns), BF16)] * chips
        + [jax.ShapeDtypeStruct((blocks,), I32), group, group],
        in_specs=[ANY] * 6,
        out_specs=[ANY] * chips + [SMEM, ANY, ANY],
        scratch_shapes=[
            pltpu.VMEM(spectrum.shape, BF16),
            pltpu.SMEM((blocks,), I32),
            pltpu.SMEM(tilt_pos.shape, I32),
            pltpu.VMEM(pair_tilt.shape, I32),
            pltpu.VMEM(pair_tile_within.shape, I32),
            pltpu.VMEM(depth_weights.shape, BF16),
            pltpu.SMEM((n_pen,), I32),
            pltpu.VMEM((2 * tiles, blocks * depth), BF16),
            pltpu.VMEM(group.shape, F32),
            pltpu.VMEM(group.shape, F32),
            pltpu.SemaphoreType.DMA((5,)),
            pltpu.SemaphoreType.DMA((blocks,)),
            pltpu.SemaphoreType.DMA((n_pen, per_owner)),
            pltpu.SemaphoreType.DMA((2,)),
        ],
        compiler_params=pltpu.CompilerParams(vmem_limit_bytes=62 << 20),
    )(owner, tilt_pos, pair_tilt, pair_tile_within, depth_weights, spectrum)
    kept = [outs[0]] + [between(outs[i], 2 * i) for i in range(1, chips)]

    arrived = across(sent_sums, 1)
    step = 2
    while step < n_kz:
        sums = (sums + arrived).reshape(-1, 2, 2 * chunk, columns)
        sums, arrived = sums[:, 0], across(sums[:, 1], step)
        step *= 2

    sent = measured.reshape(2, n_pen, columns).transpose(1, 0, 2)
    got = lax.all_to_all(sent, "pen", split_axis=0, concat_axis=0, tiled=True)
    measured_rows = got.transpose(1, 0, 2).reshape(2 * chunk, columns)
    own, table = pl.pallas_call(
        call(residual_and_table, n_kz, chunk, per_owner, tiles_per_tilt),
        out_shape=[
            jax.ShapeDtypeStruct((2 * chunk, columns), BF16),
            jax.ShapeDtypeStruct((4 * tiles, 2 * per_owner * depth), BF16),
        ],
        in_specs=[SMEM, SMEM] + [VMEM] * 6,
        out_specs=[VMEM, VMEM],
        scratch_shapes=[pltpu.VMEM((blocks, pairs), I32)],
        compiler_params=pltpu.CompilerParams(vmem_limit_bytes=8 << 20),
    )(
        inverse,
        tilt_pos,
        pair_tilt,
        pair_tile_within,
        depth_weights,
        sums.reshape(2 * chunk, columns),
        arrived.reshape(2 * chunk, columns),
        measured_rows,
    )

    held = own
    step = 1
    while 2 * step < n_kz:
        held = jnp.concatenate([held, across(held, step)], axis=0)
        step *= 2
    def take_other(arrived, after):
        return pl.pallas_call(
            call(other_core, len(arrived)),
            out_shape=jax.ShapeDtypeStruct((len(arrived), *pair), BF16),
            in_specs=[ANY] * (len(arrived) + len(after)),
            out_specs=ANY,
            scratch_shapes=[pltpu.SemaphoreType.DMA((len(arrived),))],
            compiler_params=pltpu.CompilerParams(vmem_limit_bytes=8 << 20),
        )(*arrived, *after)

    own_swapped = between(outs[0][1], 1)
    near_swapped = between(take_other(kept[1:2], [held]), 1)
    held = pl.pallas_call(
        join_tiles,
        out_shape=jax.ShapeDtypeStruct((2 * tiles, columns), BF16),
        in_specs=[VMEM, VMEM, ANY, ANY],
        out_specs=VMEM,
        compiler_params=pltpu.CompilerParams(vmem_limit_bytes=8 << 20),
    )(held, across(held, step), own_swapped, near_swapped)
    like = [held] + [between(held, 2 * i) for i in range(1, chips)]
    far_swapped = between(take_other(kept[2:], like[1:]), 1)
    stacked = pl.pallas_call(
        stack_tiles,
        out_shape=jax.ShapeDtypeStruct((chips, 2 * tiles, columns), BF16),
        in_specs=[VMEM] * chips,
        out_specs=VMEM,
        compiler_params=pltpu.CompilerParams(vmem_limit_bytes=8 << 20),
    )(*like)
    other = between(stacked, 1)

    scratch = [pltpu.VMEM((chips, *pair), BF16), pltpu.SemaphoreType.DMA((chips,))]
    shapes = [
        jax.ShapeDtypeStruct((per_owner, 2, depth, cells), BF16),
        jax.ShapeDtypeStruct((tile_dev, 2, cells), BF16),
    ]
    begun, part = pl.pallas_call(
        call(adjoint_like, n_pen, chunk, per_owner),
        out_shape=shapes,
        in_specs=[VMEM] * (n_pen + 1),
        out_specs=[ANY, VMEM],
        scratch_shapes=scratch,
        compiler_params=pltpu.CompilerParams(vmem_limit_bytes=16 << 20),
    )(table, *kept, *like)
    updated, residual = pl.pallas_call(
        call(adjoint_other, n_pen, chunk, per_owner),
        out_shape=shapes,
        in_specs=[VMEM, ANY] + [VMEM] * 5,
        out_specs=[ANY, ANY],
        scratch_shapes=[*scratch, pltpu.VMEM(measured.shape, BF16), pltpu.SemaphoreType.DMA],
        input_output_aliases={1: 0},
        compiler_params=pltpu.CompilerParams(vmem_limit_bytes=16 << 20),
    )(table, begun, part, own_swapped, near_swapped, far_swapped, other)
    return (updated, residual)


def solution(mesh):
    return jax.shard_map(
        body,
        mesh=mesh,
        in_specs=(
            P("kz", None, None, "pen"),
            P("kz", None, None),
            P("kz", None),
            P("kz", None),
            P(),
            P("kz"),
            P(("kz", "pen"), None, None),
        ),
        out_specs=(P(("kz", "pen"), None, None, None), P(("kz", "pen"), None, None)),
        check_vma=False,
    )
```

```python
import jax
import jax.numpy as jnp
from jax import lax
from jax.experimental import pallas as pl
from jax.experimental.pallas import tpu as pltpu
from jax.sharding import PartitionSpec as P

BF16 = jnp.bfloat16
F32 = jnp.float32
I32 = jnp.int32
SMEM = pl.BlockSpec(memory_space=pltpu.SMEM)
VMEM = pl.BlockSpec(memory_space=pltpu.VMEM)
ANY = pl.BlockSpec(memory_space=pl.ANY)


def split_hi_lo(value):
    hi = value.astype(BF16)
    return hi, (value - hi.astype(F32)).astype(BF16)


def slots(tilt_pos_ref, tilt, within, tiles_per_tilt, flip):
    place = jnp.zeros_like(tilt)
    for t in range(tilt_pos_ref.shape[0]):
        place = jnp.where(tilt == t, tilt_pos_ref[t], place)
    return (place * tiles_per_tilt + within) ^ flip


def order_and_forward(n_pen, n_kz, chunk, per_owner, tiles_per_tilt, owner_ref, tilt_pos_ref, tilt_ref,
                      within_ref, weights_ref, spectrum_ref, *rest):
    chips = n_pen // 2
    outs, rest = rest[:chips], rest[chips:]
    inverse_ref, kept_ref, sent_ref, held, owner, tilt_pos, tilt, within, weights, rest = *rest[:9], rest[9:]
    count, table, kept, sent, small_sems, in_sems, out_sems, sum_sems = rest
    blocks, pairs, depth = weights_ref.shape
    columns = spectrum_ref.shape[3]
    tiles = n_kz * chunk
    pen = lax.axis_index("pen")
    small = []
    for i, (from_ref, to) in enumerate(
        ((owner_ref, owner), (tilt_pos_ref, tilt_pos), (tilt_ref, tilt), (within_ref, within), (weights_ref, weights))
    ):
        small.append(pltpu.make_async_copy(from_ref, to, small_sems.at[i]))
        small[i].start()
    gets, puts = [], []
    for b in range(blocks):
        gets.append(pltpu.make_async_copy(spectrum_ref.at[b], held.at[b], in_sems.at[b]))
        gets[b].start()
    for o in range(n_pen):
        count[o] = 0
    for copy in small:
        copy.wait()
    for b in range(blocks):
        o = owner[b]
        r = count[o]
        count[o] = r + 1
        inverse_ref[o * per_owner + r] = b
    slot = slots(tilt_pos, tilt[...], within[...], tiles_per_tilt, lax.axis_index("kz") * chunk)
    rows = lax.broadcasted_iota(I32, (tiles, pairs), 0)
    for b in range(blocks):
        hot = jnp.where(slot[b : b + 1, :] == rows, 1.0, 0.0).astype(BF16)
        hi, lo = split_hi_lo(jnp.dot(hot, weights[b], preferred_element_type=F32))
        table[:tiles, b * depth : (b + 1) * depth] = hi
        table[tiles:, b * depth : (b + 1) * depth] = lo
    for q in range(n_pen):
        for r in range(per_owner):
            b = inverse_ref[(pen ^ q) * per_owner + r]
            from_ref = held.at[b]
            pltpu.make_async_copy(spectrum_ref.at[b], from_ref, in_sems.at[b]).wait()
            puts.append(pltpu.make_async_copy(from_ref, outs[q // 2].at[q % 2, r], out_sems.at[q, r]))
            puts[-1].start()
    for c in range(2):
        both = jnp.dot(
            table[...],
            held[:, c].reshape(blocks * depth, columns),
            preferred_element_type=F32,
        )
        total = both[:tiles] + both[tiles:]
        for k in range(n_kz):
            to = sent if k % 2 else kept
            to[k // 2, c * chunk : (c + 1) * chunk, :] = total[k * chunk : (k + 1) * chunk]
    puts.append(pltpu.make_async_copy(kept, kept_ref, sum_sems.at[0]))
    puts[-1].start()
    puts.append(pltpu.make_async_copy(sent, sent_ref, sum_sems.at[1]))
    puts[-1].start()
    for put in puts:
        put.wait()


def residual_and_table(n_kz, chunk, per_owner, tiles_per_tilt, inverse_ref, tilt_pos_ref, tilt_ref, within_ref,
                       weights_ref, sums_ref, arrived_ref, got_ref, swapped_ref, own_ref, out_ref, slot_ref, measured):
    core = lax.axis_index("pen") & 1
    for i in range(got_ref.shape[0]):
        mine, theirs = got_ref[i, core].astype(F32), swapped_ref[i, core].astype(F32)
        first, second = jnp.where(core == 0, mine, theirs), jnp.where(core == 0, theirs, mine)
        for c in range(2):
            row = c * chunk + 2 * i
            measured[row : row + 1, :] = first[c : c + 1]
            measured[row + 1 : row + 2, :] = second[c : c + 1]
    own_ref[...] = (sums_ref[...] + arrived_ref[...] - measured[...]).astype(BF16)
    pairs, depth = weights_ref.shape[1:]
    rows_all = n_kz * 2 * chunk
    flip = lax.axis_index("kz") * chunk
    slot_ref[...] = slots(tilt_pos_ref, tilt_ref[...], within_ref[...], tiles_per_tilt, flip)
    rows = lax.broadcasted_iota(I32, (rows_all, pairs), 0)
    for r in range(per_owner):
        b = inverse_ref[lax.axis_index("pen") * per_owner + r]
        at = slot_ref[pl.ds(b, 1), :]
        low = at & (chunk - 1)
        for c in range(2):
            place = (at - low) * 2 + c * chunk + low
            hot = jnp.where(place == rows, -8.0, 0.0).astype(BF16)
            hi, lo = split_hi_lo(jnp.dot(hot, weights_ref[b], preferred_element_type=F32))
            first = (c * per_owner + r) * depth
            out_ref[:rows_all, first : first + depth] = hi
            out_ref[rows_all:, first : first + depth] = lo


def join_tiles(first_ref, second_ref, *rest):
    out_ref = rest[-1]
    rows = first_ref.shape[0]
    out_ref[:rows] = first_ref[...]
    out_ref[rows:] = second_ref[...]


def other_core(count, *refs):
    in_refs, (out_ref, sems) = refs[:count], refs[-2:]
    copies = []
    for i, in_ref in enumerate(in_refs):
        copies.append(pltpu.make_async_copy(in_ref.at[1], out_ref.at[i], sems.at[i]))
        copies[i].start()
    for copy in copies:
        copy.wait()


def stack_tiles(*refs):
    in_refs, out_ref = refs[:-1], refs[-1]
    for i, in_ref in enumerate(in_refs):
        out_ref[i] = in_ref[...]


def adjoint(n_pen, chunk, per_owner, core, table_ref, blocks, tiles, out_ref, residual_ref, made, out_sems):
    pen = lax.axis_index("pen")
    depth, columns = made.shape[3:]
    rows = tiles[0].shape[0]
    pick_row = lax.broadcasted_iota(I32, (16, rows), 0)
    pick_at = lax.broadcasted_iota(I32, (16, rows), 1)
    pick = jnp.where(pick_at == pick_row * chunk + pen, 1.0, 0.0)
    pick = jnp.where(pick_row < 2, pick, 0.0).astype(BF16)
    puts = []
    for i in range(n_pen // 2):
        first_column = pl.multiple_of((pen ^ (2 * i + core)) * columns, columns)
        here = tiles[i][...]
        step = lax.dot_general(
            table_ref[...],
            jnp.concatenate([here, here], axis=0),
            (((0,), (0,)), ((), ())),
            preferred_element_type=F32,
        )
        for r in range(per_owner):
            for c in range(2):
                first = (c * per_owner + r) * depth
                held = blocks[i][r, c].astype(F32)
                made[i, r, c] = (held + step[first : first + depth]).astype(BF16)
        to = out_ref.at[:, :, :, pl.ds(first_column, columns)]
        puts.append(pltpu.make_async_copy(made.at[i], to, out_sems.at[i]))
        puts[-1].start()
        own = jnp.dot(pick, here, preferred_element_type=F32)
        residual_ref[0, :, pl.ds(first_column, columns)] = own[:2].astype(BF16)
    return puts


def adjoint_like(n_pen, chunk, per_owner, table_ref, *rest):
    chips = n_pen // 2
    kept, tiles, (out_ref, residual_ref, made, out_sems) = rest[:chips], rest[chips:n_pen], rest[n_pen:]
    residual_ref[...] = jnp.zeros_like(residual_ref)
    blocks = [one.at[0] for one in kept]
    for put in adjoint(n_pen, chunk, per_owner, 0, table_ref, blocks, tiles, out_ref, residual_ref, made, out_sems):
        put.wait()


def adjoint_other(n_pen, chunk, per_owner, table_ref, begun_ref, part_ref, own_ref, near_ref, far_ref, tiles_ref,
                  out_ref, residual_ref, made, out_sems, whole, whole_sem):
    del begun_ref
    chips = n_pen // 2
    whole[...] = part_ref[...]
    blocks = [own_ref, near_ref.at[0]] + [far_ref.at[i] for i in range(chips - 2)]
    tiles = [tiles_ref.at[i] for i in range(chips)]
    puts = adjoint(n_pen, chunk, per_owner, 1, table_ref, blocks, tiles, out_ref, whole, made, out_sems)
    puts.append(pltpu.make_async_copy(whole, residual_ref, whole_sem))
    puts[-1].start()
    for put in puts:
        put.wait()


def body(spectrum, depth_weights, pair_tilt, pair_tile_within, tilt_pos, owner, measured):
    n_pen = lax.axis_size("pen")
    n_kz = lax.axis_size("kz")
    blocks, _, depth, columns = spectrum.shape
    per_owner = blocks // n_pen
    pairs = depth_weights.shape[1]
    tile_dev, _, cells = measured.shape
    chunk = tile_dev * n_pen
    tiles = chunk * n_kz
    tiles_per_tilt = tiles // tilt_pos.shape[0]

    chips = n_pen // 2

    def call(kernel, *static):
        def bound(*refs):
            return kernel(*static, *refs)
        return bound

    def across(value, k):
        return lax.ppermute(value, "kz", [(i, i ^ k) for i in range(n_kz)])

    def between(value, k):
        return lax.ppermute(value, "pen", [(i, i ^ k) for i in range(n_pen)])

    pair = (per_owner, 2, depth, columns)
    group = jax.ShapeDtypeStruct((n_kz // 2, 2 * chunk, columns), F32)
    *outs, inverse, sums, sent_sums = pl.pallas_call(
        call(order_and_forward, n_pen, n_kz, chunk, per_owner, tiles_per_tilt),
        out_shape=[jax.ShapeDtypeStruct((2, per_owner, 2, depth, columns), BF16)] * chips
        + [jax.ShapeDtypeStruct((blocks,), I32), group, group],
        in_specs=[ANY] * 6,
        out_specs=[ANY] * chips + [SMEM, ANY, ANY],
        scratch_shapes=[
            pltpu.VMEM(spectrum.shape, BF16),
            pltpu.SMEM((blocks,), I32),
            pltpu.SMEM(tilt_pos.shape, I32),
            pltpu.VMEM(pair_tilt.shape, I32),
            pltpu.VMEM(pair_tile_within.shape, I32),
            pltpu.VMEM(depth_weights.shape, BF16),
            pltpu.SMEM((n_pen,), I32),
            pltpu.VMEM((2 * tiles, blocks * depth), BF16),
            pltpu.VMEM(group.shape, F32),
            pltpu.VMEM(group.shape, F32),
            pltpu.SemaphoreType.DMA((5,)),
            pltpu.SemaphoreType.DMA((blocks,)),
            pltpu.SemaphoreType.DMA((n_pen, per_owner)),
            pltpu.SemaphoreType.DMA((2,)),
        ],
        compiler_params=pltpu.CompilerParams(vmem_limit_bytes=62 << 20),
    )(owner, tilt_pos, pair_tilt, pair_tile_within, depth_weights, spectrum)
    kept = [outs[0]] + [between(outs[i], 2 * i) for i in range(1, chips)]

    arrived = across(sent_sums, 1)
    step = 2
    while step < n_kz:
        sums = (sums + arrived).reshape(-1, 2, 2 * chunk, columns)
        sums, arrived = sums[:, 0], across(sums[:, 1], step)
        step *= 2

    sent = measured.reshape(2, n_pen, columns).transpose(1, 0, 2)
    cores = [[2 * i + core for i in range(chips)] for core in range(2)]
    got = lax.all_to_all(sent, "pen", split_axis=0, concat_axis=0, tiled=True, axis_index_groups=cores)
    got = got.reshape(chips, 2, 2, columns)
    got_swapped = between(got, 1)
    own, table = pl.pallas_call(
        call(residual_and_table, n_kz, chunk, per_owner, tiles_per_tilt),
        out_shape=[
            jax.ShapeDtypeStruct((2 * chunk, columns), BF16),
            jax.ShapeDtypeStruct((4 * tiles, 2 * per_owner * depth), BF16),
        ],
        in_specs=[SMEM, SMEM] + [VMEM] * 7,
        out_specs=[VMEM, VMEM],
        scratch_shapes=[pltpu.VMEM((blocks, pairs), I32), pltpu.VMEM((2 * chunk, columns), F32)],
        compiler_params=pltpu.CompilerParams(vmem_limit_bytes=8 << 20),
    )(
        inverse,
        tilt_pos,
        pair_tilt,
        pair_tile_within,
        depth_weights,
        sums.reshape(2 * chunk, columns),
        arrived.reshape(2 * chunk, columns),
        got,
        got_swapped,
    )

    held = own
    step = 1
    while 2 * step < n_kz:
        held = jnp.concatenate([held, across(held, step)], axis=0)
        step *= 2
    def take_other(arrived, after):
        return pl.pallas_call(
            call(other_core, len(arrived)),
            out_shape=jax.ShapeDtypeStruct((len(arrived), *pair), BF16),
            in_specs=[ANY] * (len(arrived) + len(after)),
            out_specs=ANY,
            scratch_shapes=[pltpu.SemaphoreType.DMA((len(arrived),))],
            compiler_params=pltpu.CompilerParams(vmem_limit_bytes=8 << 20),
        )(*arrived, *after)

    own_swapped = between(outs[0][1], 1)
    near_swapped = between(take_other(kept[1:2], [held]), 1)
    held = pl.pallas_call(
        join_tiles,
        out_shape=jax.ShapeDtypeStruct((2 * tiles, columns), BF16),
        in_specs=[VMEM, VMEM, ANY, ANY],
        out_specs=VMEM,
        compiler_params=pltpu.CompilerParams(vmem_limit_bytes=8 << 20),
    )(held, across(held, step), own_swapped, near_swapped)
    like = [held] + [between(held, 2 * i) for i in range(1, chips)]
    far_swapped = between(take_other(kept[2:], like[1:]), 1)
    stacked = pl.pallas_call(
        stack_tiles,
        out_shape=jax.ShapeDtypeStruct((chips, 2 * tiles, columns), BF16),
        in_specs=[VMEM] * chips,
        out_specs=VMEM,
        compiler_params=pltpu.CompilerParams(vmem_limit_bytes=8 << 20),
    )(*like)
    other = between(stacked, 1)

    scratch = [pltpu.VMEM((chips, *pair), BF16), pltpu.SemaphoreType.DMA((chips,))]
    shapes = [
        jax.ShapeDtypeStruct((per_owner, 2, depth, cells), BF16),
        jax.ShapeDtypeStruct((tile_dev, 2, cells), BF16),
    ]
    begun, part = pl.pallas_call(
        call(adjoint_like, n_pen, chunk, per_owner),
        out_shape=shapes,
        in_specs=[VMEM] * (n_pen + 1),
        out_specs=[ANY, VMEM],
        scratch_shapes=scratch,
        compiler_params=pltpu.CompilerParams(vmem_limit_bytes=16 << 20),
    )(table, *kept, *like)
    updated, residual = pl.pallas_call(
        call(adjoint_other, n_pen, chunk, per_owner),
        out_shape=shapes,
        in_specs=[VMEM, ANY] + [VMEM] * 5,
        out_specs=[ANY, ANY],
        scratch_shapes=[*scratch, pltpu.VMEM(measured.shape, BF16), pltpu.SemaphoreType.DMA],
        input_output_aliases={1: 0},
        compiler_params=pltpu.CompilerParams(vmem_limit_bytes=16 << 20),
    )(table, begun, part, own_swapped, near_swapped, far_swapped, other)
    return (updated, residual)


def solution(mesh):
    return jax.shard_map(
        body,
        mesh=mesh,
        in_specs=(
            P("kz", None, None, "pen"),
            P("kz", None, None),
            P("kz", None),
            P("kz", None),
            P(),
            P("kz"),
            P(("kz", "pen"), None, None),
        ),
        out_specs=(P(("kz", "pen"), None, None, None), P(("kz", "pen"), None, None)),
        check_vma=False,
    )
```

```python
import jax
import jax.numpy as jnp
from jax import lax
from jax.experimental import pallas as pl
from jax.experimental.pallas import tpu as pltpu
from jax.sharding import PartitionSpec as P

BF16 = jnp.bfloat16
F32 = jnp.float32
I32 = jnp.int32
SMEM = pl.BlockSpec(memory_space=pltpu.SMEM)
VMEM = pl.BlockSpec(memory_space=pltpu.VMEM)
ANY = pl.BlockSpec(memory_space=pl.ANY)


def split_hi_lo(value):
    hi = value.astype(BF16)
    return hi, (value - hi.astype(F32)).astype(BF16)


def slots(tilt_pos_ref, tilt, within, tiles_per_tilt, flip):
    place = jnp.zeros_like(tilt)
    for t in range(tilt_pos_ref.shape[0]):
        place = jnp.where(tilt == t, tilt_pos_ref[t], place)
    return (place * tiles_per_tilt + within) ^ flip


def order_and_forward(n_pen, n_kz, chunk, per_owner, tiles_per_tilt, owner_ref, tilt_pos_ref, tilt_ref,
                      within_ref, weights_ref, spectrum_ref, *rest):
    chips = n_pen // 2
    outs, rest = rest[:chips], rest[chips:]
    kept_ref, sent_ref, held, owner, tilt_pos, tilt, within, weights, rest = *rest[:8], rest[8:]
    count, table, kept, sent, small_sems, in_sems, out_sems, sum_sems = rest
    blocks, pairs, depth = weights_ref.shape
    columns = spectrum_ref.shape[3]
    tiles = n_kz * chunk
    pen = lax.axis_index("pen")
    small = []
    for i, (from_ref, to) in enumerate(
        ((owner_ref, owner), (tilt_pos_ref, tilt_pos), (tilt_ref, tilt), (within_ref, within), (weights_ref, weights))
    ):
        small.append(pltpu.make_async_copy(from_ref, to, small_sems.at[i]))
        small[i].start()
    gets, puts = [], []
    for b in range(blocks):
        gets.append(pltpu.make_async_copy(spectrum_ref.at[b], held.at[b], in_sems.at[b]))
        gets[b].start()
    for o in range(n_pen):
        count[o] = 0
    for copy in small:
        copy.wait()
    slot = slots(tilt_pos, tilt[...], within[...], tiles_per_tilt, lax.axis_index("kz") * chunk)
    rows = lax.broadcasted_iota(I32, (tiles, pairs), 0)
    for b in range(blocks):
        hot = jnp.where(slot[b : b + 1, :] == rows, 1.0, 0.0).astype(BF16)
        hi, lo = split_hi_lo(jnp.dot(hot, weights[b], preferred_element_type=F32))
        table[:tiles, b * depth : (b + 1) * depth] = hi
        table[tiles:, b * depth : (b + 1) * depth] = lo
    for b in range(blocks):
        o = owner[b]
        r = count[o]
        count[o] = r + 1
        q = o ^ pen
        gets[b].wait()
        for i in range(chips):

            @pl.when(q >> 1 == i)
            def _(b=b, r=r, q=q, i=i):
                pltpu.make_async_copy(held.at[b], outs[i].at[q & 1, r], out_sems.at[q, r]).start()

    for q in range(n_pen):
        for r in range(per_owner):
            puts.append(pltpu.make_async_copy(held.at[0], outs[q // 2].at[q % 2, r], out_sems.at[q, r]))
    for c in range(2):
        both = jnp.dot(
            table[...],
            held[:, c].reshape(blocks * depth, columns),
            preferred_element_type=F32,
        )
        total = both[:tiles] + both[tiles:]
        for k in range(n_kz):
            to = sent if k % 2 else kept
            to[k // 2, c * chunk : (c + 1) * chunk, :] = total[k * chunk : (k + 1) * chunk]
    puts.append(pltpu.make_async_copy(kept, kept_ref, sum_sems.at[0]))
    puts[-1].start()
    puts.append(pltpu.make_async_copy(sent, sent_ref, sum_sems.at[1]))
    puts[-1].start()
    for put in puts:
        put.wait()


def residual_and_table(n_kz, chunk, per_owner, tiles_per_tilt, owner_ref, tilt_pos_ref, tilt_ref, within_ref,
                       weights_ref, sums_ref, arrived_ref, got_ref, swapped_ref, own_ref, out_ref, slot_ref, measured, owned):
    core = lax.axis_index("pen") & 1
    for i in range(got_ref.shape[0]):
        mine, theirs = got_ref[i, core].astype(F32), swapped_ref[i, core].astype(F32)
        first, second = jnp.where(core == 0, mine, theirs), jnp.where(core == 0, theirs, mine)
        for c in range(2):
            row = c * chunk + 2 * i
            measured[row : row + 1, :] = first[c : c + 1]
            measured[row + 1 : row + 2, :] = second[c : c + 1]
    own_ref[...] = (sums_ref[...] + arrived_ref[...] - measured[...]).astype(BF16)
    pairs, depth = weights_ref.shape[1:]
    rows_all = n_kz * 2 * chunk
    flip = lax.axis_index("kz") * chunk
    slot_ref[...] = slots(tilt_pos_ref, tilt_ref[...], within_ref[...], tiles_per_tilt, flip)
    rows = lax.broadcasted_iota(I32, (rows_all, pairs), 0)
    pen = lax.axis_index("pen")
    seen = jnp.int32(0)
    for b in range(owner_ref.shape[0]):
        hit = owner_ref[b] == pen

        @pl.when(hit)
        def _(b=b, seen=seen):
            owned[seen] = b

        seen = seen + hit.astype(I32)
    for r in range(per_owner):
        b = owned[r]
        at = slot_ref[pl.ds(b, 1), :]
        low = at & (chunk - 1)
        for c in range(2):
            place = (at - low) * 2 + c * chunk + low
            hot = jnp.where(place == rows, -8.0, 0.0).astype(BF16)
            hi, lo = split_hi_lo(jnp.dot(hot, weights_ref[b], preferred_element_type=F32))
            first = (c * per_owner + r) * depth
            out_ref[:rows_all, first : first + depth] = hi
            out_ref[rows_all:, first : first + depth] = lo


def join_tiles(first_ref, second_ref, *rest):
    out_ref = rest[-1]
    rows = first_ref.shape[0]
    out_ref[:rows] = first_ref[...]
    out_ref[rows:] = second_ref[...]


def other_core(count, *refs):
    in_refs, (out_ref, sems) = refs[:count], refs[-2:]
    copies = []
    for i, in_ref in enumerate(in_refs):
        copies.append(pltpu.make_async_copy(in_ref.at[1], out_ref.at[i], sems.at[i]))
        copies[i].start()
    for copy in copies:
        copy.wait()


def stack_tiles(*refs):
    in_refs, out_ref = refs[:-1], refs[-1]
    for i, in_ref in enumerate(in_refs):
        out_ref[i] = in_ref[...]


def adjoint(n_pen, chunk, per_owner, core, table_ref, blocks, tiles, out_ref, residual_ref, made, out_sems):
    pen = lax.axis_index("pen")
    depth, columns = made.shape[3:]
    rows = tiles[0].shape[0]
    pick_row = lax.broadcasted_iota(I32, (16, rows), 0)
    pick_at = lax.broadcasted_iota(I32, (16, rows), 1)
    pick = jnp.where(pick_at == pick_row * chunk + pen, 1.0, 0.0)
    pick = jnp.where(pick_row < 2, pick, 0.0).astype(BF16)
    puts = []
    for i in range(n_pen // 2):
        first_column = pl.multiple_of((pen ^ (2 * i + core)) * columns, columns)
        here = tiles[i][...]
        step = lax.dot_general(
            table_ref[...],
            jnp.concatenate([here, here], axis=0),
            (((0,), (0,)), ((), ())),
            preferred_element_type=F32,
        )
        for r in range(per_owner):
            for c in range(2):
                first = (c * per_owner + r) * depth
                held = blocks[i][r, c].astype(F32)
                made[i, r, c] = (held + step[first : first + depth]).astype(BF16)
        to = out_ref.at[:, :, :, pl.ds(first_column, columns)]
        puts.append(pltpu.make_async_copy(made.at[i], to, out_sems.at[i]))
        puts[-1].start()
        own = jnp.dot(pick, here, preferred_element_type=F32)
        residual_ref[0, :, pl.ds(first_column, columns)] = own[:2].astype(BF16)
    return puts


def adjoint_like(n_pen, chunk, per_owner, table_ref, *rest):
    chips = n_pen // 2
    kept, tiles, (out_ref, residual_ref, made, out_sems) = rest[:chips], rest[chips:n_pen], rest[n_pen:]
    residual_ref[...] = jnp.zeros_like(residual_ref)
    blocks = [one.at[0] for one in kept]
    for put in adjoint(n_pen, chunk, per_owner, 0, table_ref, blocks, tiles, out_ref, residual_ref, made, out_sems):
        put.wait()


def adjoint_other(n_pen, chunk, per_owner, table_ref, begun_ref, part_ref, own_ref, near_ref, far_ref, tiles_ref,
                  out_ref, residual_ref, made, out_sems, whole, whole_sem):
    del begun_ref
    chips = n_pen // 2
    whole[...] = part_ref[...]
    blocks = [own_ref, near_ref.at[0]] + [far_ref.at[i] for i in range(chips - 2)]
    tiles = [tiles_ref.at[i] for i in range(chips)]
    puts = adjoint(n_pen, chunk, per_owner, 1, table_ref, blocks, tiles, out_ref, whole, made, out_sems)
    puts.append(pltpu.make_async_copy(whole, residual_ref, whole_sem))
    puts[-1].start()
    for put in puts:
        put.wait()


def body(spectrum, depth_weights, pair_tilt, pair_tile_within, tilt_pos, owner, measured):
    n_pen = lax.axis_size("pen")
    n_kz = lax.axis_size("kz")
    blocks, _, depth, columns = spectrum.shape
    per_owner = blocks // n_pen
    pairs = depth_weights.shape[1]
    tile_dev, _, cells = measured.shape
    chunk = tile_dev * n_pen
    tiles = chunk * n_kz
    tiles_per_tilt = tiles // tilt_pos.shape[0]

    chips = n_pen // 2

    def call(kernel, *static):
        def bound(*refs):
            return kernel(*static, *refs)
        return bound

    def across(value, k):
        return lax.ppermute(value, "kz", [(i, i ^ k) for i in range(n_kz)])

    def between(value, k):
        return lax.ppermute(value, "pen", [(i, i ^ k) for i in range(n_pen)])

    pair = (per_owner, 2, depth, columns)
    group = jax.ShapeDtypeStruct((n_kz // 2, 2 * chunk, columns), F32)
    *outs, sums, sent_sums = pl.pallas_call(
        call(order_and_forward, n_pen, n_kz, chunk, per_owner, tiles_per_tilt),
        out_shape=[jax.ShapeDtypeStruct((2, per_owner, 2, depth, columns), BF16)] * chips
        + [group, group],
        in_specs=[ANY] * 6,
        out_specs=[ANY] * (chips + 2),
        scratch_shapes=[
            pltpu.VMEM(spectrum.shape, BF16),
            pltpu.SMEM((blocks,), I32),
            pltpu.SMEM(tilt_pos.shape, I32),
            pltpu.VMEM(pair_tilt.shape, I32),
            pltpu.VMEM(pair_tile_within.shape, I32),
            pltpu.VMEM(depth_weights.shape, BF16),
            pltpu.SMEM((n_pen,), I32),
            pltpu.VMEM((2 * tiles, blocks * depth), BF16),
            pltpu.VMEM(group.shape, F32),
            pltpu.VMEM(group.shape, F32),
            pltpu.SemaphoreType.DMA((5,)),
            pltpu.SemaphoreType.DMA((blocks,)),
            pltpu.SemaphoreType.DMA((n_pen, per_owner)),
            pltpu.SemaphoreType.DMA((2,)),
        ],
        compiler_params=pltpu.CompilerParams(vmem_limit_bytes=62 << 20),
    )(owner, tilt_pos, pair_tilt, pair_tile_within, depth_weights, spectrum)
    kept = [outs[0]] + [between(outs[i], 2 * i) for i in range(1, chips)]

    arrived = across(sent_sums, 1)
    step = 2
    while step < n_kz:
        sums = (sums + arrived).reshape(-1, 2, 2 * chunk, columns)
        sums, arrived = sums[:, 0], across(sums[:, 1], step)
        step *= 2

    sent = measured.reshape(2, n_pen, columns).transpose(1, 0, 2)
    cores = [[2 * i + core for i in range(chips)] for core in range(2)]
    got = lax.all_to_all(sent, "pen", split_axis=0, concat_axis=0, tiled=True, axis_index_groups=cores)
    got = got.reshape(chips, 2, 2, columns)
    got_swapped = between(got, 1)
    own, table = pl.pallas_call(
        call(residual_and_table, n_kz, chunk, per_owner, tiles_per_tilt),
        out_shape=[
            jax.ShapeDtypeStruct((2 * chunk, columns), BF16),
            jax.ShapeDtypeStruct((4 * tiles, 2 * per_owner * depth), BF16),
        ],
        in_specs=[SMEM, SMEM] + [VMEM] * 7,
        out_specs=[VMEM, VMEM],
        scratch_shapes=[
            pltpu.VMEM((blocks, pairs), I32),
            pltpu.VMEM((2 * chunk, columns), F32),
            pltpu.SMEM((per_owner,), I32),
        ],
        compiler_params=pltpu.CompilerParams(vmem_limit_bytes=8 << 20),
    )(
        owner,
        tilt_pos,
        pair_tilt,
        pair_tile_within,
        depth_weights,
        sums.reshape(2 * chunk, columns),
        arrived.reshape(2 * chunk, columns),
        got,
        got_swapped,
    )

    held = own
    step = 1
    while 2 * step < n_kz:
        held = jnp.concatenate([held, across(held, step)], axis=0)
        step *= 2
    def take_other(arrived, after):
        return pl.pallas_call(
            call(other_core, len(arrived)),
            out_shape=jax.ShapeDtypeStruct((len(arrived), *pair), BF16),
            in_specs=[ANY] * (len(arrived) + len(after)),
            out_specs=ANY,
            scratch_shapes=[pltpu.SemaphoreType.DMA((len(arrived),))],
            compiler_params=pltpu.CompilerParams(vmem_limit_bytes=8 << 20),
        )(*arrived, *after)

    own_swapped = between(outs[0][1], 1)
    near_swapped = between(take_other(kept[1:2], [held]), 1)
    held = pl.pallas_call(
        join_tiles,
        out_shape=jax.ShapeDtypeStruct((2 * tiles, columns), BF16),
        in_specs=[VMEM, VMEM, ANY, ANY],
        out_specs=VMEM,
        compiler_params=pltpu.CompilerParams(vmem_limit_bytes=8 << 20),
    )(held, across(held, step), own_swapped, near_swapped)
    like = [held] + [between(held, 2 * i) for i in range(1, chips)]
    far_swapped = between(take_other(kept[2:], like[1:]), 1)
    stacked = pl.pallas_call(
        stack_tiles,
        out_shape=jax.ShapeDtypeStruct((chips, 2 * tiles, columns), BF16),
        in_specs=[VMEM] * chips,
        out_specs=VMEM,
        compiler_params=pltpu.CompilerParams(vmem_limit_bytes=8 << 20),
    )(*like)
    other = between(stacked, 1)

    scratch = [pltpu.VMEM((chips, *pair), BF16), pltpu.SemaphoreType.DMA((chips,))]
    shapes = [
        jax.ShapeDtypeStruct((per_owner, 2, depth, cells), BF16),
        jax.ShapeDtypeStruct((tile_dev, 2, cells), BF16),
    ]
    begun, part = pl.pallas_call(
        call(adjoint_like, n_pen, chunk, per_owner),
        out_shape=shapes,
        in_specs=[VMEM] * (n_pen + 1),
        out_specs=[ANY, VMEM],
        scratch_shapes=scratch,
        compiler_params=pltpu.CompilerParams(vmem_limit_bytes=16 << 20),
    )(table, *kept, *like)
    updated, residual = pl.pallas_call(
        call(adjoint_other, n_pen, chunk, per_owner),
        out_shape=shapes,
        in_specs=[VMEM, ANY] + [VMEM] * 5,
        out_specs=[ANY, ANY],
        scratch_shapes=[*scratch, pltpu.VMEM(measured.shape, BF16), pltpu.SemaphoreType.DMA],
        input_output_aliases={1: 0},
        compiler_params=pltpu.CompilerParams(vmem_limit_bytes=16 << 20),
    )(table, begun, part, own_swapped, near_swapped, far_swapped, other)
    return (updated, residual)


def solution(mesh):
    return jax.shard_map(
        body,
        mesh=mesh,
        in_specs=(
            P("kz", None, None, "pen"),
            P("kz", None, None),
            P("kz", None),
            P("kz", None),
            P(),
            P("kz"),
            P(("kz", "pen"), None, None),
        ),
        out_specs=(P(("kz", "pen"), None, None, None), P(("kz", "pen"), None, None)),
        check_vma=False,
    )
```

```python
import jax
import jax.numpy as jnp
from jax import lax
from jax.experimental import pallas as pl
from jax.experimental.pallas import tpu as pltpu
from jax.sharding import PartitionSpec as P

BF16 = jnp.bfloat16
F32 = jnp.float32
I32 = jnp.int32
SMEM = pl.BlockSpec(memory_space=pltpu.SMEM)
VMEM = pl.BlockSpec(memory_space=pltpu.VMEM)
ANY = pl.BlockSpec(memory_space=pl.ANY)


def split_hi_lo(value):
    hi = value.astype(BF16)
    return hi, (value - hi.astype(F32)).astype(BF16)


def slots(tilt_pos_ref, tilt, within, tiles_per_tilt, flip):
    place = jnp.zeros_like(tilt)
    for t in range(tilt_pos_ref.shape[0]):
        place = jnp.where(tilt == t, tilt_pos_ref[t], place)
    return (place * tiles_per_tilt + within) ^ flip


def order_and_forward(n_pen, n_kz, chunk, per_owner, tiles_per_tilt, owner_ref, tilt_pos_ref, tilt_ref,
                      within_ref, weights_ref, spectrum_ref, *rest):
    chips = n_pen // 2
    outs, rest = rest[:chips], rest[chips:]
    kept_ref, sent_ref, held, owner, tilt_pos, tilt, within, weights, rest = *rest[:8], rest[8:]
    count, table, kept, sent, small_sems, in_sems, out_sems, sum_sems = rest
    blocks, pairs, depth = weights_ref.shape
    columns = spectrum_ref.shape[3]
    tiles = n_kz * chunk
    pen = lax.axis_index("pen")
    small = []
    for i, (from_ref, to) in enumerate(
        ((owner_ref, owner), (tilt_pos_ref, tilt_pos), (tilt_ref, tilt), (within_ref, within), (weights_ref, weights))
    ):
        small.append(pltpu.make_async_copy(from_ref, to, small_sems.at[i]))
        small[i].start()
    gets, puts = [], []
    for b in range(blocks):
        gets.append(pltpu.make_async_copy(spectrum_ref.at[b], held.at[b], in_sems.at[b]))
        gets[b].start()
    for o in range(n_pen):
        count[o] = 0
    for copy in small:
        copy.wait()
    slot = slots(tilt_pos, tilt[...], within[...], tiles_per_tilt, lax.axis_index("kz") * chunk)
    rows = lax.broadcasted_iota(I32, (tiles, pairs), 0)
    for b in range(blocks):
        hot = jnp.where(slot[b : b + 1, :] == rows, 1.0, 0.0).astype(BF16)
        hi, lo = split_hi_lo(jnp.dot(hot, weights[b], preferred_element_type=F32))
        table[:tiles, b * depth : (b + 1) * depth] = hi
        table[tiles:, b * depth : (b + 1) * depth] = lo
    both = [jnp.zeros((2 * tiles, columns), F32)] * 2
    for first in range(0, blocks, 4):
        for b in range(first, first + 4):
            o = owner[b]
            r = count[o]
            count[o] = r + 1
            q = o ^ pen
            gets[b].wait()
            for i in range(chips):

                @pl.when(q >> 1 == i)
                def _(b=b, r=r, q=q, i=i):
                    pltpu.make_async_copy(held.at[b], outs[i].at[q & 1, r], out_sems.at[q, r]).start()

        weight = table[:, first * depth : (first + 4) * depth]
        for c in range(2):
            here = held[first : first + 4, c].reshape(4 * depth, columns)
            both[c] = both[c] + jnp.dot(weight, here, preferred_element_type=F32)
    for c in range(2):
        total = both[c][:tiles] + both[c][tiles:]
        for k in range(n_kz):
            to = sent if k % 2 else kept
            to[k // 2, c * chunk : (c + 1) * chunk, :] = total[k * chunk : (k + 1) * chunk]
    for q in range(n_pen):
        for r in range(per_owner):
            puts.append(pltpu.make_async_copy(held.at[0], outs[q // 2].at[q % 2, r], out_sems.at[q, r]))
    puts.append(pltpu.make_async_copy(kept, kept_ref, sum_sems.at[0]))
    puts[-1].start()
    puts.append(pltpu.make_async_copy(sent, sent_ref, sum_sems.at[1]))
    puts[-1].start()
    for put in puts:
        put.wait()


def residual_and_table(n_kz, chunk, per_owner, tiles_per_tilt, owner_ref, tilt_pos_ref, tilt_ref, within_ref,
                       weights_ref, sums_ref, arrived_ref, got_ref, swapped_ref, own_ref, out_ref, slot_ref, measured, owned):
    core = lax.axis_index("pen") & 1
    for i in range(got_ref.shape[0]):
        mine, theirs = got_ref[i, core].astype(F32), swapped_ref[i, core].astype(F32)
        first, second = jnp.where(core == 0, mine, theirs), jnp.where(core == 0, theirs, mine)
        for c in range(2):
            row = c * chunk + 2 * i
            measured[row : row + 1, :] = first[c : c + 1]
            measured[row + 1 : row + 2, :] = second[c : c + 1]
    own_ref[...] = (sums_ref[...] + arrived_ref[...] - measured[...]).astype(BF16)
    pairs, depth = weights_ref.shape[1:]
    rows_all = n_kz * 2 * chunk
    flip = lax.axis_index("kz") * chunk
    slot_ref[...] = slots(tilt_pos_ref, tilt_ref[...], within_ref[...], tiles_per_tilt, flip)
    rows = lax.broadcasted_iota(I32, (rows_all, pairs), 0)
    pen = lax.axis_index("pen")
    seen = jnp.int32(0)
    for b in range(owner_ref.shape[0]):
        hit = owner_ref[b] == pen

        @pl.when(hit)
        def _(b=b, seen=seen):
            owned[seen] = b

        seen = seen + hit.astype(I32)
    for r in range(per_owner):
        b = owned[r]
        at = slot_ref[pl.ds(b, 1), :]
        low = at & (chunk - 1)
        for c in range(2):
            place = (at - low) * 2 + c * chunk + low
            hot = jnp.where(place == rows, -8.0, 0.0).astype(BF16)
            hi, lo = split_hi_lo(jnp.dot(hot, weights_ref[b], preferred_element_type=F32))
            first = (c * per_owner + r) * depth
            out_ref[:rows_all, first : first + depth] = hi
            out_ref[rows_all:, first : first + depth] = lo


def join_tiles(first_ref, second_ref, *rest):
    out_ref = rest[-1]
    rows = first_ref.shape[0]
    out_ref[:rows] = first_ref[...]
    out_ref[rows:] = second_ref[...]


def other_core(count, *refs):
    in_refs, (out_ref, sems) = refs[:count], refs[-2:]
    copies = []
    for i, in_ref in enumerate(in_refs):
        copies.append(pltpu.make_async_copy(in_ref.at[1], out_ref.at[i], sems.at[i]))
        copies[i].start()
    for copy in copies:
        copy.wait()


def stack_tiles(*refs):
    in_refs, out_ref = refs[:-1], refs[-1]
    for i, in_ref in enumerate(in_refs):
        out_ref[i] = in_ref[...]


def adjoint(n_pen, chunk, per_owner, core, table_ref, blocks, tiles, out_ref, residual_ref, made, out_sems):
    pen = lax.axis_index("pen")
    depth, columns = made.shape[3:]
    rows = tiles[0].shape[0]
    pick_row = lax.broadcasted_iota(I32, (16, rows), 0)
    pick_at = lax.broadcasted_iota(I32, (16, rows), 1)
    pick = jnp.where(pick_at == pick_row * chunk + pen, 1.0, 0.0)
    pick = jnp.where(pick_row < 2, pick, 0.0).astype(BF16)
    puts = []
    for i in range(n_pen // 2):
        first_column = pl.multiple_of((pen ^ (2 * i + core)) * columns, columns)
        here = tiles[i][...]
        step = lax.dot_general(
            table_ref[...],
            jnp.concatenate([here, here], axis=0),
            (((0,), (0,)), ((), ())),
            preferred_element_type=F32,
        )
        for r in range(per_owner):
            for c in range(2):
                first = (c * per_owner + r) * depth
                held = blocks[i][r, c].astype(F32)
                made[i, r, c] = (held + step[first : first + depth]).astype(BF16)
        to = out_ref.at[:, :, :, pl.ds(first_column, columns)]
        puts.append(pltpu.make_async_copy(made.at[i], to, out_sems.at[i]))
        puts[-1].start()
        own = jnp.dot(pick, here, preferred_element_type=F32)
        residual_ref[0, :, pl.ds(first_column, columns)] = own[:2].astype(BF16)
    return puts


def adjoint_like(n_pen, chunk, per_owner, table_ref, *rest):
    chips = n_pen // 2
    kept, tiles, (out_ref, residual_ref, made, out_sems) = rest[:chips], rest[chips:n_pen], rest[n_pen:]
    residual_ref[...] = jnp.zeros_like(residual_ref)
    blocks = [one.at[0] for one in kept]
    for put in adjoint(n_pen, chunk, per_owner, 0, table_ref, blocks, tiles, out_ref, residual_ref, made, out_sems):
        put.wait()


def adjoint_other(n_pen, chunk, per_owner, table_ref, begun_ref, part_ref, own_ref, near_ref, far_ref, tiles_ref,
                  out_ref, residual_ref, made, out_sems, whole, whole_sem):
    del begun_ref
    chips = n_pen // 2
    whole[...] = part_ref[...]
    blocks = [own_ref, near_ref.at[0]] + [far_ref.at[i] for i in range(chips - 2)]
    tiles = [tiles_ref.at[i] for i in range(chips)]
    puts = adjoint(n_pen, chunk, per_owner, 1, table_ref, blocks, tiles, out_ref, whole, made, out_sems)
    puts.append(pltpu.make_async_copy(whole, residual_ref, whole_sem))
    puts[-1].start()
    for put in puts:
        put.wait()


def body(spectrum, depth_weights, pair_tilt, pair_tile_within, tilt_pos, owner, measured):
    n_pen = lax.axis_size("pen")
    n_kz = lax.axis_size("kz")
    blocks, _, depth, columns = spectrum.shape
    per_owner = blocks // n_pen
    pairs = depth_weights.shape[1]
    tile_dev, _, cells = measured.shape
    chunk = tile_dev * n_pen
    tiles = chunk * n_kz
    tiles_per_tilt = tiles // tilt_pos.shape[0]

    chips = n_pen // 2

    def call(kernel, *static):
        def bound(*refs):
            return kernel(*static, *refs)
        return bound

    def across(value, k):
        return lax.ppermute(value, "kz", [(i, i ^ k) for i in range(n_kz)])

    def between(value, k):
        return lax.ppermute(value, "pen", [(i, i ^ k) for i in range(n_pen)])

    pair = (per_owner, 2, depth, columns)
    group = jax.ShapeDtypeStruct((n_kz // 2, 2 * chunk, columns), F32)
    *outs, sums, sent_sums = pl.pallas_call(
        call(order_and_forward, n_pen, n_kz, chunk, per_owner, tiles_per_tilt),
        out_shape=[jax.ShapeDtypeStruct((2, per_owner, 2, depth, columns), BF16)] * chips
        + [group, group],
        in_specs=[ANY] * 6,
        out_specs=[ANY] * (chips + 2),
        scratch_shapes=[
            pltpu.VMEM(spectrum.shape, BF16),
            pltpu.SMEM((blocks,), I32),
            pltpu.SMEM(tilt_pos.shape, I32),
            pltpu.VMEM(pair_tilt.shape, I32),
            pltpu.VMEM(pair_tile_within.shape, I32),
            pltpu.VMEM(depth_weights.shape, BF16),
            pltpu.SMEM((n_pen,), I32),
            pltpu.VMEM((2 * tiles, blocks * depth), BF16),
            pltpu.VMEM(group.shape, F32),
            pltpu.VMEM(group.shape, F32),
            pltpu.SemaphoreType.DMA((5,)),
            pltpu.SemaphoreType.DMA((blocks,)),
            pltpu.SemaphoreType.DMA((n_pen, per_owner)),
            pltpu.SemaphoreType.DMA((2,)),
        ],
        compiler_params=pltpu.CompilerParams(vmem_limit_bytes=62 << 20),
    )(owner, tilt_pos, pair_tilt, pair_tile_within, depth_weights, spectrum)
    kept = [outs[0]] + [between(outs[i], 2 * i) for i in range(1, chips)]

    arrived = across(sent_sums, 1)
    step = 2
    while step < n_kz:
        sums = (sums + arrived).reshape(-1, 2, 2 * chunk, columns)
        sums, arrived = sums[:, 0], across(sums[:, 1], step)
        step *= 2

    sent = measured.reshape(2, n_pen, columns).transpose(1, 0, 2)
    cores = [[2 * i + core for i in range(chips)] for core in range(2)]
    got = lax.all_to_all(sent, "pen", split_axis=0, concat_axis=0, tiled=True, axis_index_groups=cores)
    got = got.reshape(chips, 2, 2, columns)
    got_swapped = between(got, 1)
    own, table = pl.pallas_call(
        call(residual_and_table, n_kz, chunk, per_owner, tiles_per_tilt),
        out_shape=[
            jax.ShapeDtypeStruct((2 * chunk, columns), BF16),
            jax.ShapeDtypeStruct((4 * tiles, 2 * per_owner * depth), BF16),
        ],
        in_specs=[SMEM, SMEM] + [VMEM] * 7,
        out_specs=[VMEM, VMEM],
        scratch_shapes=[
            pltpu.VMEM((blocks, pairs), I32),
            pltpu.VMEM((2 * chunk, columns), F32),
            pltpu.SMEM((per_owner,), I32),
        ],
        compiler_params=pltpu.CompilerParams(vmem_limit_bytes=8 << 20),
    )(
        owner,
        tilt_pos,
        pair_tilt,
        pair_tile_within,
        depth_weights,
        sums.reshape(2 * chunk, columns),
        arrived.reshape(2 * chunk, columns),
        got,
        got_swapped,
    )

    held = own
    step = 1
    while 2 * step < n_kz:
        held = jnp.concatenate([held, across(held, step)], axis=0)
        step *= 2
    def take_other(arrived, after):
        return pl.pallas_call(
            call(other_core, len(arrived)),
            out_shape=jax.ShapeDtypeStruct((len(arrived), *pair), BF16),
            in_specs=[ANY] * (len(arrived) + len(after)),
            out_specs=ANY,
            scratch_shapes=[pltpu.SemaphoreType.DMA((len(arrived),))],
            compiler_params=pltpu.CompilerParams(vmem_limit_bytes=8 << 20),
        )(*arrived, *after)

    own_swapped = between(outs[0][1], 1)
    near_swapped = between(take_other(kept[1:2], [held]), 1)
    held = pl.pallas_call(
        join_tiles,
        out_shape=jax.ShapeDtypeStruct((2 * tiles, columns), BF16),
        in_specs=[VMEM, VMEM, ANY, ANY],
        out_specs=VMEM,
        compiler_params=pltpu.CompilerParams(vmem_limit_bytes=8 << 20),
    )(held, across(held, step), own_swapped, near_swapped)
    like = [held] + [between(held, 2 * i) for i in range(1, chips)]
    far_swapped = between(take_other(kept[2:], like[1:]), 1)
    stacked = pl.pallas_call(
        stack_tiles,
        out_shape=jax.ShapeDtypeStruct((chips, 2 * tiles, columns), BF16),
        in_specs=[VMEM] * chips,
        out_specs=VMEM,
        compiler_params=pltpu.CompilerParams(vmem_limit_bytes=8 << 20),
    )(*like)
    other = between(stacked, 1)

    scratch = [pltpu.VMEM((chips, *pair), BF16), pltpu.SemaphoreType.DMA((chips,))]
    shapes = [
        jax.ShapeDtypeStruct((per_owner, 2, depth, cells), BF16),
        jax.ShapeDtypeStruct((tile_dev, 2, cells), BF16),
    ]
    begun, part = pl.pallas_call(
        call(adjoint_like, n_pen, chunk, per_owner),
        out_shape=shapes,
        in_specs=[VMEM] * (n_pen + 1),
        out_specs=[ANY, VMEM],
        scratch_shapes=scratch,
        compiler_params=pltpu.CompilerParams(vmem_limit_bytes=16 << 20),
    )(table, *kept, *like)
    updated, residual = pl.pallas_call(
        call(adjoint_other, n_pen, chunk, per_owner),
        out_shape=shapes,
        in_specs=[VMEM, ANY] + [VMEM] * 5,
        out_specs=[ANY, ANY],
        scratch_shapes=[*scratch, pltpu.VMEM(measured.shape, BF16), pltpu.SemaphoreType.DMA],
        input_output_aliases={1: 0},
        compiler_params=pltpu.CompilerParams(vmem_limit_bytes=16 << 20),
    )(table, begun, part, own_swapped, near_swapped, far_swapped, other)
    return (updated, residual)


def solution(mesh):
    return jax.shard_map(
        body,
        mesh=mesh,
        in_specs=(
            P("kz", None, None, "pen"),
            P("kz", None, None),
            P("kz", None),
            P("kz", None),
            P(),
            P("kz"),
            P(("kz", "pen"), None, None),
        ),
        out_specs=(P(("kz", "pen"), None, None, None), P(("kz", "pen"), None, None)),
        check_vma=False,
    )
```

```python
import jax
import jax.numpy as jnp
from jax import lax
from jax.experimental import pallas as pl
from jax.experimental.pallas import tpu as pltpu
from jax.sharding import PartitionSpec as P

BF16 = jnp.bfloat16
F32 = jnp.float32
I32 = jnp.int32
SMEM = pl.BlockSpec(memory_space=pltpu.SMEM)
VMEM = pl.BlockSpec(memory_space=pltpu.VMEM)
ANY = pl.BlockSpec(memory_space=pl.ANY)


def split_hi_lo(value):
    hi = value.astype(BF16)
    return hi, (value - hi.astype(F32)).astype(BF16)


def slots(tilt_pos_ref, tilt, within, tiles_per_tilt, flip):
    place = jnp.zeros_like(tilt)
    for t in range(tilt_pos_ref.shape[0]):
        place = jnp.where(tilt == t, tilt_pos_ref[t], place)
    return (place * tiles_per_tilt + within) ^ flip


def order_and_forward(n_pen, n_kz, chunk, per_owner, tiles_per_tilt, owner_ref, tilt_pos_ref, tilt_ref,
                      within_ref, weights_ref, spectrum_ref, *rest):
    chips = n_pen // 2
    outs, rest = rest[:chips], rest[chips:]
    kept_ref, sent_ref, held, owner, tilt_pos, tilt, within, weights, rest = *rest[:8], rest[8:]
    count, table, kept, sent, small_sems, in_sems, out_sems, sum_sems = rest
    blocks, pairs, depth = weights_ref.shape
    columns = spectrum_ref.shape[3]
    tiles = n_kz * chunk
    pen = lax.axis_index("pen")
    small = []
    for i, (from_ref, to) in enumerate(
        ((owner_ref, owner), (tilt_pos_ref, tilt_pos), (tilt_ref, tilt), (within_ref, within), (weights_ref, weights))
    ):
        small.append(pltpu.make_async_copy(from_ref, to, small_sems.at[i]))
        small[i].start()
    gets, puts = [], []
    for b in range(blocks):
        gets.append(pltpu.make_async_copy(spectrum_ref.at[b], held.at[b], in_sems.at[b]))
        gets[b].start()
    for o in range(n_pen):
        count[o] = 0
    for copy in small:
        copy.wait()
    slot = slots(tilt_pos, tilt[...], within[...], tiles_per_tilt, lax.axis_index("kz") * chunk)
    rows = lax.broadcasted_iota(I32, (tiles, pairs), 0)
    for b in range(blocks):
        hot = jnp.where(slot[b : b + 1, :] == rows, 1.0, 0.0).astype(BF16)
        hi, lo = split_hi_lo(jnp.dot(hot, weights[b], preferred_element_type=F32))
        table[:tiles, b * depth : (b + 1) * depth] = hi
        table[tiles:, b * depth : (b + 1) * depth] = lo
    for b in range(blocks):
        o = owner[b]
        r = count[o]
        count[o] = r + 1
        q = o ^ pen
        gets[b].wait()
        for i in range(chips):

            @pl.when(q >> 1 == i)
            def _(b=b, r=r, q=q, i=i):
                pltpu.make_async_copy(held.at[b], outs[i].at[q & 1, r], out_sems.at[q, r]).start()

    for q in range(n_pen):
        for r in range(per_owner):
            puts.append(pltpu.make_async_copy(held.at[0], outs[q // 2].at[q % 2, r], out_sems.at[q, r]))
    for c in range(2):
        both = jnp.dot(
            table[...],
            held[:, c].reshape(blocks * depth, columns),
            preferred_element_type=F32,
        )
        total = both[:tiles] + both[tiles:]
        for k in range(n_kz):
            to = sent if k % 2 else kept
            to[k // 2, c * chunk : (c + 1) * chunk, :] = total[k * chunk : (k + 1) * chunk]
    puts.append(pltpu.make_async_copy(kept, kept_ref, sum_sems.at[0]))
    puts[-1].start()
    puts.append(pltpu.make_async_copy(sent, sent_ref, sum_sems.at[1]))
    puts[-1].start()
    for put in puts:
        put.wait()


def residual_and_table(n_kz, chunk, per_owner, tiles_per_tilt, owner_ref, tilt_pos_ref, tilt_ref, within_ref,
                       weights_ref, sums_ref, arrived_ref, got_ref, swapped_ref, own_ref, out_ref, slot_ref, measured, owned):
    core = lax.axis_index("pen") & 1
    for i in range(got_ref.shape[0]):
        mine, theirs = got_ref[i, core].astype(F32), swapped_ref[i, core].astype(F32)
        first, second = jnp.where(core == 0, mine, theirs), jnp.where(core == 0, theirs, mine)
        for c in range(2):
            row = c * chunk + 2 * i
            measured[row : row + 1, :] = first[c : c + 1]
            measured[row + 1 : row + 2, :] = second[c : c + 1]
    own_ref[...] = (sums_ref[...] + arrived_ref[...] - measured[...]).astype(BF16)
    pairs, depth = weights_ref.shape[1:]
    rows_all = n_kz * 2 * chunk
    flip = lax.axis_index("kz") * chunk
    slot_ref[...] = slots(tilt_pos_ref, tilt_ref[...], within_ref[...], tiles_per_tilt, flip)
    rows = lax.broadcasted_iota(I32, (rows_all, pairs), 0)
    pen = lax.axis_index("pen")
    seen = jnp.int32(0)
    for b in range(owner_ref.shape[0]):
        hit = owner_ref[b] == pen

        @pl.when(hit)
        def _(b=b, seen=seen):
            owned[seen] = b

        seen = seen + hit.astype(I32)
    for r in range(per_owner):
        b = owned[r]
        at = slot_ref[pl.ds(b, 1), :]
        low = at & (chunk - 1)
        for c in range(2):
            place = (at - low) * 2 + c * chunk + low
            hot = jnp.where(place == rows, -8.0, 0.0).astype(BF16)
            hi, lo = split_hi_lo(jnp.dot(hot, weights_ref[b], preferred_element_type=F32))
            first = (c * per_owner + r) * depth
            out_ref[:rows_all, first : first + depth] = hi
            out_ref[rows_all:, first : first + depth] = lo


def join_tiles(first_ref, second_ref, *rest):
    out_ref = rest[-1]
    rows = first_ref.shape[0]
    out_ref[:rows] = first_ref[...]
    out_ref[rows:] = second_ref[...]


def other_core(count, *refs):
    in_refs, (out_ref, sems) = refs[:count], refs[-2:]
    copies = []
    for i, in_ref in enumerate(in_refs):
        copies.append(pltpu.make_async_copy(in_ref.at[1], out_ref.at[i], sems.at[i]))
        copies[i].start()
    for copy in copies:
        copy.wait()


def stack_tiles(*refs):
    in_refs, out_ref = refs[:-1], refs[-1]
    for i, in_ref in enumerate(in_refs):
        out_ref[i] = in_ref[...]


def adjoint(n_pen, chunk, per_owner, core, table_ref, blocks, tiles, out_ref, residual_ref, made, out_sems):
    pen = lax.axis_index("pen")
    depth, columns = made.shape[3:]
    rows = tiles[0].shape[0]
    pick_row = lax.broadcasted_iota(I32, (16, rows), 0)
    pick_at = lax.broadcasted_iota(I32, (16, rows), 1)
    pick = jnp.where(pick_at == pick_row * chunk + pen, 1.0, 0.0)
    pick = jnp.where(pick_row < 2, pick, 0.0).astype(BF16)
    puts = []
    for i in range(n_pen // 2):
        first_column = pl.multiple_of((pen ^ (2 * i + core)) * columns, columns)
        here = tiles[i][...]
        step = lax.dot_general(
            table_ref[...],
            jnp.concatenate([here, here], axis=0),
            (((0,), (0,)), ((), ())),
            preferred_element_type=F32,
        )
        for r in range(per_owner):
            for c in range(2):
                first = (c * per_owner + r) * depth
                held = blocks[i][r, c].astype(F32)
                made[i, r, c] = (held + step[first : first + depth]).astype(BF16)
        to = out_ref.at[:, :, :, pl.ds(first_column, columns)]
        puts.append(pltpu.make_async_copy(made.at[i], to, out_sems.at[i]))
        puts[-1].start()
        own = jnp.dot(pick, here, preferred_element_type=F32)
        residual_ref[0, :, pl.ds(first_column, columns)] = own[:2].astype(BF16)
    return puts


def adjoint_like(n_pen, chunk, per_owner, table_ref, *rest):
    chips = n_pen // 2
    kept, tiles, (out_ref, residual_ref, made, out_sems) = rest[:chips], rest[chips:n_pen], rest[n_pen:]
    residual_ref[...] = jnp.zeros_like(residual_ref)
    blocks = [one.at[0] for one in kept]
    for put in adjoint(n_pen, chunk, per_owner, 0, table_ref, blocks, tiles, out_ref, residual_ref, made, out_sems):
        put.wait()


def adjoint_other(n_pen, chunk, per_owner, table_ref, begun_ref, part_ref, near_ref, far_ref, tiles_ref,
                  out_ref, residual_ref, made, out_sems, whole, whole_sem):
    del begun_ref
    chips = n_pen // 2
    whole[...] = part_ref[...]
    blocks = [near_ref.at[0], near_ref.at[1]] + [far_ref.at[i] for i in range(chips - 2)]
    tiles = [tiles_ref.at[i] for i in range(chips)]
    puts = adjoint(n_pen, chunk, per_owner, 1, table_ref, blocks, tiles, out_ref, whole, made, out_sems)
    puts.append(pltpu.make_async_copy(whole, residual_ref, whole_sem))
    puts[-1].start()
    for put in puts:
        put.wait()


def body(spectrum, depth_weights, pair_tilt, pair_tile_within, tilt_pos, owner, measured):
    n_pen = lax.axis_size("pen")
    n_kz = lax.axis_size("kz")
    blocks, _, depth, columns = spectrum.shape
    per_owner = blocks // n_pen
    pairs = depth_weights.shape[1]
    tile_dev, _, cells = measured.shape
    chunk = tile_dev * n_pen
    tiles = chunk * n_kz
    tiles_per_tilt = tiles // tilt_pos.shape[0]

    chips = n_pen // 2

    def call(kernel, *static):
        def bound(*refs):
            return kernel(*static, *refs)
        return bound

    def across(value, k):
        return lax.ppermute(value, "kz", [(i, i ^ k) for i in range(n_kz)])

    def between(value, k):
        return lax.ppermute(value, "pen", [(i, i ^ k) for i in range(n_pen)])

    pair = (per_owner, 2, depth, columns)
    group = jax.ShapeDtypeStruct((n_kz // 2, 2 * chunk, columns), F32)
    *outs, sums, sent_sums = pl.pallas_call(
        call(order_and_forward, n_pen, n_kz, chunk, per_owner, tiles_per_tilt),
        out_shape=[jax.ShapeDtypeStruct((2, per_owner, 2, depth, columns), BF16)] * chips
        + [group, group],
        in_specs=[ANY] * 6,
        out_specs=[ANY] * (chips + 2),
        scratch_shapes=[
            pltpu.VMEM(spectrum.shape, BF16),
            pltpu.SMEM((blocks,), I32),
            pltpu.SMEM(tilt_pos.shape, I32),
            pltpu.VMEM(pair_tilt.shape, I32),
            pltpu.VMEM(pair_tile_within.shape, I32),
            pltpu.VMEM(depth_weights.shape, BF16),
            pltpu.SMEM((n_pen,), I32),
            pltpu.VMEM((2 * tiles, blocks * depth), BF16),
            pltpu.VMEM(group.shape, F32),
            pltpu.VMEM(group.shape, F32),
            pltpu.SemaphoreType.DMA((5,)),
            pltpu.SemaphoreType.DMA((blocks,)),
            pltpu.SemaphoreType.DMA((n_pen, per_owner)),
            pltpu.SemaphoreType.DMA((2,)),
        ],
        compiler_params=pltpu.CompilerParams(vmem_limit_bytes=62 << 20),
    )(owner, tilt_pos, pair_tilt, pair_tile_within, depth_weights, spectrum)
    kept = [outs[0]] + [between(outs[i], 2 * i) for i in range(1, chips)]

    arrived = across(sent_sums, 1)
    step = 2
    while step < n_kz:
        sums = (sums + arrived).reshape(-1, 2, 2 * chunk, columns)
        sums, arrived = sums[:, 0], across(sums[:, 1], step)
        step *= 2

    sent = measured.reshape(2, n_pen, columns).transpose(1, 0, 2)
    cores = [[2 * i + core for i in range(chips)] for core in range(2)]
    got = lax.all_to_all(sent, "pen", split_axis=0, concat_axis=0, tiled=True, axis_index_groups=cores)
    got = got.reshape(chips, 2, 2, columns)
    got_swapped = between(got, 1)
    own, table = pl.pallas_call(
        call(residual_and_table, n_kz, chunk, per_owner, tiles_per_tilt),
        out_shape=[
            jax.ShapeDtypeStruct((2 * chunk, columns), BF16),
            jax.ShapeDtypeStruct((4 * tiles, 2 * per_owner * depth), BF16),
        ],
        in_specs=[SMEM, SMEM] + [VMEM] * 7,
        out_specs=[VMEM, VMEM],
        scratch_shapes=[
            pltpu.VMEM((blocks, pairs), I32),
            pltpu.VMEM((2 * chunk, columns), F32),
            pltpu.SMEM((per_owner,), I32),
        ],
        compiler_params=pltpu.CompilerParams(vmem_limit_bytes=8 << 20),
    )(
        owner,
        tilt_pos,
        pair_tilt,
        pair_tile_within,
        depth_weights,
        sums.reshape(2 * chunk, columns),
        arrived.reshape(2 * chunk, columns),
        got,
        got_swapped,
    )

    held = own
    step = 1
    while 2 * step < n_kz:
        held = jnp.concatenate([held, across(held, step)], axis=0)
        step *= 2
    def take_other(arrived, after):
        return pl.pallas_call(
            call(other_core, len(arrived)),
            out_shape=jax.ShapeDtypeStruct((len(arrived), *pair), BF16),
            in_specs=[ANY] * (len(arrived) + len(after)),
            out_specs=ANY,
            scratch_shapes=[pltpu.SemaphoreType.DMA((len(arrived),))],
            compiler_params=pltpu.CompilerParams(vmem_limit_bytes=8 << 20),
        )(*arrived, *after)

    near_swapped = between(take_other(kept[:2], [held]), 1)
    held = pl.pallas_call(
        join_tiles,
        out_shape=jax.ShapeDtypeStruct((2 * tiles, columns), BF16),
        in_specs=[VMEM, VMEM, ANY],
        out_specs=VMEM,
        compiler_params=pltpu.CompilerParams(vmem_limit_bytes=8 << 20),
    )(held, across(held, step), near_swapped)
    like = [held] + [between(held, 2 * i) for i in range(1, chips)]
    far_swapped = between(take_other(kept[2:], like[1:]), 1)
    stacked = pl.pallas_call(
        stack_tiles,
        out_shape=jax.ShapeDtypeStruct((chips, 2 * tiles, columns), BF16),
        in_specs=[VMEM] * chips,
        out_specs=VMEM,
        compiler_params=pltpu.CompilerParams(vmem_limit_bytes=8 << 20),
    )(*like)
    other = between(stacked, 1)

    scratch = [pltpu.VMEM((chips, *pair), BF16), pltpu.SemaphoreType.DMA((chips,))]
    shapes = [
        jax.ShapeDtypeStruct((per_owner, 2, depth, cells), BF16),
        jax.ShapeDtypeStruct((tile_dev, 2, cells), BF16),
    ]
    begun, part = pl.pallas_call(
        call(adjoint_like, n_pen, chunk, per_owner),
        out_shape=shapes,
        in_specs=[VMEM] * (n_pen + 1),
        out_specs=[ANY, VMEM],
        scratch_shapes=scratch,
        compiler_params=pltpu.CompilerParams(vmem_limit_bytes=16 << 20),
    )(table, *kept, *like)
    updated, residual = pl.pallas_call(
        call(adjoint_other, n_pen, chunk, per_owner),
        out_shape=shapes,
        in_specs=[VMEM, ANY] + [VMEM] * 4,
        out_specs=[ANY, ANY],
        scratch_shapes=[*scratch, pltpu.VMEM(measured.shape, BF16), pltpu.SemaphoreType.DMA],
        input_output_aliases={1: 0},
        compiler_params=pltpu.CompilerParams(vmem_limit_bytes=16 << 20),
    )(table, begun, part, near_swapped, far_swapped, other)
    return (updated, residual)


def solution(mesh):
    return jax.shard_map(
        body,
        mesh=mesh,
        in_specs=(
            P("kz", None, None, "pen"),
            P("kz", None, None),
            P("kz", None),
            P("kz", None),
            P(),
            P("kz"),
            P(("kz", "pen"), None, None),
        ),
        out_specs=(P(("kz", "pen"), None, None, None), P(("kz", "pen"), None, None)),
        check_vma=False,
    )
```
